256 devices in a mesh: fsdp: 32 (over y, x, core), tp: 8 (over z).
Axes of the slice: x: 4, y: 4, z: 8, core: 2. Of those that a mesh axis runs over, the one named last changes fastest.
Arguments:
- grad: bfloat16 [8192, 28672], P('fsdp', 'tp'), may hold values from -54 to 54, as said below
- momentum: bfloat16 [8192, 28672], P('fsdp', 'tp'), may hold values from -6 to 6
- basis: bfloat16 [28672, 256], P('tp'), may hold values from -6 to 6
Outputs:
- update: bfloat16 [8192, 28672], P('fsdp', 'tp')
- new_momentum: bfloat16 [8192, 28672], P('fsdp', 'tp')
- new_basis: bfloat16 [28672, 256], P('tp')
The draws below stay inside these ranges and needn't reach their ends.
Inputs may be any that keep to these rules, and one draw needn't show every extreme that they name: `grad`: a gradient whose rows and columns carry scales of about 0.3 to 3.
All inputs are finite; a program needn't handle non-finite values.
Results may differ from the reference program's by a relative error of at most 0.0078.
Values may be sent and summed in bfloat16 or wider, within the bound.
A program may use at most 64 MiB of HBM per device.

```python
import math
import jax
import jax.numpy as jnp
from jax import lax

M = 8192
N = 28672
RANK = 256
MU = 90


def draw_grad(key, part):
    key = jax.random.fold_in(key, 11)
    key_rows, key_cols, key_base = jax.random.split(key, 3)
    row_scale = jnp.exp(jax.random.uniform(key_rows, (M, 1), jnp.float32, math.log(0.3), math.log(3.0)))
    col_scale = jnp.exp(jax.random.uniform(key_cols, (1, N), jnp.float32, math.log(0.3), math.log(3.0)))
    base = jax.random.truncated_normal(key_base, -6.0, 6.0, (M, N), jnp.float32)
    return (base * row_scale * col_scale).astype(jnp.bfloat16)


def level_of(own_key, extent, cuts, smallest, top_value):
    factor_of = 1.0
    for position, shards_of in cuts:
        draws = jax.random.uniform(jax.random.fold_in(jax.random.fold_in(own_key, 6), position), (shards_of,), jnp.float32, smallest / len(cuts), top_value / len(cuts))
        factor_of = factor_of * jnp.repeat(jnp.exp(draws), extent[position] // shards_of).reshape((-1,) + (1,) * (len(extent) - 1 - position))
    return factor_of


def bell_draw(own_key, dims, deviation, most, shards=(), dtype=jnp.bfloat16):
    result = jax.random.normal(own_key, dims, jnp.float32) * deviation
    if len(shards) > 0:
        result = level_of(own_key, dims, shards, -0.22, 0.18) * result
    return jnp.clip(result, min=-most, max=most).astype(dtype)


def setup_inputs(seed: int = 0) -> dict:
    seeds = jax.random.split(jax.random.key(seed), 4)
    grad = draw_grad(jax.random.fold_in(seeds[3], 71), 0)
    momentum = bell_draw(seeds[1], (M, N), 1.0, 6.0, ((0, 32), (1, 8)))
    basis = bell_draw(seeds[2], (N, RANK), 1.0, 6.0, ((0, 8),))
    return {"grad": grad, "momentum": momentum, "basis": basis}


def reference(grad, momentum, basis):
    buffer = momentum.astype(jnp.float32) + grad.astype(jnp.float32)
    buffer_half = buffer.astype(jnp.bfloat16)
    left = jnp.dot(buffer_half.astype(jnp.float32), basis.astype(jnp.float32), preferred_element_type=jnp.float32) * (1.0 / math.sqrt(N))
    gram = jnp.dot(left.T.astype(jnp.float32), left.astype(jnp.float32), precision=lax.Precision.HIGHEST, preferred_element_type=jnp.float32)
    lower = jnp.linalg.cholesky(gram)
    ortho = lax.linalg.triangular_solve(lower, left, left_side=False, lower=True, transpose_a=True).astype(jnp.bfloat16)
    right = lax.dot_general(buffer_half.astype(jnp.float32), ortho.astype(jnp.float32), (((0,), (0,)), ((), ())), preferred_element_type=jnp.float32)
    scale = jnp.sqrt(lax.optimization_barrier(jnp.sum(right * right, axis=0)) / N + 1e-06)
    new_basis = (right / scale[None, :]).astype(jnp.bfloat16)
    scaled = (ortho.astype(jnp.float32) * scale[None, :]).astype(jnp.bfloat16)
    lowrank = lax.dot_general(scaled.astype(jnp.float32), new_basis.astype(jnp.float32), (((1,), (1,)), ((), ())), preferred_element_type=jnp.float32)
    new_momentum = (buffer - (1.0 - MU / 100.0) * lowrank).astype(jnp.bfloat16)
    product = lax.dot_general(ortho.astype(jnp.float32), new_basis.astype(jnp.float32), (((1,), (1,)), ((), ())), preferred_element_type=jnp.float32)
    update = (product * math.sqrt(M / RANK)).astype(jnp.bfloat16)
    return (update, new_momentum, new_basis)
```

```python
import math

import jax
import jax.numpy as jnp
from jax import lax
from jax.experimental import pallas as pl
from jax.experimental.pallas import tpu as pltpu
from jax.sharding import PartitionSpec as P

M = 8192
N = 28672
RANK = 256
MU = 90

MESH = pl.DeviceIdType.MESH
HI = lax.Precision.HIGHEST
F32 = jnp.float32
BF16 = jnp.bfloat16
NX, NY, NZ = 4, 4, 8
NF = NX * NY * 2
ROWS = M // NF
COLS = N // NZ
CHUNK = 896
BLOCK = COLS // NF
VMEM_LIMIT = 48 * 1024 * 1024


def dot(a, b, ca, cb, precision=None):
    return lax.dot_general(
        a, b, (((ca,), (cb,)), ((), ())), precision=precision, preferred_element_type=F32
    )


def lower_inverse(gram, b=32, s8=8):
    n = gram.shape[0]
    rows = lax.broadcasted_iota(jnp.int32, (8, 128), 0)
    lanes = lax.broadcasted_iota(jnp.int32, (b, n), 1)
    sub = lax.broadcasted_iota(jnp.int32, (b, n), 0)
    panels = [gram[p * b:(p + 1) * b, :] for p in range(n // b)]
    done = []
    tiles = b // 8
    for p in range(n // b):
        r0 = p * b
        P = panels[p]
        nt = n // 128
        home = r0 // 128
        ident = jnp.where(lanes == sub + r0, 1.0, 0.0)[:, home * 128:(home + 1) * 128]
        M = [[P[8 * a:8 * a + 8, 128 * l:128 * l + 128] for l in range(nt)] + [ident[8 * a:8 * a + 8]] for a in range(tiles)]
        piv = [jnp.ones((8, 128), jnp.float32) for _ in range(tiles)]
        for s in range(b // s8):
            a0 = s
            C = []
            for k in range(s8):
                lane = r0 - home * 128 + s * s8 + k
                C.append([jnp.broadcast_to(M[a][home][:, lane:lane + 1], (8, 128)) if a >= a0 else None for a in range(tiles)])
            for j in range(s8):
                sj = jnp.broadcast_to(C[j][a0][j:j + 1, :], (8, 128))
                inv = 1.0 / sj
                w = [None] * tiles
                for a in range(a0, tiles):
                    wa = C[j][a] * inv
                    if a == a0:
                        wa = jnp.where(rows > j, wa, 0.0)
                    w[a] = wa
                for k in range(j + 1, s8):
                    bk = jnp.broadcast_to(C[j][a0][k:k + 1, :], (8, 128))
                    for a in range(a0, tiles):
                        C[k][a] = C[k][a] - w[a] * bk
                piv[a0] = jnp.where(rows == j, sj, piv[a0])
                for l in range(nt + 1):
                    row = jnp.broadcast_to(M[a0][l][j:j + 1, :], (8, 128))
                    for a in range(a0, tiles):
                        M[a][l] = M[a][l] - w[a] * row
        rs = [lax.rsqrt(v) for v in piv]
        full = []
        for a in range(tiles):
            out = [M[a][l] * rs[a] for l in range(nt + 1)]
            z = out.pop()
            ln = lax.broadcasted_iota(jnp.int32, (8, 128), 1) + home * 128
            out[home] = jnp.where((ln >= r0) & (ln < r0 + b), z, out[home])
            full.append(jnp.concatenate(out, axis=1))
        U = jnp.concatenate(full, axis=0)
        done.append(U)
        if p + 1 < n // b:
            r1 = r0 + b
            upd = lax.dot_general(U, U, (((0,), (0,)), ((), ())), precision=HI, preferred_element_type=jnp.float32)
            for q in range(p + 1, n // b):
                old = jnp.where((lanes >= r0) & (lanes < r1), 0.0, panels[q])
                panels[q] = old - upd[q * b:(q + 1) * b, :]
    W = jnp.concatenate(done, axis=0)
    li = lax.broadcasted_iota(jnp.int32, (n, n), 1)
    si = lax.broadcasted_iota(jnp.int32, (n, n), 0)
    return jnp.where(li <= si, W, 0.0)


def gram_kernel(g_hbm, m_hbm, b_hbm, left, gram, gbuf, mbuf, bbuf, part, rz, gpart, rg, own, r2,
                load, s_rz, r_rz, s_az, r_az, s_rg, r_rg, s_r2, r_r2, s_ag, r_ag):
    f = lax.axis_index("fsdp")
    t = lax.axis_index("tp")
    nc = COLS // CHUNK
    loads = []
    for c in range(nc):
        cols = pl.ds(c * CHUNK, CHUNK)
        three = [
            pltpu.make_async_copy(g_hbm.at[:, cols], gbuf.at[:, cols], load.at[3 * c]),
            pltpu.make_async_copy(m_hbm.at[:, cols], mbuf.at[:, cols], load.at[3 * c + 1]),
            pltpu.make_async_copy(b_hbm.at[cols, :], bbuf.at[cols, :], load.at[3 * c + 2]),
        ]
        for cp in three:
            cp.start()
        loads.append(three)
    zs = [lax.rem(t + j, NZ) for j in range(NZ)]
    fs = [lax.rem(f + j, NF) for j in range(NF)]
    barrier = pltpu.get_barrier_semaphore()
    for j in range(1, NZ):
        pl.semaphore_signal(barrier, inc=1, device_id=(f, zs[j]), device_id_type=MESH)
    for j in range(1, NF):
        pl.semaphore_signal(barrier, inc=1, device_id=(fs[j], t), device_id_type=MESH)

    for c in range(nc):
        for cp in loads[c]:
            cp.wait()
        cols = pl.ds(c * CHUNK, CHUNK)
        half = (mbuf[:, cols].astype(F32) + gbuf[:, cols].astype(F32)).astype(BF16)
        term = dot(half, bbuf[cols, :], 1, 0)
        if c == 0:
            part[...] = term
        else:
            part[...] += term
    part[...] = part[...] * (1.0 / math.sqrt(N))
    pl.semaphore_wait(barrier, NZ - 1 + NF - 1)

    def piece(z, size):
        return pl.ds(pl.multiple_of(z * size, size), size)

    sends = []

    def exchange(j, src, dst, ss, rs, dev):
        cp = pltpu.make_async_remote_copy(
            src_ref=src, dst_ref=dst, send_sem=ss.at[j - 1], recv_sem=rs.at[j - 1],
            device_id=dev, device_id_type=MESH,
        )
        cp.start()
        sends.append(cp)
        return cp

    zr = ROWS // NZ
    cps = [exchange(j, part.at[piece(zs[j], zr), :], rz.at[j - 1], s_rz, r_rz, (f, zs[j])) for j in range(1, NZ)]
    mine = part[piece(t, zr), :]
    for j in range(1, NZ):
        cps[j - 1].wait_recv()
        mine = mine + rz[j - 1]
    left[piece(t, zr), :] = mine
    az = [exchange(j, left.at[piece(t, zr), :], left.at[piece(t, zr), :], s_az, r_az, (f, zs[j])) for j in range(1, NZ)]

    gr = RANK // NF
    gpart[...] = dot(mine, mine, 0, 0, HI)
    cps = [exchange(j, gpart.at[piece(fs[j], gr), :], rg.at[j - 1], s_rg, r_rg, (fs[j], t)) for j in range(1, NF)]
    acc = gpart[piece(f, gr), :]
    for j in range(1, NF):
        cps[j - 1].wait_recv()
        acc = acc + rg[j - 1]
    own[...] = acc
    cps = [exchange(j, own, r2.at[j - 1], s_r2, r_r2, (f, zs[j])) for j in range(1, NZ)]
    for j in range(1, NZ):
        cps[j - 1].wait_recv()
        acc = acc + r2[j - 1]
    gram[piece(f, gr), :] = acc
    cps = [exchange(j, gram.at[piece(f, gr), :], gram.at[piece(f, gr), :], s_ag, r_ag, (fs[j], t)) for j in range(1, NF)]
    for cp in cps:
        cp.wait_recv()
    for cp in az:
        cp.wait_recv()
    for cp in sends:
        cp.wait_send()


def factor_kernel(gram, left, inverse, ortho):
    w = lower_inverse(gram[...])
    inverse[...] = w
    ortho[...] = dot(left[...], w, 1, 1, HI).astype(BF16)


def right_kernel(g_hbm, m_hbm, left, inverse, out, squares, gbuf, mbuf, r, rc, ra, rb, sa, sb, ra2, rb2, sq, sz,
                 load, s_c, r_c, s_1, r_1, s_2, r_2, s_q, r_q, s_z, r_z, s_g2, r_g2, s_g1, r_g1, s_gc, r_gc):
    f = lax.axis_index("fsdp")
    t = lax.axis_index("tp")
    core = lax.rem(f, 2)
    x = lax.rem(f // 2, NX)
    y = f // (2 * NX)
    other = 1 - core

    def dev(px, py, pc):
        return ((py * NX + px) * 2 + pc, t)

    xs = [lax.rem(x + j, NX) for j in range(NX)]
    ys = [lax.rem(y + j, NY) for j in range(NY)]
    zs = [lax.rem(t + j, NZ) for j in range(NZ)]
    fs = [lax.rem(f + j, NF) for j in range(NF)]
    sibling = dev(x, y, other)
    wide = COLS // 2
    nk = wide // CHUNK
    qk = NX // nk
    loads = []
    for i, pc in enumerate((other, core)):
        for k in range(nk):
            cols = pl.ds(pl.multiple_of(pc * wide + k * CHUNK, 128), CHUNK)
            two = [
                pltpu.make_async_copy(g_hbm.at[:, cols], gbuf.at[:, cols], load.at[2 * (i * nk + k)]),
                pltpu.make_async_copy(m_hbm.at[:, cols], mbuf.at[:, cols], load.at[2 * (i * nk + k) + 1]),
            ]
            for cp in two:
                cp.start()
            loads.append((cols, two))
    barrier = pltpu.get_barrier_semaphore()
    for j in range(1, NZ):
        pl.semaphore_signal(barrier, inc=1, device_id=(f, zs[j]), device_id_type=MESH)
    for j in range(1, NF):
        pl.semaphore_signal(barrier, inc=1, device_id=(fs[j], t), device_id_type=MESH)

    sends = []

    def exchange(src, dst, ss, rs, device):
        cp = pltpu.make_async_remote_copy(
            src_ref=src, dst_ref=dst, send_sem=ss, recv_sem=rs, device_id=device, device_id_type=MESH
        )
        cp.start()
        sends.append(cp)
        return cp

    hi = left[...].astype(BF16)
    lo = (left[...] - hi.astype(F32)).astype(BF16)

    def product(i, k, pc):
        cols, two = loads[i * nk + k]
        for cp in two:
            cp.wait()
        half = (mbuf[:, cols].astype(F32) + gbuf[:, cols].astype(F32)).astype(BF16)
        val = dot(half, hi, 0, 0) + dot(half, lo, 0, 0)
        for h in range(2):
            r[h, pc, k * qk:(k + 1) * qk] = val[:, 128 * h:128 * h + 128].reshape(qk, NY, BLOCK, 128)

    cc = []
    for k in range(nk):
        product(0, k, other)
        if k == 0:
            pl.semaphore_wait(barrier, NZ - 1 + NF - 1)
        qs = pl.ds(k * qk, qk)
        cc.append([
            exchange(r.at[h, other, qs], rc.at[h, qs], s_c.at[2 * k + h], r_c.at[2 * k + h], sibling)
            for h in range(2)
        ])
    for k in range(nk):
        product(1, k, core)
    for k in range(nk):
        for h in range(2):
            cc[k][h].wait_recv()
            qs = pl.ds(k * qk, qk)
            r[h, core, qs] = r[h, core, qs] + rc[h, qs]
    one = []
    for j in range(1, NX):
        one.append(exchange(r.at[0, core, xs[j]], ra.at[j - 1], s_1.at[j - 1], r_1.at[j - 1], dev(xs[j], y, core)))
        one.append(exchange(r.at[1, core, :, ys[j]], rb.at[j - 1], s_1.at[2 + j], r_1.at[2 + j], dev(x, ys[j], core)))
    for cp in one:
        cp.wait_recv()
    sa[...] = r[0, core, x] + ra[0] + ra[1] + ra[2]
    sb[...] = r[1, core, :, y] + rb[0] + rb[1] + rb[2]
    two = []
    for j in range(1, NX):
        two.append(exchange(sa.at[ys[j]], ra2.at[j - 1], s_2.at[j - 1], r_2.at[j - 1], dev(x, ys[j], core)))
        two.append(exchange(sb.at[xs[j]], rb2.at[j - 1], s_2.at[2 + j], r_2.at[2 + j], dev(xs[j], y, core)))
    for cp in two:
        cp.wait_recv()
    shard = jnp.concatenate(
        [sa[y] + ra2[0] + ra2[1] + ra2[2], sb[x] + rb2[0] + rb2[1] + rb2[2]], axis=1
    )
    right = dot(shard, inverse[...], 1, 1, HI)
    sq[f] = jnp.broadcast_to(jnp.sum(right * right, axis=0, keepdims=True), (8, RANK))
    sqs = [exchange(sq.at[f], sq.at[f], s_q.at[j - 1], r_q.at[j - 1], (fs[j], t)) for j in range(1, NF)]
    rounded = right.astype(BF16)
    for h in range(2):
        out[h, core, x, y] = rounded[:, 128 * h:128 * h + 128]
    g2 = []
    for j in range(1, NX):
        g2.append(exchange(out.at[0, core, x, y], out.at[0, core, x, y], s_g2.at[j - 1], r_g2.at[j - 1], dev(x, ys[j], core)))
        g2.append(exchange(out.at[1, core, x, y], out.at[1, core, x, y], s_g2.at[2 + j], r_g2.at[2 + j], dev(xs[j], y, core)))
    for cp in g2:
        cp.wait_recv()
    g1 = []
    for j in range(1, NX):
        g1.append(exchange(out.at[0, core, x], out.at[0, core, x], s_g1.at[j - 1], r_g1.at[j - 1], dev(xs[j], y, core)))
        g1.append(exchange(out.at[1, core, :, y], out.at[1, core, :, y], s_g1.at[2 + j], r_g1.at[2 + j], dev(x, ys[j], core)))
    gc = [
        exchange(out.at[0, core, x], out.at[0, core, x], s_gc.at[0], r_gc.at[0], sibling),
        exchange(out.at[1, core, :, y], out.at[1, core, :, y], s_gc.at[1], r_gc.at[1], sibling),
    ]
    for cp in sqs:
        cp.wait_recv()
    sz[t] = jnp.sum(sq[...], axis=0)
    szs = [exchange(sz.at[t], sz.at[t], s_z.at[j - 1], r_z.at[j - 1], (f, zs[j])) for j in range(1, NZ)]
    for j in range(1, NX):
        g1[2 * j - 2].wait_recv()
        px = lax.rem(x + NX - j, NX)
        gc.append(exchange(out.at[0, core, px], out.at[0, core, px], s_gc.at[2 * j], r_gc.at[2 * j], sibling))
        g1[2 * j - 1].wait_recv()
        py = lax.rem(y + NY - j, NY)
        gc.append(exchange(out.at[1, core, :, py], out.at[1, core, :, py], s_gc.at[2 * j + 1], r_gc.at[2 * j + 1], sibling))
    for cp in szs:
        cp.wait_recv()
    squares[...] = jnp.sum(sz[...], axis=0)
    for cp in gc:
        cp.wait_recv()
    for cp in sends:
        cp.wait_send()


def output_kernel(g, m, ortho, right, squares, update, new_momentum, new_basis):
    scale = jnp.sqrt(squares[0:1, :] / N + 1e-06)
    rr = jnp.concatenate([right[0], right[1]], axis=1).astype(F32)
    nb = (rr / scale).astype(BF16)
    new_basis[...] = nb
    scaled = (ortho[...].astype(F32) * scale).astype(BF16)
    lowrank = dot(scaled, nb, 1, 1)
    buffer = m[...].astype(F32) + g[...].astype(F32)
    new_momentum[...] = (buffer - (1.0 - MU / 100.0) * lowrank).astype(BF16)
    update[...] = (dot(ortho[...], nb, 1, 1) * math.sqrt(M / RANK)).astype(BF16)


def body(grad, momentum, basis):
    anywhere = pl.BlockSpec(memory_space=pl.ANY)
    vmem = pl.BlockSpec(memory_space=pltpu.VMEM)
    dma = pltpu.SemaphoreType.DMA
    zr, gr = ROWS // NZ, RANK // NF
    left, gram = pl.pallas_call(
        gram_kernel,
        out_shape=(jax.ShapeDtypeStruct((ROWS, RANK), F32), jax.ShapeDtypeStruct((RANK, RANK), F32)),
        in_specs=[anywhere] * 3,
        out_specs=(vmem, vmem),
        scratch_shapes=[
            pltpu.VMEM((ROWS, COLS), BF16), pltpu.VMEM((ROWS, COLS), BF16), pltpu.VMEM((COLS, RANK), BF16),
            pltpu.VMEM((ROWS, RANK), F32), pltpu.VMEM((NZ - 1, zr, RANK), F32),
            pltpu.VMEM((RANK, RANK), F32), pltpu.VMEM((NF - 1, gr, RANK), F32),
            pltpu.VMEM((gr, RANK), F32), pltpu.VMEM((NZ - 1, gr, RANK), F32),
            dma((3 * (COLS // CHUNK),)),
            dma((NZ - 1,)), dma((NZ - 1,)), dma((NZ - 1,)), dma((NZ - 1,)),
            dma((NF - 1,)), dma((NF - 1,)), dma((NZ - 1,)), dma((NZ - 1,)), dma((NF - 1,)), dma((NF - 1,)),
        ],
        compiler_params=pltpu.CompilerParams(collective_id=0, has_side_effects=True, vmem_limit_bytes=VMEM_LIMIT),
        name="gram_kernel",
    )(grad, momentum, basis)
    inverse, ortho = pl.pallas_call(
        factor_kernel,
        out_shape=(jax.ShapeDtypeStruct((RANK, RANK), F32), jax.ShapeDtypeStruct((ROWS, RANK), BF16)),
        in_specs=[vmem, vmem],
        out_specs=(vmem, vmem),
        compiler_params=pltpu.CompilerParams(vmem_limit_bytes=VMEM_LIMIT),
        name="factor_kernel",
    )(gram, left)
    right, squares = pl.pallas_call(
        right_kernel,
        out_shape=(
            jax.ShapeDtypeStruct((2, 2, NX, NY, BLOCK, 128), BF16),
            jax.ShapeDtypeStruct((8, RANK), F32),
        ),
        in_specs=[anywhere, anywhere, vmem, vmem],
        out_specs=(vmem, vmem),
        scratch_shapes=[
            pltpu.VMEM((ROWS, COLS), BF16), pltpu.VMEM((ROWS, COLS), BF16),
            pltpu.VMEM((2, 2, NX, NY, BLOCK, 128), F32), pltpu.VMEM((2, NX, NY, BLOCK, 128), F32),
            pltpu.VMEM((NX - 1, NY, BLOCK, 128), F32), pltpu.VMEM((NY - 1, NX, BLOCK, 128), F32),
            pltpu.VMEM((NY, BLOCK, 128), F32), pltpu.VMEM((NX, BLOCK, 128), F32),
            pltpu.VMEM((NY - 1, BLOCK, 128), F32), pltpu.VMEM((NX - 1, BLOCK, 128), F32),
            pltpu.VMEM((NF, 8, RANK), F32), pltpu.VMEM((NZ, 8, RANK), F32),
            dma((2 * (COLS // CHUNK),)),
            dma((4,)), dma((4,)), dma((6,)), dma((6,)), dma((6,)), dma((6,)),
            dma((NF - 1,)), dma((NF - 1,)), dma((NZ - 1,)), dma((NZ - 1,)),
            dma((6,)), dma((6,)), dma((6,)), dma((6,)), dma((8,)), dma((8,)),
        ],
        compiler_params=pltpu.CompilerParams(collective_id=1, has_side_effects=True, vmem_limit_bytes=VMEM_LIMIT),
        name="right_kernel",
    )(grad, momentum, left, inverse)
    step = 512
    return pl.pallas_call(
        output_kernel,
        grid=(COLS // step,),
        out_shape=(
            jax.ShapeDtypeStruct((ROWS, COLS), BF16),
            jax.ShapeDtypeStruct((ROWS, COLS), BF16),
            jax.ShapeDtypeStruct((COLS, RANK), BF16),
        ),
        in_specs=[
            pl.BlockSpec((ROWS, step), lambda i: (0, i)),
            pl.BlockSpec((ROWS, step), lambda i: (0, i)),
            pl.BlockSpec((ROWS, RANK), lambda i: (0, 0)),
            pl.BlockSpec((2, step, 128), lambda i: (0, i, 0)),
            pl.BlockSpec((8, RANK), lambda i: (0, 0)),
        ],
        out_specs=(
            pl.BlockSpec((ROWS, step), lambda i: (0, i)),
            pl.BlockSpec((ROWS, step), lambda i: (0, i)),
            pl.BlockSpec((step, RANK), lambda i: (i, 0)),
        ),
        compiler_params=pltpu.CompilerParams(vmem_limit_bytes=VMEM_LIMIT),
        name="output_kernel",
    )(grad, momentum, ortho, right.reshape(2, COLS, 128), squares)


def solution(mesh):
    placed = (P("fsdp", "tp"), P("fsdp", "tp"), P("tp", None))
    return jax.shard_map(
        body,
        mesh=mesh,
        in_specs=placed,
        out_specs=(P("fsdp", "tp"), P("fsdp", "tp"), P("tp", None)),
        check_vma=False,
    )
```

```python
import math

import jax
import jax.numpy as jnp
from jax import lax
from jax.experimental import pallas as pl
from jax.experimental.pallas import tpu as pltpu
from jax.sharding import PartitionSpec as P

M = 8192
N = 28672
RANK = 256
MU = 90

MESH = pl.DeviceIdType.MESH
HI = lax.Precision.HIGHEST
F32 = jnp.float32
BF16 = jnp.bfloat16
NX, NY, NZ = 4, 4, 8
NF = NX * NY * 2
ROWS = M // NF
COLS = N // NZ
CHUNK = 896
BLOCK = COLS // NF
SENDS = 120
VMEM_LIMIT = 60 * 1024 * 1024


def dot(a, b, ca, cb, precision=None):
    return lax.dot_general(
        a, b, (((ca,), (cb,)), ((), ())), precision=precision, preferred_element_type=F32
    )


def lower_inverse(gram, beside, b=32, s8=8):
    n = gram.shape[0]
    rows = lax.broadcasted_iota(jnp.int32, (8, 128), 0)
    lanes = lax.broadcasted_iota(jnp.int32, (b, n), 1)
    sub = lax.broadcasted_iota(jnp.int32, (b, n), 0)
    panels = [gram[p * b:(p + 1) * b, :] for p in range(n // b)]
    done = []
    tiles = b // 8
    for p in range(n // b):
        r0 = p * b
        P = panels[p]
        nt = n // 128
        home = r0 // 128
        ident = jnp.where(lanes == sub + r0, 1.0, 0.0)[:, home * 128:(home + 1) * 128]
        M = [[P[8 * a:8 * a + 8, 128 * l:128 * l + 128] for l in range(nt)] + [ident[8 * a:8 * a + 8]] for a in range(tiles)]
        piv = [jnp.ones((8, 128), jnp.float32) for _ in range(tiles)]
        for s in range(b // s8):
            a0 = s
            C = []
            for k in range(s8):
                lane = r0 - home * 128 + s * s8 + k
                C.append([jnp.broadcast_to(M[a][home][:, lane:lane + 1], (8, 128)) if a >= a0 else None for a in range(tiles)])
            for j in range(s8):
                sj = jnp.broadcast_to(C[j][a0][j:j + 1, :], (8, 128))
                inv = 1.0 / sj
                w = [None] * tiles
                for a in range(a0, tiles):
                    wa = C[j][a] * inv
                    if a == a0:
                        wa = jnp.where(rows > j, wa, 0.0)
                    w[a] = wa
                for k in range(j + 1, s8):
                    bk = jnp.broadcast_to(C[j][a0][k:k + 1, :], (8, 128))
                    for a in range(a0, tiles):
                        C[k][a] = C[k][a] - w[a] * bk
                piv[a0] = jnp.where(rows == j, sj, piv[a0])
                for l in range(nt + 1):
                    row = jnp.broadcast_to(M[a0][l][j:j + 1, :], (8, 128))
                    for a in range(a0, tiles):
                        M[a][l] = M[a][l] - w[a] * row
        rs = [lax.rsqrt(v) for v in piv]
        full = []
        for a in range(tiles):
            out = [M[a][l] * rs[a] for l in range(nt + 1)]
            z = out.pop()
            ln = lax.broadcasted_iota(jnp.int32, (8, 128), 1) + home * 128
            out[home] = jnp.where((ln >= r0) & (ln < r0 + b), z, out[home])
            full.append(jnp.concatenate(out, axis=1))
        U = jnp.concatenate(full, axis=0)
        done.append(U)
        if p + 1 < n // b:
            r1 = r0 + b
            upd = lax.dot_general(U, U, (((0,), (0,)), ((), ())), precision=HI, preferred_element_type=jnp.float32)
            for q in range(p + 1, n // b):
                old = jnp.where((lanes >= r0) & (lanes < r1), 0.0, panels[q])
                panels[q] = old - upd[q * b:(q + 1) * b, :]
        if p in beside:
            beside[p]()
    W = jnp.concatenate(done, axis=0)
    li = lax.broadcasted_iota(jnp.int32, (n, n), 1)
    si = lax.broadcasted_iota(jnp.int32, (n, n), 0)
    return jnp.where(li <= si, W, 0.0)


def step_kernel(g_hbm, m_hbm, b_hbm, out, squares, ortho, gbuf, mbuf, bbuf, bht, part, rz, left, gpart, gc, gsum, rg, own, r2,
                gram, r, rc, f1, sab, f2, sq, qc, qx, qy, qz, load, ssem, rsem):
    f = lax.axis_index("fsdp")
    t = lax.axis_index("tp")
    core = lax.rem(f, 2)
    x = lax.rem(f // 2, NX)
    y = f // (2 * NX)
    other = 1 - core
    nc = COLS // CHUNK

    def dev(px, py, pc):
        return ((py * NX + px) * 2 + pc, t)

    xs = [lax.rem(x + j, NX) for j in range(NX)]
    ys = [lax.rem(y + j, NY) for j in range(NY)]
    zs = [lax.rem(t + j, NZ) for j in range(NZ)]
    sibling = dev(x, y, other)
    plane = [(i, j) for i in range(NX) for j in range(NY) if (i, j) != (0, 0)]
    loads = []
    for c in range(nc):
        cols = pl.ds(c * CHUNK, CHUNK)
        three = [
            pltpu.make_async_copy(b_hbm.at[cols, :], bbuf.at[cols, :], load.at[3 * c]),
            pltpu.make_async_copy(g_hbm.at[:, cols], gbuf.at[:, cols], load.at[3 * c + 1]),
            pltpu.make_async_copy(m_hbm.at[:, cols], mbuf.at[:, cols], load.at[3 * c + 2]),
        ]
        for cp in three:
            cp.start()
        loads.append(three)
    barrier = pltpu.get_barrier_semaphore()
    for j in range(1, NZ):
        pl.semaphore_signal(barrier, inc=1, device_id=(f, zs[j]), device_id_type=MESH)
    for i, j in plane:
        pl.semaphore_signal(barrier, inc=1, device_id=dev(xs[i], ys[j], core), device_id_type=MESH)
    pl.semaphore_signal(barrier, inc=1, device_id=sibling, device_id_type=MESH)

    sends = []

    def exchange(src, dst, device):
        k = len(sends)
        cp = pltpu.make_async_remote_copy(
            src_ref=src, dst_ref=dst, send_sem=ssem.at[k], recv_sem=rsem.at[k], device_id=device, device_id_type=MESH
        )
        cp.start()
        sends.append(cp)
        return cp

    def share(ref, device):
        return exchange(ref, ref, device)

    def piece(z, size):
        return pl.ds(pl.multiple_of(z * size, size), size)

    for c in range(nc):
        for cp in loads[c]:
            cp.wait()
        cols = pl.ds(c * CHUNK, CHUNK)
        half = (mbuf[:, cols].astype(F32) + gbuf[:, cols].astype(F32)).astype(BF16)
        gbuf[:, cols] = half
        term = dot(half, bbuf[cols, :], 1, 0)
        if c == 0:
            part[...] = term
        else:
            part[...] += term
    part[...] = part[...] * (1.0 / math.sqrt(N))
    pl.semaphore_wait(barrier, NZ + len(plane))

    zr = ROWS // NZ
    cps = [exchange(part.at[piece(zs[j], zr), :], rz.at[j - 1], (f, zs[j])) for j in range(1, NZ)]
    for c in range(nc):
        cols = pl.ds(c * CHUNK, CHUNK)
        bht[cols, :] = gbuf[:, cols].T
    mine = part[piece(t, zr), :]
    for j in range(1, NZ):
        cps[j - 1].wait_recv()
        mine = mine + rz[j - 1]
    left[piece(t, zr), :] = mine

    def z_block(j):
        return left.at[piece(zs[j % NZ], zr), :]

    def z_half(j, k):
        return left.at[pl.ds(pl.multiple_of(zs[j % NZ] * zr + k * (zr // 2), zr // 2), zr // 2), :]

    up, down = (f, zs[1]), (f, zs[NZ - 1])
    az = [(share(z_block(0), up), share(z_block(0), down))]

    def z_step(k):
        az[-1][0].wait_recv()
        az[-1][1].wait_recv()
        if k < 3:
            az.append((share(z_block(NZ - k), up), share(z_block(k), down)))
        else:
            az.append((share(z_half(NZ - k, 0), up), share(z_half(k, 1), down)))

    gh = RANK // 2
    gr = gh // (NX * NY)
    gpart[...] = dot(mine, mine, 0, 0, HI)
    cp = exchange(gpart.at[piece(other, gh), :], gc, sibling)
    cp.wait_recv()
    gsum[...] = gpart[piece(core, gh), :] + gc[...]
    cps = [
        exchange(gsum.at[piece(ys[j] * NX + xs[i], gr), :], rg.at[k], dev(xs[i], ys[j], core))
        for k, (i, j) in enumerate(plane)
    ]
    z_step(1)
    acc = gsum[piece(y * NX + x, gr), :]
    for k, cp in enumerate(cps):
        cp.wait_recv()
        acc = acc + rg[k]
    own[...] = acc
    cps = [exchange(own, r2.at[j - 1], (f, zs[j])) for j in range(1, NZ)]
    z_step(2)
    for j in range(1, NZ):
        cps[j - 1].wait_recv()
        acc = acc + r2[j - 1]
    grow = pl.ds(pl.multiple_of(core * gh + (y * NX + x) * gr, gr), gr)
    gram[grow, :] = acc
    cps = [share(gram.at[grow, :], dev(xs[i], ys[j], core)) for i, j in plane]
    z_step(3)
    az[-1][0].wait_recv()
    az[-1][1].wait_recv()

    hi = left[...].astype(BF16)
    lo = (left[...] - hi.astype(F32)).astype(BF16)
    wide = COLS // 2
    nk = wide // CHUNK
    qk = NX // nk

    def product(k, pc):
        half = bht[pl.ds(pl.multiple_of(pc * wide + k * CHUNK, 128), CHUNK), :]
        val = dot(half, hi, 1, 0) + dot(half, lo, 1, 0)
        for h in range(2):
            r[h, pc, k * qk:(k + 1) * qk] = val[:, 128 * h:128 * h + 128].reshape(qk, NY, BLOCK, 128)

    cc = []
    for k in range(nk):
        product(k, other)
        qs = pl.ds(k * qk, qk)
        cc.append([exchange(r.at[h, other, qs], rc.at[h, qs], sibling) for h in range(2)])
    for cp in cps:
        cp.wait_recv()
    cg = share(gram.at[piece(core, gh), :], sibling)
    for k in range(nk):
        product(k, core)
    cg.wait_recv()

    east, west = dev(xs[1], y, core), dev(xs[3], y, core)
    north, south = dev(x, ys[1], core), dev(x, ys[3], core)
    ways = ((xs, east, west), (ys, north, south))
    state = {}

    def scatter_begin(name, axis, view, land):
        pos, nxt, prv = ways[axis]
        state[name] = [
            exchange(view(pos[2], 0), land(0), nxt),
            exchange(view(pos[2], 1), land(1), prv),
            exchange(view(pos[1], 1), land(2), nxt),
            exchange(view(pos[3], 0), land(3), prv),
        ]

    def scatter_relay(name, axis, view, land):
        pos, nxt, prv = ways[axis]
        cps = state[name]
        for k, (q, to) in enumerate(((pos[1], nxt), (pos[3], prv))):
            cps[k].wait_recv()
            ref = view(q, k)
            ref[...] = ref[...] + land(k)[...]
            cps.append(exchange(ref, land(4 + k), to))

    def scatter_end(name, axis, view, land):
        pos = ways[axis][0]
        cps = state[name]
        for k in range(2, 6):
            cps[k].wait_recv()
        return (
            view(pos[0], 0)[...] + land(3)[...] + land(4)[...],
            view(pos[0], 1)[...] + land(2)[...] + land(5)[...],
        )

    def first(h):
        def view(q, k):
            return r.at[0, core, q, pl.ds(2 * k, 2)] if h == 0 else r.at[1, core, pl.ds(2 * k, 2), q]
        return ("first", h), h, view, lambda k: f1.at[h, k]

    def second(h):
        size = BLOCK // 2
        return ("second", h), 1 - h, lambda q, k: sab.at[h, q, pl.ds(k * size, size)], lambda k: f2.at[h, k]

    def begin_first():
        for k in range(nk):
            qs = pl.ds(k * qk, qk)
            for h in range(2):
                cc[k][h].wait_recv()
                r[h, core, qs] = r[h, core, qs] + rc[h, qs]
        for h in range(2):
            scatter_begin(*first(h))

    def relay_first():
        for h in range(2):
            scatter_relay(*first(h))

    w = lower_inverse(gram[...], {0: begin_first, 4: relay_first})
    for h in range(2):
        lower, upper = scatter_end(*first(h))
        sab[h, 0:2] = lower
        sab[h, 2:4] = upper
        scatter_begin(*second(h))
    for h in range(2):
        scatter_relay(*second(h))
    halves = [jnp.concatenate(scatter_end(*second(h)), axis=0) for h in range(2)]
    right = dot(jnp.concatenate(halves, axis=1), w, 1, 1, HI)
    total = jnp.sum(right * right, axis=0, keepdims=True)
    srow = lax.broadcasted_iota(jnp.int32, (8, 128), 0)
    sq[...] = jnp.where(srow == 0, total[:, :128], total[:, 128:])
    rounded = right.astype(BF16)
    for h in range(2):
        out[h, core, x, y] = rounded[:, 128 * h:128 * h + 128]

    def gather_begin(axis, whole):
        pos, nxt, prv = ways[axis]
        return [share(whole(pos[0]), nxt), share(whole(pos[0]), prv)]

    def gather_relay(axis, cps, part_of):
        pos, nxt, prv = ways[axis]
        cps[0].wait_recv()
        a = share(part_of(pos[3], 0), nxt)
        cps[1].wait_recv()
        b = share(part_of(pos[1], 1), prv)
        return [a, b]

    cut = 64

    def block(h):
        return (lambda q: out.at[0, core, x, q]) if h == 0 else (lambda q: out.at[1, core, q, y])

    def block_part(h):
        rows = (pl.ds(0, cut), pl.ds(cut, BLOCK - cut))
        if h == 0:
            return lambda q, k: out.at[0, core, x, q, rows[k]]
        return lambda q, k: out.at[1, core, q, y, rows[k]]

    def band(h):
        return (lambda q: out.at[0, core, q]) if h == 0 else (lambda q: out.at[1, core, :, q])

    def band_part(h):
        if h == 0:
            return lambda q, k: out.at[0, core, q, pl.ds(2 * k, 2)]
        return lambda q, k: out.at[1, core, pl.ds(2 * k, 2), q]

    sc = exchange(sq, qc, sibling)
    ag = [gather_begin(1 - h, block(h)) for h in range(2)]
    sc.wait_recv()
    qx[x] = sq[...] + qc[...]
    sx = [share(qx.at[x], dev(xs[j], y, core)) for j in range(1, NX)]
    ag = [gather_relay(1 - h, ag[h], block_part(h)) for h in range(2)]
    for cp in sx:
        cp.wait_recv()
    qy[y] = qx[0] + qx[1] + qx[2] + qx[3]
    sy = [share(qy.at[y], dev(x, ys[j], core)) for j in range(1, NY)]
    last = []
    begun = []
    for h in range(2):
        for cp in ag[h]:
            cp.wait_recv()
        begun.append(gather_begin(h, band(h)))
        last.append(share(band(h)(ways[h][0][0]), sibling))
    for cp in sy:
        cp.wait_recv()
    qz[t] = qy[0] + qy[1] + qy[2] + qy[3]
    sz = [share(qz.at[t], (f, zs[j])) for j in range(1, NZ)]
    ortho[...] = dot(left[...], w, 1, 1, HI).astype(BF16)
    ag = [gather_relay(h, begun[h], band_part(h)) for h in range(2)]
    for h in range(2):
        for k in (3, 1):
            last.append(share(band(h)(ways[h][0][k]), sibling))
    for cp in sz:
        cp.wait_recv()
    total = qz[0]
    for j in range(1, NZ):
        total = total + qz[j]
    squares[...] = total
    for h in range(2):
        for cp in ag[h]:
            cp.wait_recv()
        last.append(share(band(h)(ways[h][0][2]), sibling))
    for cp in last:
        cp.wait_recv()
    for cp in sends:
        cp.wait_send()


def output_kernel(g, m, ortho, right, squares, update, new_momentum, new_basis):
    total = jnp.concatenate([squares[0:1, :], squares[1:2, :]], axis=1)
    scale = jnp.sqrt(total / N + 1e-06)
    rr = jnp.concatenate([right[0], right[1]], axis=1).astype(F32)
    nb = (rr / scale).astype(BF16)
    new_basis[...] = nb
    scaled = (ortho[...].astype(F32) * scale).astype(BF16)
    lowrank = dot(scaled, nb, 1, 1)
    buffer = m[...].astype(F32) + g[...].astype(F32)
    new_momentum[...] = (buffer - (1.0 - MU / 100.0) * lowrank).astype(BF16)
    update[...] = (dot(ortho[...], nb, 1, 1) * math.sqrt(M / RANK)).astype(BF16)


def body(grad, momentum, basis):
    anywhere = pl.BlockSpec(memory_space=pl.ANY)
    vmem = pl.BlockSpec(memory_space=pltpu.VMEM)
    dma = pltpu.SemaphoreType.DMA
    zr = ROWS // NZ
    gh = RANK // 2
    gr = gh // (NX * NY)
    right, squares, ortho = pl.pallas_call(
        step_kernel,
        out_shape=(
            jax.ShapeDtypeStruct((2, 2, NX, NY, BLOCK, 128), BF16),
            jax.ShapeDtypeStruct((8, 128), F32),
            jax.ShapeDtypeStruct((ROWS, RANK), BF16),
        ),
        in_specs=[anywhere] * 3,
        out_specs=(vmem, vmem, vmem),
        scratch_shapes=[
            pltpu.VMEM((ROWS, COLS), BF16), pltpu.VMEM((ROWS, COLS), BF16), pltpu.VMEM((COLS, RANK), BF16),
            pltpu.VMEM((COLS, RANK), BF16),
            pltpu.VMEM((ROWS, RANK), F32), pltpu.VMEM((NZ - 1, zr, RANK), F32), pltpu.VMEM((ROWS, RANK), F32),
            pltpu.VMEM((RANK, RANK), F32), pltpu.VMEM((gh, RANK), F32), pltpu.VMEM((gh, RANK), F32),
            pltpu.VMEM((NX * NY - 1, gr, RANK), F32), pltpu.VMEM((gr, RANK), F32), pltpu.VMEM((NZ - 1, gr, RANK), F32),
            pltpu.VMEM((RANK, RANK), F32),
            pltpu.VMEM((2, 2, NX, NY, BLOCK, 128), F32), pltpu.VMEM((2, NX, NY, BLOCK, 128), F32),
            pltpu.VMEM((2, 6, 2, BLOCK, 128), F32), pltpu.VMEM((2, NX, BLOCK, 128), F32),
            pltpu.VMEM((2, 6, BLOCK // 2, 128), F32),
            pltpu.VMEM((8, 128), F32), pltpu.VMEM((8, 128), F32),
            pltpu.VMEM((NX, 8, 128), F32), pltpu.VMEM((NY, 8, 128), F32), pltpu.VMEM((NZ, 8, 128), F32),
            dma((3 * (COLS // CHUNK),)), dma((SENDS,)), dma((SENDS,)),
        ],
        compiler_params=pltpu.CompilerParams(collective_id=0, has_side_effects=True, vmem_limit_bytes=VMEM_LIMIT),
        name="step_kernel",
    )(grad, momentum, basis)
    step = 512
    return pl.pallas_call(
        output_kernel,
        grid=(COLS // step,),
        out_shape=(
            jax.ShapeDtypeStruct((ROWS, COLS), BF16),
            jax.ShapeDtypeStruct((ROWS, COLS), BF16),
            jax.ShapeDtypeStruct((COLS, RANK), BF16),
        ),
        in_specs=[
            pl.BlockSpec((ROWS, step), lambda i: (0, i)),
            pl.BlockSpec((ROWS, step), lambda i: (0, i)),
            pl.BlockSpec((ROWS, RANK), lambda i: (0, 0)),
            pl.BlockSpec((2, step, 128), lambda i: (0, i, 0)),
            pl.BlockSpec((8, 128), lambda i: (0, 0)),
        ],
        out_specs=(
            pl.BlockSpec((ROWS, step), lambda i: (0, i)),
            pl.BlockSpec((ROWS, step), lambda i: (0, i)),
            pl.BlockSpec((step, RANK), lambda i: (i, 0)),
        ),
        compiler_params=pltpu.CompilerParams(vmem_limit_bytes=VMEM_LIMIT),
        name="output_kernel",
    )(grad, momentum, ortho, right.reshape(2, COLS, 128), squares)


def solution(mesh):
    placed = (P("fsdp", "tp"), P("fsdp", "tp"), P("tp", None))
    return jax.shard_map(
        body,
        mesh=mesh,
        in_specs=placed,
        out_specs=(P("fsdp", "tp"), P("fsdp", "tp"), P("tp", None)),
        check_vma=False,
    )
```

```python
import math

import jax
import jax.numpy as jnp
from jax import lax
from jax.experimental import pallas as pl
from jax.experimental.pallas import tpu as pltpu
from jax.sharding import PartitionSpec as P

M = 8192
N = 28672
RANK = 256
MU = 90

MESH = pl.DeviceIdType.MESH
HI = lax.Precision.HIGHEST
F32 = jnp.float32
BF16 = jnp.bfloat16
NX, NY, NZ = 4, 4, 8
NF = NX * NY * 2
ROWS = M // NF
COLS = N // NZ
CHUNK = 896
BLOCK = COLS // NF
VMEM_LIMIT = 60 * 1024 * 1024


def dot(a, b, ca, cb, precision=None):
    return lax.dot_general(
        a, b, (((ca,), (cb,)), ((), ())), precision=precision, preferred_element_type=F32
    )


def lower_inverse(gram, beside, b=32, s8=8):
    n = gram.shape[0]
    rows = lax.broadcasted_iota(jnp.int32, (8, 128), 0)
    lanes = lax.broadcasted_iota(jnp.int32, (b, n), 1)
    sub = lax.broadcasted_iota(jnp.int32, (b, n), 0)
    panels = [gram[p * b:(p + 1) * b, :] for p in range(n // b)]
    done = []
    tiles = b // 8
    for p in range(n // b):
        r0 = p * b
        P = panels[p]
        nt = n // 128
        home = r0 // 128
        ident = jnp.where(lanes == sub + r0, 1.0, 0.0)[:, home * 128:(home + 1) * 128]
        M = [[P[8 * a:8 * a + 8, 128 * l:128 * l + 128] for l in range(nt)] + [ident[8 * a:8 * a + 8]] for a in range(tiles)]
        piv = [jnp.ones((8, 128), jnp.float32) for _ in range(tiles)]
        for s in range(b // s8):
            a0 = s
            C = []
            for k in range(s8):
                lane = r0 - home * 128 + s * s8 + k
                C.append([jnp.broadcast_to(M[a][home][:, lane:lane + 1], (8, 128)) if a >= a0 else None for a in range(tiles)])
            for j in range(s8):
                sj = jnp.broadcast_to(C[j][a0][j:j + 1, :], (8, 128))
                inv = 1.0 / sj
                w = [None] * tiles
                for a in range(a0, tiles):
                    wa = C[j][a] * inv
                    if a == a0:
                        wa = jnp.where(rows > j, wa, 0.0)
                    w[a] = wa
                for k in range(j + 1, s8):
                    bk = jnp.broadcast_to(C[j][a0][k:k + 1, :], (8, 128))
                    for a in range(a0, tiles):
                        C[k][a] = C[k][a] - w[a] * bk
                piv[a0] = jnp.where(rows == j, sj, piv[a0])
                for l in range(nt + 1):
                    row = jnp.broadcast_to(M[a0][l][j:j + 1, :], (8, 128))
                    for a in range(a0, tiles):
                        M[a][l] = M[a][l] - w[a] * row
        rs = [lax.rsqrt(v) for v in piv]
        full = []
        for a in range(tiles):
            out = [M[a][l] * rs[a] for l in range(nt + 1)]
            z = out.pop()
            ln = lax.broadcasted_iota(jnp.int32, (8, 128), 1) + home * 128
            out[home] = jnp.where((ln >= r0) & (ln < r0 + b), z, out[home])
            full.append(jnp.concatenate(out, axis=1))
        U = jnp.concatenate(full, axis=0)
        done.append(U)
        if p + 1 < n // b:
            r1 = r0 + b
            upd = lax.dot_general(U, U, (((0,), (0,)), ((), ())), precision=HI, preferred_element_type=jnp.float32)
            for q in range(p + 1, n // b):
                old = jnp.where((lanes >= r0) & (lanes < r1), 0.0, panels[q])
                panels[q] = old - upd[q * b:(q + 1) * b, :]
        if p in beside:
            beside[p]()
    W = jnp.concatenate(done, axis=0)
    li = lax.broadcasted_iota(jnp.int32, (n, n), 1)
    si = lax.broadcasted_iota(jnp.int32, (n, n), 0)
    return jnp.where(li <= si, W, 0.0)


class Place:
    def __init__(self, ssem, rsem):
        self.ssem, self.rsem = ssem, rsem
        self.sends = []
        self.f = lax.axis_index("fsdp")
        self.t = lax.axis_index("tp")
        self.core = lax.rem(self.f, 2)
        self.other = 1 - self.core
        self.x = lax.rem(self.f // 2, NX)
        self.y = self.f // (2 * NX)
        self.xs = [lax.rem(self.x + j, NX) for j in range(NX)]
        self.ys = [lax.rem(self.y + j, NY) for j in range(NY)]
        self.zs = [lax.rem(self.t + j, NZ) for j in range(NZ)]
        self.sibling = self.dev(self.x, self.y, self.other)
        self.zdev = [(self.f, z) for z in self.zs]
        self.plane = [
            self.dev(self.xs[i], self.ys[j], self.core) for i in range(NX) for j in range(NY) if (i, j) != (0, 0)
        ]
        self.chips = [self.ys[j] * NX + self.xs[i] for i in range(NX) for j in range(NY) if (i, j) != (0, 0)]
        self.chip = self.y * NX + self.x
        self.ways = (
            (self.xs, self.dev(self.xs[1], self.y, self.core), self.dev(self.xs[3], self.y, self.core)),
            (self.ys, self.dev(self.x, self.ys[1], self.core), self.dev(self.x, self.ys[3], self.core)),
        )

    def dev(self, px, py, pc):
        return ((py * NX + px) * 2 + pc, self.t)

    def greet(self, devices):
        barrier = pltpu.get_barrier_semaphore()
        for device in devices:
            pl.semaphore_signal(barrier, inc=1, device_id=device, device_id_type=MESH)
        return lambda: pl.semaphore_wait(barrier, len(devices))

    def exchange(self, src, dst, device):
        k = len(self.sends)
        cp = pltpu.make_async_remote_copy(
            src_ref=src, dst_ref=dst, send_sem=self.ssem.at[k], recv_sem=self.rsem.at[k],
            device_id=device, device_id_type=MESH,
        )
        cp.start()
        self.sends.append(cp)
        return cp

    def share(self, ref, device):
        return self.exchange(ref, ref, device)

    def finish(self):
        for cp in self.sends:
            cp.wait_send()


def piece(z, size):
    return pl.ds(pl.multiple_of(z * size, size), size)


def left_kernel(g_hbm, m_hbm, b_hbm, left, bht, gbuf, mbuf, bbuf, part, rz, load, ssem, rsem):
    at = Place(ssem, rsem)
    nc = COLS // CHUNK
    loads = []
    for c in range(nc):
        cols = pl.ds(c * CHUNK, CHUNK)
        three = [
            pltpu.make_async_copy(b_hbm.at[cols, :], bbuf.at[cols, :], load.at[3 * c]),
            pltpu.make_async_copy(g_hbm.at[:, cols], gbuf.at[:, cols], load.at[3 * c + 1]),
            pltpu.make_async_copy(m_hbm.at[:, cols], mbuf.at[:, cols], load.at[3 * c + 2]),
        ]
        for cp in three:
            cp.start()
        loads.append(three)
    ready = at.greet(at.zdev[1:])
    total = None
    for c in range(nc):
        for cp in loads[c]:
            cp.wait()
        cols = pl.ds(c * CHUNK, CHUNK)
        half = (mbuf[:, cols].astype(F32) + gbuf[:, cols].astype(F32)).astype(BF16)
        gbuf[:, cols] = half
        term = dot(half, bbuf[cols, :], 1, 0)
        total = term if c == 0 else total + term
    part[...] = (total * (1.0 / math.sqrt(N))).astype(BF16)
    ready()
    zr = ROWS // NZ
    cps = [at.exchange(part.at[piece(at.zs[j], zr), :], rz.at[j - 1], at.zdev[j]) for j in range(1, NZ)]
    for c in range(nc):
        cols = pl.ds(c * CHUNK, CHUNK)
        bht[cols, :] = gbuf[:, cols].T
    mine = part[piece(at.t, zr), :].astype(F32)
    for j in range(1, NZ):
        cps[j - 1].wait_recv()
        mine = mine + rz[j - 1].astype(F32)
    left[piece(at.t, zr), :] = mine

    def z_block(j):
        return left.at[piece(at.zs[j % NZ], zr), :]

    def z_half(j, k):
        return left.at[pl.ds(pl.multiple_of(at.zs[j % NZ] * zr + k * (zr // 2), zr // 2), zr // 2), :]

    up, down = at.zdev[1], at.zdev[NZ - 1]
    now = (at.share(z_block(0), up), at.share(z_block(0), down))
    for k in range(1, 4):
        now[0].wait_recv()
        now[1].wait_recv()
        if k < 3:
            now = (at.share(z_block(NZ - k), up), at.share(z_block(k), down))
        else:
            now = (at.share(z_half(NZ - k, 0), up), at.share(z_half(k, 1), down))
    now[0].wait_recv()
    now[1].wait_recv()
    at.finish()


def gram_kernel(left, gram, gpart, gc, gsum, rg, own, r2, ssem, rsem):
    at = Place(ssem, rsem)
    ready = at.greet(at.zdev[1:] + at.plane + [at.sibling])
    zr = ROWS // NZ
    gh = RANK // 2
    gr = gh // (NX * NY)
    mine = left[piece(at.t, zr), :]
    gpart[...] = dot(mine, mine, 0, 0, HI)
    ready()
    at.exchange(gpart.at[piece(at.other, gh), :], gc, at.sibling).wait_recv()
    gsum[...] = gpart[piece(at.core, gh), :] + gc[...]
    cps = [at.exchange(gsum.at[piece(at.chips[k], gr), :], rg.at[k], device) for k, device in enumerate(at.plane)]
    acc = gsum[piece(at.chip, gr), :]
    for k, cp in enumerate(cps):
        cp.wait_recv()
        acc = acc + rg[k]
    own[...] = acc
    cps = [at.exchange(own, r2.at[j - 1], at.zdev[j]) for j in range(1, NZ)]
    for j in range(1, NZ):
        cps[j - 1].wait_recv()
        acc = acc + r2[j - 1]
    grow = pl.ds(pl.multiple_of(at.core * gh + at.chip * gr, gr), gr)
    gram[grow, :] = acc
    cps = [at.share(gram.at[grow, :], device) for device in at.plane]
    for cp in cps:
        cp.wait_recv()
    at.share(gram.at[piece(at.core, gh), :], at.sibling).wait_recv()
    at.finish()


def scatter_kernel(gram, left, bht, shard, ortho, r, rc, f1, sab, f2, ssem, rsem):
    at = Place(ssem, rsem)
    ready = at.greet([at.sibling, *at.ways[0][1:], *at.ways[1][1:]])
    hi = left[...].astype(BF16)
    lo = (left[...] - hi.astype(F32)).astype(BF16)
    wide = COLS // 2
    nk = wide // CHUNK
    qk = NX // nk

    def product(k, pc):
        half = bht[pl.ds(pl.multiple_of(pc * wide + k * CHUNK, 128), CHUNK), :]
        val = dot(half, hi, 1, 0) + dot(half, lo, 1, 0)
        for h in range(2):
            r[h, pc, k * qk:(k + 1) * qk] = val[:, 128 * h:128 * h + 128].reshape(qk, NY, BLOCK, 128)

    cc = []
    core, other, sibling, exchange = at.core, at.other, at.sibling, at.exchange
    for k in range(nk):
        product(k, other)
        if k == 0:
            ready()
        qs = pl.ds(k * qk, qk)
        cc.append([exchange(r.at[h, other, qs], rc.at[h, qs], sibling) for h in range(2)])
    for k in range(nk):
        product(k, core)

    ways = at.ways
    state = {}

    def scatter_begin(name, axis, view, land):
        pos, nxt, prv = ways[axis]
        state[name] = [
            exchange(view(pos[2], 0), land(0), nxt),
            exchange(view(pos[2], 1), land(1), prv),
            exchange(view(pos[1], 1), land(2), nxt),
            exchange(view(pos[3], 0), land(3), prv),
        ]

    def scatter_relay(name, axis, view, land):
        pos, nxt, prv = ways[axis]
        cps = state[name]
        for k, (q, to) in enumerate(((pos[1], nxt), (pos[3], prv))):
            cps[k].wait_recv()
            ref = view(q, k)
            ref[...] = ref[...] + land(k)[...]
            cps.append(exchange(ref, land(4 + k), to))

    def scatter_end(name, axis, view, land):
        pos = ways[axis][0]
        cps = state[name]
        for k in range(2, 6):
            cps[k].wait_recv()
        return (
            view(pos[0], 0)[...] + land(3)[...] + land(4)[...],
            view(pos[0], 1)[...] + land(2)[...] + land(5)[...],
        )

    def first(h):
        def view(q, k):
            return r.at[0, core, q, pl.ds(2 * k, 2)] if h == 0 else r.at[1, core, pl.ds(2 * k, 2), q]
        return ("first", h), h, view, lambda k: f1.at[h, k]

    def second(h):
        size = BLOCK // 2
        return ("second", h), 1 - h, lambda q, k: sab.at[h, q, pl.ds(k * size, size)], lambda k: f2.at[h, k]

    def begin_first():
        for k in range(nk):
            qs = pl.ds(k * qk, qk)
            for h in range(2):
                cc[k][h].wait_recv()
                r[h, core, qs] = r[h, core, qs] + rc[h, qs]
        for h in range(2):
            scatter_begin(*first(h))

    def relay_first():
        for h in range(2):
            scatter_relay(*first(h))

    w = lower_inverse(gram[...], {0: begin_first, 4: relay_first})
    for h in range(2):
        lower, upper = scatter_end(*first(h))
        sab[h, 0:2] = lower
        sab[h, 2:4] = upper
        scatter_begin(*second(h))
    for h in range(2):
        scatter_relay(*second(h))
    halves = [jnp.concatenate(scatter_end(*second(h)), axis=0) for h in range(2)]
    right = dot(jnp.concatenate(halves, axis=1), w, 1, 1, HI)
    shard[...] = right
    ortho[...] = dot(left[...], w, 1, 1, HI).astype(BF16)
    at.finish()


def gather_kernel(shard, out, squares, sq, qc, qx, qy, qz, ssem, rsem):
    at = Place(ssem, rsem)
    ready = at.greet(
        at.zdev[1:] + [at.sibling]
        + [at.dev(at.xs[j], at.y, at.core) for j in range(1, NX)] + [at.dev(at.x, at.ys[j], at.core) for j in range(1, NY)]
    )
    core, sibling, exchange, share, dev, ways = at.core, at.sibling, at.exchange, at.share, at.dev, at.ways
    x, y, t, f, xs, ys, zs = at.x, at.y, at.t, at.f, at.xs, at.ys, at.zs
    right = shard[...]
    total = jnp.sum(right * right, axis=0, keepdims=True)
    srow = lax.broadcasted_iota(jnp.int32, (8, 128), 0)
    sq[...] = jnp.where(srow == 0, total[:, :128], total[:, 128:])
    rounded = right.astype(BF16)
    for h in range(2):
        out[h, core, x, y] = rounded[:, 128 * h:128 * h + 128]
    ready()

    def gather_begin(axis, whole):
        pos, nxt, prv = ways[axis]
        return [share(whole(pos[0]), nxt), share(whole(pos[0]), prv)]

    def gather_relay(axis, cps, part_of):
        pos, nxt, prv = ways[axis]
        cps[0].wait_recv()
        a = share(part_of(pos[3], 0), nxt)
        cps[1].wait_recv()
        b = share(part_of(pos[1], 1), prv)
        return [a, b]

    cut = 64

    def block(h):
        return (lambda q: out.at[0, core, x, q]) if h == 0 else (lambda q: out.at[1, core, q, y])

    def block_part(h):
        rows = (pl.ds(0, cut), pl.ds(cut, BLOCK - cut))
        if h == 0:
            return lambda q, k: out.at[0, core, x, q, rows[k]]
        return lambda q, k: out.at[1, core, q, y, rows[k]]

    def band(h):
        return (lambda q: out.at[0, core, q]) if h == 0 else (lambda q: out.at[1, core, :, q])

    def band_part(h):
        if h == 0:
            return lambda q, k: out.at[0, core, q, pl.ds(2 * k, 2)]
        return lambda q, k: out.at[1, core, pl.ds(2 * k, 2), q]

    sc = exchange(sq, qc, sibling)
    ag = [gather_begin(1 - h, block(h)) for h in range(2)]
    sc.wait_recv()
    qx[x] = sq[...] + qc[...]
    sx = [share(qx.at[x], dev(xs[j], y, core)) for j in range(1, NX)]
    ag = [gather_relay(1 - h, ag[h], block_part(h)) for h in range(2)]
    for cp in sx:
        cp.wait_recv()
    qy[y] = qx[0] + qx[1] + qx[2] + qx[3]
    sy = [share(qy.at[y], dev(x, ys[j], core)) for j in range(1, NY)]
    last = []
    begun = []
    for h in range(2):
        for cp in ag[h]:
            cp.wait_recv()
        begun.append(gather_begin(h, band(h)))
        last.append(share(band(h)(ways[h][0][0]), sibling))
    for cp in sy:
        cp.wait_recv()
    qz[t] = qy[0] + qy[1] + qy[2] + qy[3]
    sz = [share(qz.at[t], (f, zs[j])) for j in range(1, NZ)]
    ag = [gather_relay(h, begun[h], band_part(h)) for h in range(2)]
    for h in range(2):
        for k in (3, 1):
            last.append(share(band(h)(ways[h][0][k]), sibling))
    for cp in sz:
        cp.wait_recv()
    total = qz[0]
    for j in range(1, NZ):
        total = total + qz[j]
    squares[...] = total
    for h in range(2):
        for cp in ag[h]:
            cp.wait_recv()
        last.append(share(band(h)(ways[h][0][2]), sibling))
    for cp in last:
        cp.wait_recv()
    at.finish()


def output_kernel(g, m, ortho, right, squares, update, new_momentum, new_basis):
    total = jnp.concatenate([squares[0:1, :], squares[1:2, :]], axis=1)
    scale = jnp.sqrt(total / N + 1e-06)
    rr = jnp.concatenate([right[0], right[1]], axis=1).astype(F32)
    nb = (rr / scale).astype(BF16)
    new_basis[...] = nb
    scaled = (ortho[...].astype(F32) * scale).astype(BF16)
    both = dot(jnp.concatenate([scaled, ortho[...]], axis=0), nb.T, 1, 0)
    lowrank = both[:ROWS]
    buffer = m[...].astype(F32) + g[...].astype(F32)
    new_momentum[...] = (buffer - (1.0 - MU / 100.0) * lowrank).astype(BF16)
    update[...] = (both[ROWS:] * math.sqrt(M / RANK)).astype(BF16)


def call(kernel, ident, outs, ins, scratch, sends, loads=0):
    dma = pltpu.SemaphoreType.DMA
    sems = ([dma((loads,))] if loads else []) + [dma((sends,)), dma((sends,))]
    return pl.pallas_call(
        kernel,
        out_shape=tuple(jax.ShapeDtypeStruct(*o) for o in outs),
        in_specs=[pl.BlockSpec(memory_space=pl.ANY if loads else pltpu.VMEM)] * ins,
        out_specs=tuple(pl.BlockSpec(memory_space=pltpu.VMEM) for _ in outs),
        scratch_shapes=[pltpu.VMEM(*v) for v in scratch] + sems,
        compiler_params=pltpu.CompilerParams(collective_id=ident, has_side_effects=True, vmem_limit_bytes=VMEM_LIMIT),
        name=kernel.__name__,
    )


def body(grad, momentum, basis):
    zr = ROWS // NZ
    gh = RANK // 2
    gr = gh // (NX * NY)
    square = ((RANK, RANK), F32)
    left, bht = call(
        left_kernel, 0, [((ROWS, RANK), F32), ((COLS, RANK), BF16)], 3,
        [((ROWS, COLS), BF16), ((ROWS, COLS), BF16), ((COLS, RANK), BF16), ((ROWS, RANK), BF16), ((NZ - 1, zr, RANK), BF16)],
        NZ - 1 + 8, 3 * (COLS // CHUNK),
    )(grad, momentum, basis)
    (gram,) = call(
        gram_kernel, 1, [square], 1,
        [square, ((gh, RANK), F32), ((gh, RANK), F32), ((NX * NY - 1, gr, RANK), F32), ((gr, RANK), F32), ((NZ - 1, gr, RANK), F32)],
        2 * (NX * NY - 1) + NZ - 1 + 2,
    )(left)
    shard, ortho = call(
        scatter_kernel, 2, [((BLOCK, RANK), F32), ((ROWS, RANK), BF16)], 3,
        [
            ((2, 2, NX, NY, BLOCK, 128), F32), ((2, NX, NY, BLOCK, 128), F32),
            ((2, 6, 2, BLOCK, 128), F32), ((2, NX, BLOCK, 128), F32), ((2, 6, BLOCK // 2, 128), F32),
        ],
        28,
    )(gram, left, bht)
    right, squares = call(
        gather_kernel, 3, [((2, 2, NX, NY, BLOCK, 128), BF16), ((8, 128), F32)], 1,
        [((8, 128), F32), ((8, 128), F32), ((NX, 8, 128), F32), ((NY, 8, 128), F32), ((NZ, 8, 128), F32)],
        38,
    )(shard)
    step = 896
    return pl.pallas_call(
        output_kernel,
        grid=(COLS // step,),
        out_shape=(
            jax.ShapeDtypeStruct((ROWS, COLS), BF16),
            jax.ShapeDtypeStruct((ROWS, COLS), BF16),
            jax.ShapeDtypeStruct((COLS, RANK), BF16),
        ),
        in_specs=[
            pl.BlockSpec((ROWS, step), lambda i: (0, i)),
            pl.BlockSpec((ROWS, step), lambda i: (0, i)),
            pl.BlockSpec((ROWS, RANK), lambda i: (0, 0)),
            pl.BlockSpec((2, step, 128), lambda i: (0, i, 0)),
            pl.BlockSpec((8, 128), lambda i: (0, 0)),
        ],
        out_specs=(
            pl.BlockSpec((ROWS, step), lambda i: (0, i)),
            pl.BlockSpec((ROWS, step), lambda i: (0, i)),
            pl.BlockSpec((step, RANK), lambda i: (i, 0)),
        ),
        compiler_params=pltpu.CompilerParams(vmem_limit_bytes=VMEM_LIMIT),
        name="output_kernel",
    )(grad, momentum, ortho, right.reshape(2, COLS, 128), squares)


def solution(mesh):
    placed = (P("fsdp", "tp"), P("fsdp", "tp"), P("tp", None))
    return jax.shard_map(
        body,
        mesh=mesh,
        in_specs=placed,
        out_specs=(P("fsdp", "tp"), P("fsdp", "tp"), P("tp", None)),
        check_vma=False,
    )
```

```python
import math

import jax
import jax.numpy as jnp
from jax import lax
from jax.experimental import pallas as pl
from jax.experimental.pallas import tpu as pltpu
from jax.sharding import PartitionSpec as P

M = 8192
N = 28672
RANK = 256
MU = 90

MESH = pl.DeviceIdType.MESH
HI = lax.Precision.HIGHEST
F32 = jnp.float32
BF16 = jnp.bfloat16
NX, NY, NZ = 4, 4, 8
NF = NX * NY * 2
ROWS = M // NF
COLS = N // NZ
CHUNK = 896
BLOCK = COLS // NF
VMEM_LIMIT = 60 * 1024 * 1024


def dot(a, b, ca, cb, precision=None):
    return lax.dot_general(
        a, b, (((ca,), (cb,)), ((), ())), precision=precision, preferred_element_type=F32
    )


def lower_inverse(gram, b=64, s8=8):
    n = gram.shape[0]
    tiles = b // 8
    nt = n // 128
    rows = lax.broadcasted_iota(jnp.int32, (8, 128), 0)
    ln = lax.broadcasted_iota(jnp.int32, (8, 128), 1)
    lanes = lax.broadcasted_iota(jnp.int32, (b, n), 1)
    panels = [gram[p * b:(p + 1) * b, :] for p in range(n // b)]
    done = []
    for p in range(n // b):
        r0 = p * b
        home = r0 // 128
        P_ = panels[p]
        M_ = [[P_[8 * a:8 * a + 8, 128 * l:128 * l + 128] for l in range(nt)] for a in range(tiles)]
        for a in range(tiles):
            M_[a].append(jnp.where(ln + home * 128 == rows + (r0 + 8 * a), 1.0, 0.0))
        piv = [jnp.ones((8, 128), F32) for _ in range(tiles)]
        for s in range(b // s8):
            C = []
            for k in range(s8):
                lane = r0 - home * 128 + s * s8 + k
                C.append([
                    jnp.broadcast_to(M_[a][home][:, lane:lane + 1], (8, 128)) if a >= s else None for a in range(tiles)
                ])
            for j in range(s8):
                sj = jnp.broadcast_to(C[j][s][j:j + 1, :], (8, 128))
                near = pl.reciprocal(sj, approx=True)
                inv = near * (2.0 - sj * near)
                w = [C[j][a] * inv if a >= s else None for a in range(tiles)]
                for k in range(j + 1, s8):
                    bk = jnp.broadcast_to(C[j][s][k:k + 1, :], (8, 128))
                    for a in range(s, tiles):
                        C[k][a] = C[k][a] - w[a] * bk
                w[s] = jnp.where(rows > j, w[s], 0.0)
                piv[s] = jnp.where(rows == j, sj, piv[s])
                for l in range(nt + 1):
                    row = jnp.broadcast_to(M_[s][l][j:j + 1, :], (8, 128))
                    for a in range(s, tiles):
                        M_[a][l] = M_[a][l] - w[a] * row
        full = []
        for a in range(tiles):
            root = lax.rsqrt(piv[a])
            out = [v * root for v in M_[a]]
            ident = out.pop()
            at = ln + home * 128
            out[home] = jnp.where((at >= r0) & (at < r0 + b), ident, out[home])
            full.append(jnp.concatenate(out, axis=1))
        U = jnp.concatenate(full, axis=0)
        done.append(U)
        if p + 1 < n // b:
            r1 = r0 + b
            cut = r1 // 128 * 128
            upd = dot(U[:, cut:], U, 0, 0, HI)
            for q in range(p + 1, n // b):
                old = jnp.where((lanes >= r0) & (lanes < r1), 0.0, panels[q])
                panels[q] = old - upd[q * b - cut:(q + 1) * b - cut, :]
    W = jnp.concatenate(done, axis=0)
    li = lax.broadcasted_iota(jnp.int32, (n, n), 1)
    si = lax.broadcasted_iota(jnp.int32, (n, n), 0)
    return jnp.where(li <= si, W, 0.0)


class Place:
    def __init__(self, ssem, rsem):
        self.ssem, self.rsem = ssem, rsem
        self.sends = []
        self.f = lax.axis_index("fsdp")
        self.t = lax.axis_index("tp")
        self.core = lax.rem(self.f, 2)
        self.other = 1 - self.core
        self.x = lax.rem(self.f // 2, NX)
        self.y = self.f // (2 * NX)
        self.xs = [lax.rem(self.x + j, NX) for j in range(NX)]
        self.ys = [lax.rem(self.y + j, NY) for j in range(NY)]
        self.zs = [lax.rem(self.t + j, NZ) for j in range(NZ)]
        self.sibling = self.dev(self.x, self.y, self.other)
        self.zdev = [(self.f, z) for z in self.zs]
        self.all = [lax.rem(self.f + j, NF) for j in range(NF)]
        self.fdev = [(g, self.t) for g in self.all]
        self.plane = [
            self.dev(self.xs[i], self.ys[j], self.core) for i in range(NX) for j in range(NY) if (i, j) != (0, 0)
        ]
        self.chips = [self.ys[j] * NX + self.xs[i] for i in range(NX) for j in range(NY) if (i, j) != (0, 0)]
        self.chip = self.y * NX + self.x
        self.ways = (
            (self.xs, self.dev(self.xs[1], self.y, self.core), self.dev(self.xs[3], self.y, self.core)),
            (self.ys, self.dev(self.x, self.ys[1], self.core), self.dev(self.x, self.ys[3], self.core)),
        )

    def dev(self, px, py, pc):
        return ((py * NX + px) * 2 + pc, self.t)

    def greet(self, devices):
        barrier = pltpu.get_barrier_semaphore()
        for device in devices:
            pl.semaphore_signal(barrier, inc=1, device_id=device, device_id_type=MESH)
        return lambda: pl.semaphore_wait(barrier, len(devices))

    def exchange(self, src, dst, device):
        k = len(self.sends)
        cp = pltpu.make_async_remote_copy(
            src_ref=src, dst_ref=dst, send_sem=self.ssem.at[k], recv_sem=self.rsem.at[k],
            device_id=device, device_id_type=MESH,
        )
        cp.start()
        self.sends.append(cp)
        return cp

    def share(self, ref, device):
        return self.exchange(ref, ref, device)

    def finish(self):
        for cp in self.sends:
            cp.wait_send()


def piece(z, size):
    return pl.ds(pl.multiple_of(z * size, size), size)


def step_kernel(g_hbm, m_hbm, b_hbm, out, both, inverse, gbuf, mbuf, bbuf, bht, part, rz, left, gpart, rg, own, r2, gram,
                r, rc, r16, f1, sab, f2, sq, qc, qp, qz, load, ssem, rsem):
    at = Place(ssem, rsem)
    core, other, x, y, xs, ys = at.core, at.other, at.x, at.y, at.xs, at.ys
    nc = COLS // CHUNK
    loads = []
    for c in range(nc):
        cols = pl.ds(c * CHUNK, CHUNK)
        three = [
            pltpu.make_async_copy(b_hbm.at[cols, :], bbuf.at[cols, :], load.at[3 * c]),
            pltpu.make_async_copy(g_hbm.at[:, cols], gbuf.at[:, cols], load.at[3 * c + 1]),
            pltpu.make_async_copy(m_hbm.at[:, cols], mbuf.at[:, cols], load.at[3 * c + 2]),
        ]
        for cp in three:
            cp.start()
        loads.append(three)
    ready = at.greet(at.zdev[1:] + at.fdev[1:])
    total = None
    for c in range(nc):
        for cp in loads[c]:
            cp.wait()
        cols = pl.ds(c * CHUNK, CHUNK)
        half = (mbuf[:, cols].astype(F32) + gbuf[:, cols].astype(F32)).astype(BF16)
        gbuf[:, cols] = half
        term = dot(half, bbuf[cols, :], 1, 0)
        total = term if c == 0 else total + term
    part[...] = (total * (1.0 / math.sqrt(N))).astype(BF16)
    ready()
    zr = ROWS // NZ
    cps = [at.exchange(part.at[piece(at.zs[j], zr), :], rz.at[j - 1], at.zdev[j]) for j in range(1, NZ)]
    for c in range(nc):
        cols = pl.ds(c * CHUNK, CHUNK)
        bht[cols, :] = gbuf[:, cols].T
    mine = part[piece(at.t, zr), :].astype(F32)
    for j in range(1, NZ):
        cps[j - 1].wait_recv()
        mine = mine + rz[j - 1].astype(F32)
    mine = mine.astype(BF16)
    left[piece(at.t, zr), :] = mine
    az = [at.share(left.at[piece(at.t, zr), :], at.zdev[j]) for j in range(1, NZ)]

    gr = RANK // NF
    gpart[...] = dot(mine, mine, 0, 0)
    cps = [at.exchange(gpart.at[piece(at.all[j], gr), :], rg.at[j - 1], at.fdev[j]) for j in range(1, NF)]
    acc = gpart[piece(at.f, gr), :]
    for j in range(1, NF):
        cps[j - 1].wait_recv()
        acc = acc + rg[j - 1]
    own[...] = acc
    cps = [at.exchange(own, r2.at[j - 1], at.zdev[j]) for j in range(1, NZ)]

    for cp in az:
        cp.wait_recv()
    wide = COLS // 2
    nk = wide // CHUNK
    qk = NX // nk

    def product(k, pc):
        half = bht[pl.ds(pl.multiple_of(pc * wide + k * CHUNK, 128), CHUNK), :]
        val = dot(half, left[...], 1, 0)
        for h in range(2):
            r[h, pc, k * qk:(k + 1) * qk] = val[:, 128 * h:128 * h + 128].reshape(qk, NY, BLOCK, 128)

    cc = []
    for k in range(nk):
        product(k, other)
        qs = pl.ds(k * qk, qk)
        cc.append([at.exchange(r.at[h, other, qs], rc.at[h, qs], at.sibling) for h in range(2)])
    for j in range(1, NZ):
        cps[j - 1].wait_recv()
        acc = acc + r2[j - 1]
    grow = piece(at.f, gr)
    gram[grow, :] = acc
    ga = [at.share(gram.at[grow, :], at.fdev[j]) for j in range(1, NF)]
    for k in range(nk):
        product(k, core)
    for k in range(nk):
        qs = pl.ds(k * qk, qk)
        for h in range(2):
            cc[k][h].wait_recv()
            total = r[h, core, qs] + rc[h, qs]
            r[h, core, qs] = total
            r16[h, qs] = total.astype(BF16)
    one = [[], []]
    for j in range(1, NX):
        one[0].append(at.exchange(r16.at[0, xs[j]], f1.at[0, j - 1], at.dev(xs[j], y, core)))
        one[1].append(at.exchange(r16.at[1, :, ys[j]], f1.at[1, j - 1], at.dev(x, ys[j], core)))
    for cp in ga:
        cp.wait_recv()
    w = lower_inverse(gram[...])
    two = [[], []]
    for h in range(2):
        total = r[0, core, x] if h == 0 else r[1, core, :, y]
        for j in range(1, NX):
            one[h][j - 1].wait_recv()
            total = total + f1[h, j - 1].astype(F32)
        sab[h] = total
        for j in range(1, NX):
            if h == 0:
                two[h].append(at.exchange(sab.at[h, ys[j]], f2.at[h, j - 1], at.dev(x, ys[j], core)))
            else:
                two[h].append(at.exchange(sab.at[h, xs[j]], f2.at[h, j - 1], at.dev(xs[j], y, core)))
    ortho = dot(left[...].astype(F32), w, 1, 1, HI)
    both[0:ROWS, :] = ortho.astype(BF16)
    halves = []
    for h in range(2):
        total = sab[h, y if h == 0 else x]
        for j in range(1, NX):
            two[h][j - 1].wait_recv()
            total = total + f2[h, j - 1]
        halves.append(total)
    right = dot(jnp.concatenate(halves, axis=1), w, 1, 1, HI)
    rounded = right.astype(BF16)
    for h in range(2):
        out[h, core, x, y] = rounded[:, 128 * h:128 * h + 128]
    g2 = []
    for j in range(1, NX):
        g2.append(at.share(out.at[0, core, x, y], at.dev(x, ys[j], core)))
        g2.append(at.share(out.at[1, core, x, y], at.dev(xs[j], y, core)))
    total = jnp.sum(right * right, axis=0, keepdims=True)
    srow = lax.broadcasted_iota(jnp.int32, (8, 128), 0)
    sq[...] = jnp.where(srow == 0, total[:, :128], total[:, 128:])
    sc = at.exchange(sq, qc, at.sibling)
    sc.wait_recv()
    qp[at.chip] = sq[...] + qc[...]
    sp = [at.share(qp.at[at.chip], device) for device in at.plane]
    for cp in g2:
        cp.wait_recv()

    def band(h, q, k=None):
        if k is None:
            return out.at[0, core, q] if h == 0 else out.at[1, core, :, q]
        return out.at[0, core, q, pl.ds(2 * k, 2)] if h == 0 else out.at[1, core, pl.ds(2 * k, 2), q]

    begun = []
    for h in range(2):
        pos, nxt, prv = at.ways[h]
        begun.append([at.share(band(h, pos[0], 0), nxt), at.share(band(h, pos[0], 1), prv)])
    for h in range(2):
        pos, nxt, prv = at.ways[h]
        begun[h] += [at.share(band(h, pos[0], 1), nxt), at.share(band(h, pos[0], 0), prv)]
    last = [at.share(band(h, at.ways[h][0][0]), at.sibling) for h in range(2)]
    for cp in sp:
        cp.wait_recv()
    total = qp[0]
    for j in range(1, NX * NY):
        total = total + qp[j]
    qz[at.t] = total
    sz = [at.share(qz.at[at.t], at.zdev[j]) for j in range(1, NZ)]
    relays = []
    for h in range(2):
        pos, nxt, prv = at.ways[h]
        begun[h][0].wait_recv()
        relays.append(at.share(band(h, pos[3], 0), nxt))
        begun[h][1].wait_recv()
        relays.append(at.share(band(h, pos[1], 1), prv))
    for cp in sz:
        cp.wait_recv()
    total = qz[0]
    for j in range(1, NZ):
        total = total + qz[j]
    scale = jnp.sqrt(jnp.concatenate([total[0:1, :], total[1:2, :]], axis=1) / N + 1e-06)
    inverse[...] = jnp.broadcast_to(1.0 / scale, (8, RANK))
    both[ROWS:, :] = (ortho * (math.sqrt(M / RANK) / scale)).astype(BF16)
    for h in range(2):
        pos = at.ways[h][0]
        begun[h][2].wait_recv()
        last.append(at.share(band(h, pos[3]), at.sibling))
        begun[h][3].wait_recv()
        last.append(at.share(band(h, pos[1]), at.sibling))
    for h in range(2):
        pos = at.ways[h][0]
        for k in range(2):
            relays[2 * h + k].wait_recv()
            last.append(at.share(band(h, pos[2], k), at.sibling))
    for cp in last:
        cp.wait_recv()
    at.finish()


def output_kernel(g, m, both, right, inverse, update, new_momentum, new_basis):
    rr = jnp.concatenate([right[0], right[1]], axis=1)
    product = dot(both[...], rr, 1, 1)
    buffer = m[...].astype(F32) + g[...].astype(F32)
    new_momentum[...] = (buffer - (1.0 - MU / 100.0) * product[:ROWS]).astype(BF16)
    update[...] = product[ROWS:].astype(BF16)
    new_basis[...] = (rr.astype(F32) * inverse[0:1, :]).astype(BF16)


def body(grad, momentum, basis):
    dma = pltpu.SemaphoreType.DMA
    zr = ROWS // NZ
    gr = RANK // NF
    sends = 7 + 7 + 31 + 7 + 31 + 4 + 6 + 6 + 6 + 1 + 15 + 8 + 2 + 7 + 4 + 8
    right, both, inverse = pl.pallas_call(
        step_kernel,
        out_shape=(
            jax.ShapeDtypeStruct((2, 2, NX, NY, BLOCK, 128), BF16),
            jax.ShapeDtypeStruct((2 * ROWS, RANK), BF16),
            jax.ShapeDtypeStruct((8, RANK), F32),
        ),
        in_specs=[pl.BlockSpec(memory_space=pl.ANY)] * 3,
        out_specs=tuple(pl.BlockSpec(memory_space=pltpu.VMEM) for _ in range(3)),
        scratch_shapes=[
            pltpu.VMEM((ROWS, COLS), BF16), pltpu.VMEM((ROWS, COLS), BF16), pltpu.VMEM((COLS, RANK), BF16),
            pltpu.VMEM((COLS, RANK), BF16),
            pltpu.VMEM((ROWS, RANK), BF16), pltpu.VMEM((NZ - 1, zr, RANK), BF16), pltpu.VMEM((ROWS, RANK), BF16),
            pltpu.VMEM((RANK, RANK), F32), pltpu.VMEM((NF - 1, gr, RANK), F32),
            pltpu.VMEM((gr, RANK), F32), pltpu.VMEM((NZ - 1, gr, RANK), F32), pltpu.VMEM((RANK, RANK), F32),
            pltpu.VMEM((2, 2, NX, NY, BLOCK, 128), F32), pltpu.VMEM((2, NX, NY, BLOCK, 128), F32),
            pltpu.VMEM((2, NX, NY, BLOCK, 128), BF16), pltpu.VMEM((2, 3, 4, BLOCK, 128), BF16),
            pltpu.VMEM((2, 4, BLOCK, 128), F32), pltpu.VMEM((2, 3, BLOCK, 128), F32),
            pltpu.VMEM((8, 128), F32), pltpu.VMEM((8, 128), F32),
            pltpu.VMEM((NX * NY, 8, 128), F32), pltpu.VMEM((NZ, 8, 128), F32),
            dma((3 * (COLS // CHUNK),)), dma((sends,)), dma((sends,)),
        ],
        compiler_params=pltpu.CompilerParams(collective_id=0, has_side_effects=True, vmem_limit_bytes=VMEM_LIMIT),
        name="step_kernel",
    )(grad, momentum, basis)
    step = 512
    return pl.pallas_call(
        output_kernel,
        grid=(COLS // step,),
        out_shape=(
            jax.ShapeDtypeStruct((ROWS, COLS), BF16),
            jax.ShapeDtypeStruct((ROWS, COLS), BF16),
            jax.ShapeDtypeStruct((COLS, RANK), BF16),
        ),
        in_specs=[
            pl.BlockSpec((ROWS, step), lambda i: (0, i)),
            pl.BlockSpec((ROWS, step), lambda i: (0, i)),
            pl.BlockSpec((2 * ROWS, RANK), lambda i: (0, 0)),
            pl.BlockSpec((2, step, 128), lambda i: (0, i, 0)),
            pl.BlockSpec((8, RANK), lambda i: (0, 0)),
        ],
        out_specs=(
            pl.BlockSpec((ROWS, step), lambda i: (0, i)),
            pl.BlockSpec((ROWS, step), lambda i: (0, i)),
            pl.BlockSpec((step, RANK), lambda i: (i, 0)),
        ),
        compiler_params=pltpu.CompilerParams(vmem_limit_bytes=VMEM_LIMIT),
        name="output_kernel",
    )(grad, momentum, both, right.reshape(2, COLS, 128), inverse)


def solution(mesh):
    placed = (P("fsdp", "tp"), P("fsdp", "tp"), P("tp", None))
    return jax.shard_map(
        body,
        mesh=mesh,
        in_specs=placed,
        out_specs=(P("fsdp", "tp"), P("fsdp", "tp"), P("tp", None)),
        check_vma=False,
    )
```

```python
import math

import jax
import jax.numpy as jnp
from jax import lax
from jax.experimental import pallas as pl
from jax.experimental.pallas import tpu as pltpu
from jax.sharding import PartitionSpec as P

M = 8192
N = 28672
RANK = 256
MU = 90

MESH = pl.DeviceIdType.MESH
HI = lax.Precision.HIGHEST
F32 = jnp.float32
BF16 = jnp.bfloat16
NX, NY, NZ = 4, 4, 8
NF = NX * NY * 2
ROWS = M // NF
COLS = N // NZ
CHUNK = 896
BLOCK = COLS // NF
STEP = 512
VMEM_LIMIT = 60 * 1024 * 1024


def dot(a, b, ca, cb, precision=None):
    return lax.dot_general(
        a, b, (((ca,), (cb,)), ((), ())), precision=precision, preferred_element_type=F32
    )


def lane_of(tile, j):
    return jnp.broadcast_to(tile[j:j + 1, :], tile.shape)


def reciprocal(v):
    near = pl.reciprocal(v, approx=True)
    return near * (2.0 - v * near)


def lower_inverse(gram, beside, b=64, s8=8):
    n = gram.shape[0]
    tiles = b // 8
    nt = n // 128
    rows = lax.broadcasted_iota(jnp.int32, (8, 128), 0)
    ln = lax.broadcasted_iota(jnp.int32, (8, 128), 1)
    lanes = lax.broadcasted_iota(jnp.int32, (b, n), 1)
    panels = [gram[p * b:(p + 1) * b, :] for p in range(n // b)]
    done = []
    for p in range(n // b):
        r0 = p * b
        home = r0 // 128
        P_ = panels[p]
        M_ = [[P_[8 * a:8 * a + 8, 128 * l:128 * l + 128] for l in range(nt)] for a in range(tiles)]
        for a in range(tiles):
            M_[a].append(jnp.where(ln + home * 128 == rows + (r0 + 8 * a), 1.0, 0.0))
        piv = [jnp.ones((8, 128), F32) for _ in range(tiles)]
        for s in range(b // s8):
            C = []
            for k in range(s8):
                lane = r0 - home * 128 + s * s8 + k
                C.append([
                    jnp.broadcast_to(M_[a][home][:, lane:lane + 1], (8, 128)) if a >= s else None for a in range(tiles)
                ])
            for j in range(0, s8, 2):
                first, second = C[j], C[j + 1]
                p11 = lane_of(first[s], j)
                p12 = lane_of(first[s], j + 1)
                p22 = lane_of(second[s], j + 1)
                det = p11 * p22 - p12 * p12
                inv1 = reciprocal(p11)
                mult = p12 * inv1
                inv2 = p11 * reciprocal(det)
                w1 = [first[a] * inv1 if a >= s else None for a in range(tiles)]
                w2 = [(second[a] - first[a] * mult) * inv2 if a >= s else None for a in range(tiles)]
                for k in range(j + 2, s8):
                    b1 = lane_of(first[s], k)
                    b2 = lane_of(second[s], k) - b1 * mult
                    for a in range(s, tiles):
                        C[k][a] = (C[k][a] - w1[a] * b1) - w2[a] * b2
                w1[s] = jnp.where(rows > j, w1[s], 0.0)
                w2[s] = jnp.where(rows > j + 1, w2[s], 0.0)
                piv[s] = jnp.where(rows == j, p11, jnp.where(rows == j + 1, det * inv1, piv[s]))
                for l in range(nt + 1):
                    b1 = lane_of(M_[s][l], j)
                    b2 = lane_of(M_[s][l], j + 1) - b1 * mult
                    for a in range(s, tiles):
                        M_[a][l] = (M_[a][l] - w1[a] * b1) - w2[a] * b2
        full = []
        for a in range(tiles):
            root = lax.rsqrt(piv[a])
            out = [v * root for v in M_[a]]
            ident = out.pop()
            at = ln + home * 128
            out[home] = jnp.where((at >= r0) & (at < r0 + b), ident, out[home])
            full.append(jnp.concatenate(out, axis=1))
        U = jnp.concatenate(full, axis=0)
        done.append(U)
        if p + 1 < n // b:
            r1 = r0 + b
            cut = r1 // 128 * 128
            upd = dot(U[:, cut:], U, 0, 0, HI)
            for q in range(p + 1, n // b):
                old = jnp.where((lanes >= r0) & (lanes < r1), 0.0, panels[q])
                panels[q] = old - upd[q * b - cut:(q + 1) * b - cut, :]
            if p in beside:
                beside[p]()
    W = jnp.concatenate(done, axis=0)
    li = lax.broadcasted_iota(jnp.int32, (n, n), 1)
    si = lax.broadcasted_iota(jnp.int32, (n, n), 0)
    return jnp.where(li <= si, W, 0.0)


class Place:
    def __init__(self, ssem, rsem):
        self.ssem, self.rsem = ssem, rsem
        self.sends = []
        self.f = lax.axis_index("fsdp")
        self.t = lax.axis_index("tp")
        self.core = lax.rem(self.f, 2)
        self.other = 1 - self.core
        self.x = lax.rem(self.f // 2, NX)
        self.y = self.f // (2 * NX)
        self.xs = [lax.rem(self.x + j, NX) for j in range(NX)]
        self.ys = [lax.rem(self.y + j, NY) for j in range(NY)]
        self.zs = [lax.rem(self.t + j, NZ) for j in range(NZ)]
        self.sibling = self.dev(self.x, self.y, self.other)
        self.zdev = [(self.f, z) for z in self.zs]
        self.all = [lax.rem(self.f + j, NF) for j in range(NF)]
        self.fdev = [(g, self.t) for g in self.all]
        self.plane = [
            self.dev(self.xs[i], self.ys[j], self.core) for i in range(NX) for j in range(NY) if (i, j) != (0, 0)
        ]
        self.chips = [self.ys[j] * NX + self.xs[i] for i in range(NX) for j in range(NY) if (i, j) != (0, 0)]
        self.chip = self.y * NX + self.x
        self.ways = (
            (self.xs, self.dev(self.xs[1], self.y, self.core), self.dev(self.xs[3], self.y, self.core)),
            (self.ys, self.dev(self.x, self.ys[1], self.core), self.dev(self.x, self.ys[3], self.core)),
        )

    def dev(self, px, py, pc):
        return ((py * NX + px) * 2 + pc, self.t)

    def greet(self, devices):
        barrier = pltpu.get_barrier_semaphore()
        for device in devices:
            pl.semaphore_signal(barrier, inc=1, device_id=device, device_id_type=MESH)
        return lambda: pl.semaphore_wait(barrier, len(devices))

    def exchange(self, src, dst, device):
        k = len(self.sends)
        cp = pltpu.make_async_remote_copy(
            src_ref=src, dst_ref=dst, send_sem=self.ssem.at[k], recv_sem=self.rsem.at[k],
            device_id=device, device_id_type=MESH,
        )
        cp.start()
        self.sends.append(cp)
        return cp

    def share(self, ref, device):
        return self.exchange(ref, ref, device)

    def finish(self):
        for cp in self.sends:
            cp.wait_send()


def piece(z, size):
    return pl.ds(pl.multiple_of(z * size, size), size)


def step_kernel(g_hbm, m_hbm, b_hbm, out, both, inverse, gbuf, mbuf, bbuf, bht, part, rz, left, gpart, rg, own, r2, gram,
                r, rc, r16, f1, sab, f2, sq, qc, qp, qz, load, ssem, rsem):
    at = Place(ssem, rsem)
    core, other, x, y, xs, ys = at.core, at.other, at.x, at.y, at.xs, at.ys
    nc = COLS // CHUNK
    loads = []
    for c in range(nc):
        cols = pl.ds(c * CHUNK, CHUNK)
        three = [
            pltpu.make_async_copy(b_hbm.at[cols, :], bbuf.at[cols, :], load.at[3 * c]),
            pltpu.make_async_copy(g_hbm.at[:, cols], gbuf.at[:, cols], load.at[3 * c + 1]),
            pltpu.make_async_copy(m_hbm.at[:, cols], mbuf.at[:, cols], load.at[3 * c + 2]),
        ]
        for cp in three:
            cp.start()
        loads.append(three)
    ready = at.greet(at.zdev[1:] + at.fdev[1:])
    total = None
    for c in range(nc):
        for cp in loads[c]:
            cp.wait()
        cols = pl.ds(c * CHUNK, CHUNK)
        half = (mbuf[:, cols].astype(F32) + gbuf[:, cols].astype(F32)).astype(BF16)
        gbuf[:, cols] = half
        term = dot(half, bbuf[cols, :], 1, 0)
        total = term if c == 0 else total + term
    part[...] = (total * (1.0 / math.sqrt(N))).astype(BF16)
    ready()
    zr = ROWS // NZ
    cps = [at.exchange(part.at[piece(at.zs[j], zr), :], rz.at[j - 1], at.zdev[j]) for j in range(1, NZ)]
    for c in range(nc):
        cols = pl.ds(c * CHUNK, CHUNK)
        bht[cols, :] = gbuf[:, cols].T
    mine = part[piece(at.t, zr), :].astype(F32)
    for j in range(1, NZ):
        cps[j - 1].wait_recv()
        mine = mine + rz[j - 1].astype(F32)
    mine = mine.astype(BF16)
    left[piece(at.t, zr), :] = mine
    az = [at.share(left.at[piece(at.t, zr), :], at.zdev[j]) for j in range(1, NZ)]

    gr = RANK // NF
    gpart[...] = dot(mine, mine, 0, 0)
    cps = [at.exchange(gpart.at[piece(at.all[j], gr), :], rg.at[j - 1], at.fdev[j]) for j in range(1, NF)]
    acc = gpart[piece(at.f, gr), :]
    for j in range(1, NF):
        cps[j - 1].wait_recv()
        acc = acc + rg[j - 1]
    own[...] = acc
    cps = [at.exchange(own, r2.at[j - 1], at.zdev[j]) for j in range(1, NZ)]

    for cp in az:
        cp.wait_recv()
    wide = COLS // 2
    nk = wide // CHUNK
    qk = NX // nk

    def product(k, pc):
        half = bht[pl.ds(pl.multiple_of(pc * wide + k * CHUNK, 128), CHUNK), :]
        val = dot(half, left[...], 1, 0)
        for h in range(2):
            r[h, pc, k * qk:(k + 1) * qk] = val[:, 128 * h:128 * h + 128].reshape(qk, NY, BLOCK, 128)

    cc = []
    for k in range(nk):
        product(k, other)
        qs = pl.ds(k * qk, qk)
        cc.append([at.exchange(r.at[h, other, qs], rc.at[h, qs], at.sibling) for h in range(2)])
    for j in range(1, NZ):
        cps[j - 1].wait_recv()
        acc = acc + r2[j - 1]
    grow = piece(at.f, gr)
    gram[grow, :] = acc
    ga = [at.share(gram.at[grow, :], at.fdev[j]) for j in range(1, NF)]
    for k in range(nk):
        product(k, core)
    for k in range(nk):
        qs = pl.ds(k * qk, qk)
        for h in range(2):
            cc[k][h].wait_recv()
            total = r[h, core, qs] + rc[h, qs]
            r[h, core, qs] = total
            r16[h, qs] = total.astype(BF16)
    one = [[], []]
    for j in range(1, NX):
        one[0].append(at.exchange(r16.at[0, xs[j]], f1.at[0, j - 1], at.dev(xs[j], y, core)))
        one[1].append(at.exchange(r16.at[1, :, ys[j]], f1.at[1, j - 1], at.dev(x, ys[j], core)))
    for cp in ga:
        cp.wait_recv()
    two = [[], []]

    def second_stage():
        for h in range(2):
            total = r[0, core, x] if h == 0 else r[1, core, :, y]
            for j in range(1, NX):
                one[h][j - 1].wait_recv()
                total = total + f1[h, j - 1].astype(F32)
            sab[h] = total
            for j in range(1, NX):
                if h == 0:
                    two[h].append(at.exchange(sab.at[h, ys[j]], f2.at[h, j - 1], at.dev(x, ys[j], core)))
                else:
                    two[h].append(at.exchange(sab.at[h, xs[j]], f2.at[h, j - 1], at.dev(xs[j], y, core)))

    w = lower_inverse(gram[...], {2: second_stage})
    ortho = dot(left[...].astype(F32), w, 1, 1, HI)
    both[0:ROWS, :] = ortho.astype(BF16)
    halves = []
    for h in range(2):
        total = sab[h, y if h == 0 else x]
        for j in range(1, NX):
            two[h][j - 1].wait_recv()
            total = total + f2[h, j - 1]
        halves.append(total)
    right = dot(jnp.concatenate(halves, axis=1), w, 1, 1, HI)
    rounded = right.astype(BF16)
    for h in range(2):
        out[h, core, x, y] = rounded[:, 128 * h:128 * h + 128]
    g2 = []
    for j in range(1, NX):
        g2.append(at.share(out.at[0, core, x, y], at.dev(x, ys[j], core)))
        g2.append(at.share(out.at[1, core, x, y], at.dev(xs[j], y, core)))
    total = jnp.sum(right * right, axis=0, keepdims=True)
    srow = lax.broadcasted_iota(jnp.int32, (8, 128), 0)
    sq[...] = jnp.where(srow == 0, total[:, :128], total[:, 128:])
    sc = at.exchange(sq, qc, at.sibling)
    sc.wait_recv()
    qp[at.chip] = sq[...] + qc[...]
    sp = [at.share(qp.at[at.chip], device) for device in at.plane]
    for cp in g2:
        cp.wait_recv()

    def band(h, q, k=None):
        if k is None:
            return out.at[0, core, q] if h == 0 else out.at[1, core, :, q]
        return out.at[0, core, q, pl.ds(2 * k, 2)] if h == 0 else out.at[1, core, pl.ds(2 * k, 2), q]

    begun = []
    for h in range(2):
        pos, nxt, prv = at.ways[h]
        begun.append([at.share(band(h, pos[0], 0), nxt), at.share(band(h, pos[0], 1), prv)])
    for h in range(2):
        pos, nxt, prv = at.ways[h]
        begun[h] += [at.share(band(h, pos[0], 1), nxt), at.share(band(h, pos[0], 0), prv)]
    last = [at.share(band(h, at.ways[h][0][0]), at.sibling) for h in range(2)]
    for cp in sp:
        cp.wait_recv()
    total = qp[0]
    for j in range(1, NX * NY):
        total = total + qp[j]
    qz[at.t] = total
    sz = [at.share(qz.at[at.t], at.zdev[j]) for j in range(1, NZ)]
    relays = []
    for h in range(2):
        pos, nxt, prv = at.ways[h]
        begun[h][0].wait_recv()
        relays.append(at.share(band(h, pos[3], 0), nxt))
        begun[h][1].wait_recv()
        relays.append(at.share(band(h, pos[1], 1), prv))
    for cp in sz:
        cp.wait_recv()
    total = qz[0]
    for j in range(1, NZ):
        total = total + qz[j]
    scale = jnp.sqrt(jnp.concatenate([total[0:1, :], total[1:2, :]], axis=1) / N + 1e-06)
    inverse[...] = jnp.broadcast_to(1.0 / scale, (8, RANK))
    both[ROWS:, :] = (ortho * (math.sqrt(M / RANK) / scale)).astype(BF16)
    for h in range(2):
        pos = at.ways[h][0]
        begun[h][2].wait_recv()
        last.append(at.share(band(h, pos[3]), at.sibling))
        begun[h][3].wait_recv()
        last.append(at.share(band(h, pos[1]), at.sibling))
    for h in range(2):
        pos = at.ways[h][0]
        for k in range(2):
            relays[2 * h + k].wait_recv()
            last.append(at.share(band(h, pos[2], k), at.sibling))
    for cp in last:
        cp.wait_recv()
    at.finish()


def output_kernel(g_hbm, m_hbm, both_hbm, right_hbm, inv_hbm, update, new_momentum, new_basis,
                  gbuf, mbuf, both, rbuf, inv, ubuf, nbuf, bbuf, load, store):
    nc = COLS // STEP
    first = [
        pltpu.make_async_copy(both_hbm, both, load.at[4 * nc]),
        pltpu.make_async_copy(inv_hbm, inv, load.at[4 * nc + 1]),
    ]
    loads = []
    for c in range(nc):
        cols = pl.ds(c * STEP, STEP)
        loads.append([
            pltpu.make_async_copy(right_hbm.at[0, cols, :], rbuf.at[0, cols, :], load.at[4 * c]),
            pltpu.make_async_copy(right_hbm.at[1, cols, :], rbuf.at[1, cols, :], load.at[4 * c + 1]),
            pltpu.make_async_copy(g_hbm.at[:, cols], gbuf.at[:, cols], load.at[4 * c + 2]),
            pltpu.make_async_copy(m_hbm.at[:, cols], mbuf.at[:, cols], load.at[4 * c + 3]),
        ])
    for cp in first:
        cp.start()
    for group in loads:
        for cp in group:
            cp.start()
    for cp in first:
        cp.wait()
    stores = []
    for c in range(nc):
        cols = pl.ds(c * STEP, STEP)
        for cp in loads[c]:
            cp.wait()
        rr = jnp.concatenate([rbuf[0, cols, :], rbuf[1, cols, :]], axis=1)
        bbuf[cols, :] = (rr.astype(F32) * inv[0:1, :]).astype(BF16)
        product = dot(both[...], rr, 1, 1)
        ubuf[:, cols] = product[ROWS:].astype(BF16)
        buffer = mbuf[:, cols].astype(F32) + gbuf[:, cols].astype(F32)
        nbuf[:, cols] = (buffer - (1.0 - MU / 100.0) * product[:ROWS]).astype(BF16)
        three = [
            pltpu.make_async_copy(bbuf.at[cols, :], new_basis.at[cols, :], store.at[3 * c]),
            pltpu.make_async_copy(ubuf.at[:, cols], update.at[:, cols], store.at[3 * c + 1]),
            pltpu.make_async_copy(nbuf.at[:, cols], new_momentum.at[:, cols], store.at[3 * c + 2]),
        ]
        for cp in three:
            cp.start()
        stores += three
    for cp in stores:
        cp.wait()


def body(grad, momentum, basis):
    dma = pltpu.SemaphoreType.DMA
    zr = ROWS // NZ
    gr = RANK // NF
    sends = 7 + 7 + 31 + 7 + 31 + 4 + 6 + 6 + 6 + 1 + 15 + 8 + 2 + 7 + 4 + 8
    right, both, inverse = pl.pallas_call(
        step_kernel,
        out_shape=(
            jax.ShapeDtypeStruct((2, 2, NX, NY, BLOCK, 128), BF16),
            jax.ShapeDtypeStruct((2 * ROWS, RANK), BF16),
            jax.ShapeDtypeStruct((8, RANK), F32),
        ),
        in_specs=[pl.BlockSpec(memory_space=pl.ANY)] * 3,
        out_specs=tuple(pl.BlockSpec(memory_space=pltpu.VMEM) for _ in range(3)),
        scratch_shapes=[
            pltpu.VMEM((ROWS, COLS), BF16), pltpu.VMEM((ROWS, COLS), BF16), pltpu.VMEM((COLS, RANK), BF16),
            pltpu.VMEM((COLS, RANK), BF16),
            pltpu.VMEM((ROWS, RANK), BF16), pltpu.VMEM((NZ - 1, zr, RANK), BF16), pltpu.VMEM((ROWS, RANK), BF16),
            pltpu.VMEM((RANK, RANK), F32), pltpu.VMEM((NF - 1, gr, RANK), F32),
            pltpu.VMEM((gr, RANK), F32), pltpu.VMEM((NZ - 1, gr, RANK), F32), pltpu.VMEM((RANK, RANK), F32),
            pltpu.VMEM((2, 2, NX, NY, BLOCK, 128), F32), pltpu.VMEM((2, NX, NY, BLOCK, 128), F32),
            pltpu.VMEM((2, NX, NY, BLOCK, 128), BF16), pltpu.VMEM((2, 3, 4, BLOCK, 128), BF16),
            pltpu.VMEM((2, 4, BLOCK, 128), F32), pltpu.VMEM((2, 3, BLOCK, 128), F32),
            pltpu.VMEM((8, 128), F32), pltpu.VMEM((8, 128), F32),
            pltpu.VMEM((NX * NY, 8, 128), F32), pltpu.VMEM((NZ, 8, 128), F32),
            dma((3 * (COLS // CHUNK),)), dma((sends,)), dma((sends,)),
        ],
        compiler_params=pltpu.CompilerParams(collective_id=0, has_side_effects=True, vmem_limit_bytes=VMEM_LIMIT),
        name="step_kernel",
    )(grad, momentum, basis)
    nc = COLS // STEP
    wide = pltpu.VMEM((ROWS, COLS), BF16)
    return pl.pallas_call(
        output_kernel,
        out_shape=(
            jax.ShapeDtypeStruct((ROWS, COLS), BF16),
            jax.ShapeDtypeStruct((ROWS, COLS), BF16),
            jax.ShapeDtypeStruct((COLS, RANK), BF16),
        ),
        in_specs=[pl.BlockSpec(memory_space=pl.ANY)] * 5,
        out_specs=tuple(pl.BlockSpec(memory_space=pl.ANY) for _ in range(3)),
        scratch_shapes=[
            wide, wide, pltpu.VMEM((2 * ROWS, RANK), BF16), pltpu.VMEM((2, COLS, 128), BF16), pltpu.VMEM((8, RANK), F32),
            wide, wide, pltpu.VMEM((COLS, RANK), BF16),
            dma((4 * nc + 2,)), dma((3 * nc,)),
        ],
        compiler_params=pltpu.CompilerParams(vmem_limit_bytes=VMEM_LIMIT),
        name="output_kernel",
    )(grad, momentum, both, right.reshape(2, COLS, 128), inverse)


def solution(mesh):
    placed = (P("fsdp", "tp"), P("fsdp", "tp"), P("tp", None))
    return jax.shard_map(
        body,
        mesh=mesh,
        in_specs=placed,
        out_specs=(P("fsdp", "tp"), P("fsdp", "tp"), P("tp", None)),
        check_vma=False,
    )
```

```python
import math

import jax
import jax.numpy as jnp
from jax import lax
from jax.experimental import pallas as pl
from jax.experimental.pallas import tpu as pltpu
from jax.sharding import PartitionSpec as P

M = 8192
N = 28672
RANK = 256
MU = 90

MESH = pl.DeviceIdType.MESH
HI = lax.Precision.HIGHEST
F32 = jnp.float32
BF16 = jnp.bfloat16
NX, NY, NZ = 4, 4, 8
NF = NX * NY * 2
ROWS = M // NF
COLS = N // NZ
CHUNK = 896
BLOCK = COLS // NF
STEP = 512
VMEM_LIMIT = 60 * 1024 * 1024


def dot(a, b, ca, cb, precision=None):
    return lax.dot_general(
        a, b, (((ca,), (cb,)), ((), ())), precision=precision, preferred_element_type=F32
    )


def lane_of(tile, j):
    return jnp.broadcast_to(tile[j:j + 1, :], tile.shape)


def reciprocal(v):
    near = pl.reciprocal(v, approx=True)
    return near * (2.0 - v * near)


def lower_inverse(gram, beside, b=64, s8=8):
    n = gram.shape[0]
    tiles = b // 8
    nt = n // 128
    rows = lax.broadcasted_iota(jnp.int32, (8, 128), 0)
    ln = lax.broadcasted_iota(jnp.int32, (8, 128), 1)
    lanes = lax.broadcasted_iota(jnp.int32, (b, n), 1)
    panels = [gram[p * b:(p + 1) * b, :] for p in range(n // b)]
    done = []
    for p in range(n // b):
        r0 = p * b
        home = r0 // 128
        P_ = panels[p]
        M_ = [[P_[8 * a:8 * a + 8, 128 * l:128 * l + 128] for l in range(nt)] for a in range(tiles)]
        for a in range(tiles):
            M_[a].append(jnp.where(ln + home * 128 == rows + (r0 + 8 * a), 1.0, 0.0))
        piv = [jnp.ones((8, 128), F32) for _ in range(tiles)]
        for s in range(b // s8):
            C = []
            for k in range(s8):
                lane = r0 - home * 128 + s * s8 + k
                C.append([
                    jnp.broadcast_to(M_[a][home][:, lane:lane + 1], (8, 128)) if a >= s else None for a in range(tiles)
                ])
            for j in range(0, s8, 2):
                first, second = C[j], C[j + 1]
                p11 = lane_of(first[s], j)
                p12 = lane_of(first[s], j + 1)
                p22 = lane_of(second[s], j + 1)
                det = p11 * p22 - p12 * p12
                inv1 = reciprocal(p11)
                mult = p12 * inv1
                inv2 = p11 * reciprocal(det)
                w1 = [first[a] * inv1 if a >= s else None for a in range(tiles)]
                w2 = [(second[a] - first[a] * mult) * inv2 if a >= s else None for a in range(tiles)]
                for k in range(j + 2, s8):
                    b1 = lane_of(first[s], k)
                    b2 = lane_of(second[s], k) - b1 * mult
                    for a in range(s, tiles):
                        C[k][a] = (C[k][a] - w1[a] * b1) - w2[a] * b2
                w1[s] = jnp.where(rows > j, w1[s], 0.0)
                w2[s] = jnp.where(rows > j + 1, w2[s], 0.0)
                piv[s] = jnp.where(rows == j, p11, jnp.where(rows == j + 1, det * inv1, piv[s]))
                for l in range(nt + 1):
                    b1 = lane_of(M_[s][l], j)
                    b2 = lane_of(M_[s][l], j + 1) - b1 * mult
                    for a in range(s, tiles):
                        M_[a][l] = (M_[a][l] - w1[a] * b1) - w2[a] * b2
        full = []
        for a in range(tiles):
            root = lax.rsqrt(piv[a])
            out = [v * root for v in M_[a]]
            ident = out.pop()
            at = ln + home * 128
            out[home] = jnp.where((at >= r0) & (at < r0 + b), ident, out[home])
            full.append(jnp.concatenate(out, axis=1))
        U = jnp.concatenate(full, axis=0)
        done.append(U)
        if p + 1 < n // b:
            r1 = r0 + b
            cut = r1 // 128 * 128
            upd = dot(U[:, cut:], U, 0, 0, HI)
            for q in range(p + 1, n // b):
                old = jnp.where((lanes >= r0) & (lanes < r1), 0.0, panels[q])
                panels[q] = old - upd[q * b - cut:(q + 1) * b - cut, :]
            if p in beside:
                beside[p]()
    W = jnp.concatenate(done, axis=0)
    li = lax.broadcasted_iota(jnp.int32, (n, n), 1)
    si = lax.broadcasted_iota(jnp.int32, (n, n), 0)
    return jnp.where(li <= si, W, 0.0)


class Place:
    def __init__(self, ssem, rsem):
        self.ssem, self.rsem = ssem, rsem
        self.sends = []
        self.f = lax.axis_index("fsdp")
        self.t = lax.axis_index("tp")
        self.core = lax.rem(self.f, 2)
        self.other = 1 - self.core
        self.x = lax.rem(self.f // 2, NX)
        self.y = self.f // (2 * NX)
        self.xs = [lax.rem(self.x + j, NX) for j in range(NX)]
        self.ys = [lax.rem(self.y + j, NY) for j in range(NY)]
        self.zs = [lax.rem(self.t + j, NZ) for j in range(NZ)]
        self.sibling = self.dev(self.x, self.y, self.other)
        self.zdev = [(self.f, z) for z in self.zs]
        self.all = [lax.rem(self.f + j, NF) for j in range(NF)]
        self.fdev = [(g, self.t) for g in self.all]
        self.plane = [
            self.dev(self.xs[i], self.ys[j], self.core) for i in range(NX) for j in range(NY) if (i, j) != (0, 0)
        ]
        self.chips = [self.ys[j] * NX + self.xs[i] for i in range(NX) for j in range(NY) if (i, j) != (0, 0)]
        self.chip = self.y * NX + self.x
        self.ways = (
            (self.xs, self.dev(self.xs[1], self.y, self.core), self.dev(self.xs[3], self.y, self.core)),
            (self.ys, self.dev(self.x, self.ys[1], self.core), self.dev(self.x, self.ys[3], self.core)),
        )

    def dev(self, px, py, pc):
        return ((py * NX + px) * 2 + pc, self.t)

    def greet(self, devices):
        barrier = pltpu.get_barrier_semaphore()
        for device in devices:
            pl.semaphore_signal(barrier, inc=1, device_id=device, device_id_type=MESH)
        return lambda: pl.semaphore_wait(barrier, len(devices))

    def exchange(self, src, dst, device):
        k = len(self.sends)
        cp = pltpu.make_async_remote_copy(
            src_ref=src, dst_ref=dst, send_sem=self.ssem.at[k], recv_sem=self.rsem.at[k],
            device_id=device, device_id_type=MESH,
        )
        cp.start()
        self.sends.append(cp)
        return cp

    def share(self, ref, device):
        return self.exchange(ref, ref, device)

    def finish(self):
        for cp in self.sends:
            cp.wait_send()


def piece(z, size):
    return pl.ds(pl.multiple_of(z * size, size), size)


def step_kernel(g_hbm, m_hbm, b_hbm, result, both, inverse, gbuf, mbuf, bbuf, bht, part, rz, left, gpart, rg, own, r2, gram,
                out, rs, r, rc, r16, f1, sab, s16, f2, sq, qc, qp, qz, load, store, ssem, rsem):
    at = Place(ssem, rsem)
    core, other, x, y, xs, ys = at.core, at.other, at.x, at.y, at.xs, at.ys
    nc = COLS // STEP
    loads = []
    for c in range(nc):
        cols = pl.ds(c * STEP, STEP)
        three = [
            pltpu.make_async_copy(b_hbm.at[cols, :], bbuf.at[cols, :], load.at[3 * c]),
            pltpu.make_async_copy(g_hbm.at[:, cols], gbuf.at[:, cols], load.at[3 * c + 1]),
            pltpu.make_async_copy(m_hbm.at[:, cols], mbuf.at[:, cols], load.at[3 * c + 2]),
        ]
        for cp in three:
            cp.start()
        loads.append(three)
    ready = at.greet(at.zdev[1:] + at.fdev[1:])
    total = None
    for c in range(nc):
        for cp in loads[c]:
            cp.wait()
        cols = pl.ds(c * STEP, STEP)
        half = (mbuf[:, cols].astype(F32) + gbuf[:, cols].astype(F32)).astype(BF16)
        gbuf[:, cols] = half
        term = dot(half, bbuf[cols, :], 1, 0)
        total = term if c == 0 else total + term
    part[...] = (total * (1.0 / math.sqrt(N))).astype(BF16)
    ready()
    zr = ROWS // NZ
    cps = [at.exchange(part.at[piece(at.zs[j], zr), :], rz.at[j - 1], at.zdev[j]) for j in range(1, NZ)]
    for c in range(nc):
        cols = pl.ds(c * STEP, STEP)
        bht[cols, :] = gbuf[:, cols].T
    mine = part[piece(at.t, zr), :].astype(F32)
    for j in range(1, NZ):
        cps[j - 1].wait_recv()
        mine = mine + rz[j - 1].astype(F32)
    mine = mine.astype(BF16)
    left[piece(at.t, zr), :] = mine
    az = [at.share(left.at[piece(at.t, zr), :], at.zdev[j]) for j in range(1, NZ)]

    gr = RANK // NF
    gpart[...] = dot(mine, mine, 0, 0)
    cps = [at.exchange(gpart.at[piece(at.all[j], gr), :], rg.at[j - 1], at.fdev[j]) for j in range(1, NF)]
    acc = gpart[piece(at.f, gr), :]
    for j in range(1, NF):
        cps[j - 1].wait_recv()
        acc = acc + rg[j - 1]
    own[...] = acc
    cps = [at.exchange(own, r2.at[j - 1], at.zdev[j]) for j in range(1, NZ)]

    for cp in az:
        cp.wait_recv()
    wide = COLS // 2
    nk = wide // CHUNK
    qk = NX // nk

    def product(k, pc, into):
        half = bht[pl.ds(pl.multiple_of(pc * wide + k * CHUNK, 128), CHUNK), :]
        val = dot(half, left[...], 1, 0)
        for h in range(2):
            into[h, k * qk:(k + 1) * qk] = val[:, 128 * h:128 * h + 128].reshape(qk, NY, BLOCK, 128).astype(into.dtype)

    cc = []
    for k in range(nk):
        product(k, other, rs)
        qs = pl.ds(k * qk, qk)
        cc.append([at.exchange(rs.at[h, qs], rc.at[h, qs], at.sibling) for h in range(2)])
    for j in range(1, NZ):
        cps[j - 1].wait_recv()
        acc = acc + r2[j - 1]
    grow = piece(at.f, gr)
    gram[grow, :] = acc
    ga = [at.share(gram.at[grow, :], at.fdev[j]) for j in range(1, NF)]
    for k in range(nk):
        product(k, core, r)
    for k in range(nk):
        qs = pl.ds(k * qk, qk)
        for h in range(2):
            cc[k][h].wait_recv()
            total = r[h, qs] + rc[h, qs].astype(F32)
            r[h, qs] = total
            r16[h, qs] = total.astype(BF16)
    one = [[], []]
    for j in range(1, NX):
        one[0].append(at.exchange(r16.at[0, xs[j]], f1.at[0, j - 1], at.dev(xs[j], y, core)))
        one[1].append(at.exchange(r16.at[1, :, ys[j]], f1.at[1, j - 1], at.dev(x, ys[j], core)))
    for cp in ga:
        cp.wait_recv()
    two = [[], []]

    def second_stage():
        for h in range(2):
            total = r[0, x] if h == 0 else r[1, :, y]
            for j in range(1, NX):
                one[h][j - 1].wait_recv()
                total = total + f1[h, j - 1].astype(F32)
            sab[h] = total
            s16[h] = total.astype(BF16)
            for j in range(1, NX):
                if h == 0:
                    two[h].append(at.exchange(s16.at[h, ys[j]], f2.at[h, j - 1], at.dev(x, ys[j], core)))
                else:
                    two[h].append(at.exchange(s16.at[h, xs[j]], f2.at[h, j - 1], at.dev(xs[j], y, core)))

    w = lower_inverse(gram[...], {2: second_stage})
    ortho = dot(left[...].astype(F32), w, 1, 1, HI)
    both[0:ROWS, :] = ortho.astype(BF16)
    halves = []
    for h in range(2):
        total = sab[h, y if h == 0 else x]
        for j in range(1, NX):
            two[h][j - 1].wait_recv()
            total = total + f2[h, j - 1].astype(F32)
        halves.append(total)
    right = dot(jnp.concatenate(halves, axis=1), w, 1, 1, HI)
    rounded = right.astype(BF16)
    for h in range(2):
        out[h, core, x, y] = rounded[:, 128 * h:128 * h + 128]
    g2 = []
    for j in range(1, NX):
        g2.append(at.share(out.at[0, core, x, y], at.dev(x, ys[j], core)))
        g2.append(at.share(out.at[1, core, x, y], at.dev(xs[j], y, core)))
    total = jnp.sum(right * right, axis=0, keepdims=True)
    srow = lax.broadcasted_iota(jnp.int32, (8, 128), 0)
    sq[...] = jnp.where(srow == 0, total[:, :128], total[:, 128:])
    sc = at.exchange(sq, qc, at.sibling)
    sc.wait_recv()
    qp[at.chip] = sq[...] + qc[...]
    sp = [at.share(qp.at[at.chip], device) for device in at.plane]
    for cp in g2:
        cp.wait_recv()

    def band(h, q, k=None, ref=out, pc=core):
        if k is None:
            return ref.at[0, pc, q] if h == 0 else ref.at[1, pc, :, q]
        return ref.at[0, pc, q, pl.ds(2 * k, 2)] if h == 0 else ref.at[1, pc, pl.ds(2 * k, 2), q]

    last, spans, stores = [], [], []

    def keep(h, q, k, pc):
        cp = pltpu.make_async_copy(band(h, q, k, out, pc), band(h, q, k, result, pc), store.at[len(stores)])
        cp.start()
        stores.append(cp)

    def forward(h, q, k=None):
        last.append(at.share(band(h, q, k), at.sibling))
        spans.append((h, q, k))
        keep(h, q, k, core)

    begun = []
    for h in range(2):
        pos, nxt, prv = at.ways[h]
        begun.append([at.share(band(h, pos[0], 0), nxt), at.share(band(h, pos[0], 1), prv)])
    for h in range(2):
        pos, nxt, prv = at.ways[h]
        begun[h] += [at.share(band(h, pos[0], 1), nxt), at.share(band(h, pos[0], 0), prv)]
    for h in range(2):
        forward(h, at.ways[h][0][0])
    for cp in sp:
        cp.wait_recv()
    total = qp[0]
    for j in range(1, NX * NY):
        total = total + qp[j]
    qz[at.t] = total
    sz = [at.share(qz.at[at.t], at.zdev[j]) for j in range(1, NZ)]
    relays = []
    for h in range(2):
        pos, nxt, prv = at.ways[h]
        begun[h][0].wait_recv()
        relays.append(at.share(band(h, pos[3], 0), nxt))
        begun[h][1].wait_recv()
        relays.append(at.share(band(h, pos[1], 1), prv))
    for cp in sz:
        cp.wait_recv()
    total = qz[0]
    for j in range(1, NZ):
        total = total + qz[j]
    scale = jnp.sqrt(jnp.concatenate([total[0:1, :], total[1:2, :]], axis=1) / N + 1e-06)
    inverse[...] = jnp.broadcast_to(1.0 / scale, (8, RANK))
    both[ROWS:, :] = (ortho * (math.sqrt(M / RANK) / scale)).astype(BF16)
    for h in range(2):
        pos = at.ways[h][0]
        begun[h][2].wait_recv()
        forward(h, pos[3])
        begun[h][3].wait_recv()
        forward(h, pos[1])
    for h in range(2):
        pos = at.ways[h][0]
        for k in range(2):
            relays[2 * h + k].wait_recv()
            forward(h, pos[2], k)
    for cp, (h, q, k) in zip(last, spans):
        cp.wait_recv()
        keep(h, q, k, other)
    at.finish()
    for cp in stores:
        cp.wait()


def output_kernel(g_hbm, m_hbm, both_hbm, right_hbm, inv_hbm, update, new_momentum, new_basis,
                  gbuf, mbuf, both, rbuf, inv, ubuf, nbuf, bbuf, load, store):
    nc = COLS // STEP
    first = [
        pltpu.make_async_copy(both_hbm, both, load.at[4 * nc]),
        pltpu.make_async_copy(inv_hbm, inv, load.at[4 * nc + 1]),
    ]
    loads = []
    for c in range(nc):
        cols = pl.ds(c * STEP, STEP)
        loads.append([
            pltpu.make_async_copy(right_hbm.at[0, cols, :], rbuf.at[0, cols, :], load.at[4 * c]),
            pltpu.make_async_copy(right_hbm.at[1, cols, :], rbuf.at[1, cols, :], load.at[4 * c + 1]),
            pltpu.make_async_copy(g_hbm.at[:, cols], gbuf.at[:, cols], load.at[4 * c + 2]),
            pltpu.make_async_copy(m_hbm.at[:, cols], mbuf.at[:, cols], load.at[4 * c + 3]),
        ])
    for cp in first:
        cp.start()
    for group in loads:
        for cp in group:
            cp.start()
    for cp in first:
        cp.wait()
    stores = []
    for c in range(nc):
        cols = pl.ds(c * STEP, STEP)
        for cp in loads[c]:
            cp.wait()
        rr = jnp.concatenate([rbuf[0, cols, :], rbuf[1, cols, :]], axis=1)
        bbuf[cols, :] = (rr.astype(F32) * inv[0:1, :]).astype(BF16)
        product = dot(both[...], rr, 1, 1)
        ubuf[:, cols] = product[ROWS:].astype(BF16)
        buffer = mbuf[:, cols].astype(F32) + gbuf[:, cols].astype(F32)
        nbuf[:, cols] = (buffer - (1.0 - MU / 100.0) * product[:ROWS]).astype(BF16)
        three = [
            pltpu.make_async_copy(bbuf.at[cols, :], new_basis.at[cols, :], store.at[3 * c]),
            pltpu.make_async_copy(ubuf.at[:, cols], update.at[:, cols], store.at[3 * c + 1]),
            pltpu.make_async_copy(nbuf.at[:, cols], new_momentum.at[:, cols], store.at[3 * c + 2]),
        ]
        for cp in three:
            cp.start()
        stores += three
    for cp in stores:
        cp.wait()


def body(grad, momentum, basis):
    dma = pltpu.SemaphoreType.DMA
    zr = ROWS // NZ
    gr = RANK // NF
    sends = 7 + 7 + 31 + 7 + 31 + 4 + 6 + 6 + 6 + 1 + 15 + 8 + 2 + 7 + 4 + 8
    right, both, inverse = pl.pallas_call(
        step_kernel,
        out_shape=(
            jax.ShapeDtypeStruct((2, 2, NX, NY, BLOCK, 128), BF16),
            jax.ShapeDtypeStruct((2 * ROWS, RANK), BF16),
            jax.ShapeDtypeStruct((8, RANK), F32),
        ),
        in_specs=[pl.BlockSpec(memory_space=pl.ANY)] * 3,
        out_specs=tuple(pl.BlockSpec(memory_space=v) for v in (pl.ANY, pltpu.VMEM, pltpu.VMEM)),
        scratch_shapes=[
            pltpu.VMEM((ROWS, COLS), BF16), pltpu.VMEM((ROWS, COLS), BF16), pltpu.VMEM((COLS, RANK), BF16),
            pltpu.VMEM((COLS, RANK), BF16),
            pltpu.VMEM((ROWS, RANK), BF16), pltpu.VMEM((NZ - 1, zr, RANK), BF16), pltpu.VMEM((ROWS, RANK), BF16),
            pltpu.VMEM((RANK, RANK), F32), pltpu.VMEM((NF - 1, gr, RANK), F32),
            pltpu.VMEM((gr, RANK), F32), pltpu.VMEM((NZ - 1, gr, RANK), F32), pltpu.VMEM((RANK, RANK), F32),
            pltpu.VMEM((2, 2, NX, NY, BLOCK, 128), BF16), pltpu.VMEM((2, NX, NY, BLOCK, 128), BF16),
            pltpu.VMEM((2, NX, NY, BLOCK, 128), F32), pltpu.VMEM((2, NX, NY, BLOCK, 128), BF16),
            pltpu.VMEM((2, NX, NY, BLOCK, 128), BF16), pltpu.VMEM((2, 3, 4, BLOCK, 128), BF16),
            pltpu.VMEM((2, 4, BLOCK, 128), F32), pltpu.VMEM((2, 4, BLOCK, 128), BF16), pltpu.VMEM((2, 3, BLOCK, 128), BF16),
            pltpu.VMEM((8, 128), F32), pltpu.VMEM((8, 128), F32),
            pltpu.VMEM((NX * NY, 8, 128), F32), pltpu.VMEM((NZ, 8, 128), F32),
            dma((3 * (COLS // STEP),)), dma((20,)), dma((sends,)), dma((sends,)),
        ],
        compiler_params=pltpu.CompilerParams(collective_id=0, has_side_effects=True, vmem_limit_bytes=VMEM_LIMIT),
        name="step_kernel",
    )(grad, momentum, basis)
    nc = COLS // STEP
    wide = pltpu.VMEM((ROWS, COLS), BF16)
    return pl.pallas_call(
        output_kernel,
        out_shape=(
            jax.ShapeDtypeStruct((ROWS, COLS), BF16),
            jax.ShapeDtypeStruct((ROWS, COLS), BF16),
            jax.ShapeDtypeStruct((COLS, RANK), BF16),
        ),
        in_specs=[pl.BlockSpec(memory_space=pl.ANY)] * 5,
        out_specs=tuple(pl.BlockSpec(memory_space=pl.ANY) for _ in range(3)),
        scratch_shapes=[
            wide, wide, pltpu.VMEM((2 * ROWS, RANK), BF16), pltpu.VMEM((2, COLS, 128), BF16), pltpu.VMEM((8, RANK), F32),
            wide, wide, pltpu.VMEM((COLS, RANK), BF16),
            dma((4 * nc + 2,)), dma((3 * nc,)),
        ],
        compiler_params=pltpu.CompilerParams(vmem_limit_bytes=VMEM_LIMIT),
        name="output_kernel",
    )(grad, momentum, both, right.reshape(2, COLS, 128), inverse)


def solution(mesh):
    placed = (P("fsdp", "tp"), P("fsdp", "tp"), P("tp", None))
    return jax.shard_map(
        body,
        mesh=mesh,
        in_specs=placed,
        out_specs=(P("fsdp", "tp"), P("fsdp", "tp"), P("tp", None)),
        check_vma=False,
    )
```

```python
import math

import jax
import jax.numpy as jnp
from jax import lax
from jax.experimental import pallas as pl
from jax.experimental.pallas import tpu as pltpu
from jax.sharding import PartitionSpec as P

M = 8192
N = 28672
RANK = 256
MU = 90

MESH = pl.DeviceIdType.MESH
HI = lax.Precision.HIGHEST
F32 = jnp.float32
BF16 = jnp.bfloat16
NX, NY, NZ = 4, 4, 8
NF = NX * NY * 2
ROWS = M // NF
COLS = N // NZ
CHUNK = 896
BLOCK = COLS // NF
STEP = 512
VMEM_LIMIT = 60 * 1024 * 1024


def dot(a, b, ca, cb, precision=None):
    return lax.dot_general(
        a, b, (((ca,), (cb,)), ((), ())), precision=precision, preferred_element_type=F32
    )


def lane_of(tile, j):
    return jnp.broadcast_to(tile[j:j + 1, :], tile.shape)


def column_of(tile, j):
    return jnp.broadcast_to(tile[:, j:j + 1], tile.shape)


def reciprocal(v):
    near = pl.reciprocal(v, approx=True)
    return near * (2.0 - v * near)


def lower_inverse(gram, beside, b=64, s8=8):
    n = gram.shape[0]
    tiles = b // 8
    nt = n // 128
    rows = lax.broadcasted_iota(jnp.int32, (8, 128), 0)
    ln = lax.broadcasted_iota(jnp.int32, (8, 128), 1)
    lanes = lax.broadcasted_iota(jnp.int32, (b, n), 1)
    panels = [gram[p * b:(p + 1) * b, :] for p in range(n // b)]
    done = []
    for p in range(n // b):
        r0 = p * b
        home = r0 // 128
        P_ = panels[p]
        M_ = [[P_[8 * a:8 * a + 8, 128 * l:128 * l + 128] for l in range(nt)] for a in range(tiles)]
        for a in range(tiles):
            M_[a].append(jnp.where(ln + home * 128 == rows + (r0 + 8 * a), 1.0, 0.0))
        piv = [jnp.ones((8, 128), F32) for _ in range(tiles)]
        ahead = None
        for s in range(tiles):
            lane = r0 - home * 128 + s * s8
            C = []
            for k in range(s8):
                C.append([column_of(M_[a][home], lane + k) if a > s else None for a in range(tiles)])
                C[k][s] = column_of(M_[s][home], lane + k) if ahead is None else ahead[k]
            ahead = [column_of(M_[s + 1][home], lane + s8 + k) for k in range(s8)] if s + 1 < tiles else None
            for j in range(0, s8, 2):
                first, second = C[j], C[j + 1]
                p11 = lane_of(first[s], j)
                p12 = lane_of(first[s], j + 1)
                p22 = lane_of(second[s], j + 1)
                det = p11 * p22 - p12 * p12
                inv1 = reciprocal(p11)
                mult = p12 * inv1
                inv2 = p11 * reciprocal(det)
                w1 = [first[a] * inv1 if a >= s else None for a in range(tiles)]
                second = [second[a] - first[a] * mult if a >= s else None for a in range(tiles)]
                w2 = [second[a] * inv2 if a >= s else None for a in range(tiles)]
                if ahead is not None:
                    for k in range(s8):
                        b1, b2 = lane_of(first[s + 1], k), lane_of(second[s + 1], k)
                        ahead[k] = (ahead[k] - w1[s + 1] * b1) - w2[s + 1] * b2
                for k in range(j + 2, s8):
                    b1 = lane_of(first[s], k)
                    b2 = lane_of(second[s], k)
                    for a in range(s, tiles):
                        C[k][a] = (C[k][a] - w1[a] * b1) - w2[a] * b2
                w1[s] = jnp.where(rows > j, w1[s], 0.0)
                w2[s] = jnp.where(rows > j + 1, w2[s], 0.0)
                piv[s] = jnp.where(rows == j, p11, jnp.where(rows == j + 1, det * inv1, piv[s]))
                for l in range(nt + 1):
                    b1 = lane_of(M_[s][l], j)
                    b2 = lane_of(M_[s][l], j + 1) - b1 * mult
                    for a in range(s, tiles):
                        M_[a][l] = (M_[a][l] - w1[a] * b1) - w2[a] * b2
        full = []
        for a in range(tiles):
            root = lax.rsqrt(piv[a])
            out = [v * root for v in M_[a]]
            ident = out.pop()
            at = ln + home * 128
            out[home] = jnp.where((at >= r0) & (at < r0 + b), ident, out[home])
            full.append(jnp.concatenate(out, axis=1))
        U = jnp.concatenate(full, axis=0)
        done.append(U)
        if p + 1 < n // b:
            r1 = r0 + b
            cut = r1 // 128 * 128
            upd = dot(U[:, cut:], U, 0, 0, HI)
            for q in range(p + 1, n // b):
                old = jnp.where((lanes >= r0) & (lanes < r1), 0.0, panels[q])
                panels[q] = old - upd[q * b - cut:(q + 1) * b - cut, :]
            if p in beside:
                beside[p]()
    W = jnp.concatenate(done, axis=0)
    li = lax.broadcasted_iota(jnp.int32, (n, n), 1)
    si = lax.broadcasted_iota(jnp.int32, (n, n), 0)
    return jnp.where(li <= si, W, 0.0)


class Place:
    def __init__(self, ssem, rsem):
        self.ssem, self.rsem = ssem, rsem
        self.sends = []
        self.f = lax.axis_index("fsdp")
        self.t = lax.axis_index("tp")
        self.core = lax.rem(self.f, 2)
        self.other = 1 - self.core
        self.x = lax.rem(self.f // 2, NX)
        self.y = self.f // (2 * NX)
        self.xs = [lax.rem(self.x + j, NX) for j in range(NX)]
        self.ys = [lax.rem(self.y + j, NY) for j in range(NY)]
        self.zs = [lax.rem(self.t + j, NZ) for j in range(NZ)]
        self.sibling = self.dev(self.x, self.y, self.other)
        self.zdev = [(self.f, z) for z in self.zs]
        self.all = [lax.rem(self.f + j, NF) for j in range(NF)]
        self.fdev = [(g, self.t) for g in self.all]
        self.plane = [
            self.dev(self.xs[i], self.ys[j], self.core) for i in range(NX) for j in range(NY) if (i, j) != (0, 0)
        ]
        self.chips = [self.ys[j] * NX + self.xs[i] for i in range(NX) for j in range(NY) if (i, j) != (0, 0)]
        self.chip = self.y * NX + self.x
        self.ways = (
            (self.xs, self.dev(self.xs[1], self.y, self.core), self.dev(self.xs[3], self.y, self.core)),
            (self.ys, self.dev(self.x, self.ys[1], self.core), self.dev(self.x, self.ys[3], self.core)),
        )

    def dev(self, px, py, pc):
        return ((py * NX + px) * 2 + pc, self.t)

    def y_x(self, i, j):
        return self.ys[j] * NX + self.xs[i]

    def greet(self, devices):
        barrier = pltpu.get_barrier_semaphore()
        for device in devices:
            pl.semaphore_signal(barrier, inc=1, device_id=device, device_id_type=MESH)
        return lambda: pl.semaphore_wait(barrier, len(devices))

    def exchange(self, src, dst, device):
        k = len(self.sends)
        cp = pltpu.make_async_remote_copy(
            src_ref=src, dst_ref=dst, send_sem=self.ssem.at[k], recv_sem=self.rsem.at[k],
            device_id=device, device_id_type=MESH,
        )
        cp.start()
        self.sends.append(cp)
        return cp

    def share(self, ref, device):
        return self.exchange(ref, ref, device)

    def finish(self):
        for cp in self.sends:
            cp.wait_send()


def piece(z, size):
    return pl.ds(pl.multiple_of(z * size, size), size)


def step_kernel(g_hbm, m_hbm, b_hbm, result, both, inverse, gbuf, mbuf, bbuf, bht, part, rz, left, gpart, rg, own, r2, gram,
                out, rs, r, rc, r16, f1, sab, s16, f2, sq, qc, qp, qz, load, store, gsem, hsem, zsem, ssem, rsem):
    at = Place(ssem, rsem)
    core, other, x, y, xs, ys = at.core, at.other, at.x, at.y, at.xs, at.ys
    nc = COLS // STEP
    loads = []
    for c in range(nc):
        cols = pl.ds(c * STEP, STEP)
        three = [
            pltpu.make_async_copy(b_hbm.at[cols, :], bbuf.at[cols, :], load.at[3 * c]),
            pltpu.make_async_copy(g_hbm.at[:, cols], gbuf.at[:, cols], load.at[3 * c + 1]),
            pltpu.make_async_copy(m_hbm.at[:, cols], mbuf.at[:, cols], load.at[3 * c + 2]),
        ]
        for cp in three:
            cp.start()
        loads.append(three)
    ready = at.greet(at.zdev[1:] + at.fdev[1:])
    total = None
    for c in range(nc):
        for cp in loads[c]:
            cp.wait()
        cols = pl.ds(c * STEP, STEP)
        half = (mbuf[:, cols].astype(F32) + gbuf[:, cols].astype(F32)).astype(BF16)
        gbuf[:, cols] = half
        term = dot(half, bbuf[cols, :], 1, 0)
        total = term if c == 0 else total + term
    part[...] = (total * (1.0 / math.sqrt(N))).astype(BF16)
    ready()
    zr = ROWS // NZ
    cps = [at.exchange(part.at[piece(at.zs[j], zr), :], rz.at[j - 1], at.zdev[j]) for j in range(1, NZ)]
    for c in range(nc):
        cols = pl.ds(c * STEP, STEP)
        bht[cols, :] = gbuf[:, cols].T
    mine = part[piece(at.t, zr), :].astype(F32)
    for j in range(1, NZ):
        cps[j - 1].wait_recv()
        mine = mine + rz[j - 1].astype(F32)
    mine = mine.astype(BF16)
    left[piece(at.t, zr), :] = mine
    az = [at.share(left.at[piece(at.t, zr), :], at.zdev[j]) for j in range(1, NZ)]

    full = dot(mine, mine, 0, 0)
    gpart[:, 0:8, :] = full[:128, :128].reshape(16, 8, 128)
    gpart[:, 8:16, :] = full[:128, 128:].reshape(16, 8, 128)
    gpart[:, 16:24, :] = full[128:, 128:].reshape(16, 8, 128)
    owner = lax.rem(x + y, 2) == core
    chips = [(i, j) for i in range(NX) for j in range(NY)]

    def to_owner(k, slot):
        i, j = chips[k]
        device = at.dev(xs[i], ys[j], lax.rem(xs[i] + ys[j], 2))
        return pltpu.make_async_remote_copy(
            src_ref=gpart.at[at.y_x(i, j)], dst_ref=rg.at[slot], send_sem=gsem.at[k], recv_sem=gsem.at[16 + slot],
            device_id=device if k else at.sibling, device_id_type=MESH,
        )

    scattered = [to_owner(k, 2 * k - 1 + core if k else 0) for k in range(16)]

    @pl.when(jnp.logical_not(owner))
    def _():
        scattered[0].start()

    for k in range(1, 16):
        scattered[k].start()

    def to_all(k, c):
        i, j = chips[k]
        return pltpu.make_async_remote_copy(
            src_ref=gram.at[at.chip], dst_ref=gram.at[at.chip], send_sem=hsem.at[2 * k + c], recv_sem=hsem.at[32 + k],
            device_id=at.dev(xs[i], ys[j], c) if k else at.sibling, device_id_type=MESH,
        )

    gathered = [to_all(0, 0)] + [to_all(k, c) for k in range(1, 16) for c in range(2)]
    across = [
        pltpu.make_async_remote_copy(
            src_ref=own, dst_ref=r2.at[j - 1], send_sem=zsem.at[j], recv_sem=zsem.at[8 + j],
            device_id=at.zdev[j], device_id_type=MESH,
        )
        for j in range(1, NZ)
    ]

    @pl.when(owner)
    def _():
        acc = gpart[at.chip]
        for slot in range(31):
            to_owner(0, slot).wait_recv()
            acc = acc + rg[slot]
        own[...] = acc
        for cp in across:
            cp.start()

    for cp in az:
        cp.wait_recv()
    wide = COLS // 2
    nk = wide // CHUNK
    qk = NX // nk

    def product(k, pc, into):
        half = bht[pl.ds(pl.multiple_of(pc * wide + k * CHUNK, 128), CHUNK), :]
        val = dot(half, left[...], 1, 0)
        for h in range(2):
            into[h, k * qk:(k + 1) * qk] = val[:, 128 * h:128 * h + 128].reshape(qk, NY, BLOCK, 128).astype(into.dtype)

    cc = []
    for k in range(nk):
        product(k, other, rs)
        qs = pl.ds(k * qk, qk)
        cc.append([at.exchange(rs.at[h, qs], rc.at[h, qs], at.sibling) for h in range(2)])

    @pl.when(owner)
    def _():
        acc = own[...]
        for j in range(1, NZ):
            across[j - 1].wait_recv()
            acc = acc + r2[j - 1]
        gram[at.chip] = acc
        for cp in gathered:
            cp.start()

    for k in range(nk):
        product(k, core, r)
    for k in range(nk):
        qs = pl.ds(k * qk, qk)
        for h in range(2):
            cc[k][h].wait_recv()
            total = r[h, qs] + rc[h, qs].astype(F32)
            r[h, qs] = total
            r16[h, qs] = total.astype(BF16)
    one = [[], []]
    for j in range(1, NX):
        one[0].append(at.exchange(r16.at[0, xs[j]], f1.at[0, j - 1], at.dev(xs[j], y, core)))
        one[1].append(at.exchange(r16.at[1, :, ys[j]], f1.at[1, j - 1], at.dev(x, ys[j], core)))
    for k in range(1, 16):
        to_all(k, 0).wait_recv()

    @pl.when(jnp.logical_not(owner))
    def _():
        to_all(0, 0).wait_recv()

    upper = jnp.concatenate([gram[:, 0:8, :].reshape(128, 128), gram[:, 8:16, :].reshape(128, 128)], axis=1)
    corner = gram[:, 16:24, :].reshape(128, 128)
    full = jnp.concatenate([upper, jnp.concatenate([jnp.zeros_like(corner), corner], axis=1)], axis=0)
    two = [[], []]

    def second_stage():
        for h in range(2):
            total = r[0, x] if h == 0 else r[1, :, y]
            for j in range(1, NX):
                one[h][j - 1].wait_recv()
                total = total + f1[h, j - 1].astype(F32)
            sab[h] = total
            s16[h] = total.astype(BF16)
            for j in range(1, NX):
                if h == 0:
                    two[h].append(at.exchange(s16.at[h, ys[j]], f2.at[h, j - 1], at.dev(x, ys[j], core)))
                else:
                    two[h].append(at.exchange(s16.at[h, xs[j]], f2.at[h, j - 1], at.dev(xs[j], y, core)))

    w = lower_inverse(full, {2: second_stage})
    ortho = dot(left[...].astype(F32), w, 1, 1, HI)
    both[0:ROWS, :] = ortho.astype(BF16)
    halves = []
    for h in range(2):
        total = sab[h, y if h == 0 else x]
        for j in range(1, NX):
            two[h][j - 1].wait_recv()
            total = total + f2[h, j - 1].astype(F32)
        halves.append(total)
    right = dot(jnp.concatenate(halves, axis=1), w, 1, 1, HI)
    rounded = right.astype(BF16)
    for h in range(2):
        out[h, core, x, y] = rounded[:, 128 * h:128 * h + 128]
    g2 = []
    for j in range(1, NX):
        g2.append(at.share(out.at[0, core, x, y], at.dev(x, ys[j], core)))
        g2.append(at.share(out.at[1, core, x, y], at.dev(xs[j], y, core)))
    total = jnp.sum(right * right, axis=0, keepdims=True)
    srow = lax.broadcasted_iota(jnp.int32, (8, 128), 0)
    sq[...] = jnp.where(srow == 0, total[:, :128], total[:, 128:])
    sc = at.exchange(sq, qc, at.sibling)
    sc.wait_recv()
    qp[at.chip] = sq[...] + qc[...]
    sp = [at.share(qp.at[at.chip], device) for device in at.plane]
    for cp in g2:
        cp.wait_recv()

    def band(h, q, k=None, ref=out, pc=core):
        if k is None:
            return ref.at[0, pc, q] if h == 0 else ref.at[1, pc, :, q]
        return ref.at[0, pc, q, pl.ds(2 * k, 2)] if h == 0 else ref.at[1, pc, pl.ds(2 * k, 2), q]

    last, spans, stores = [], [], []

    def keep(h, q, k, pc):
        cp = pltpu.make_async_copy(band(h, q, k, out, pc), band(h, q, k, result, pc), store.at[len(stores)])
        cp.start()
        stores.append(cp)

    def forward(h, q, k=None):
        last.append(at.share(band(h, q, k), at.sibling))
        spans.append((h, q, k))
        keep(h, q, k, core)

    begun = []
    for h in range(2):
        pos, nxt, prv = at.ways[h]
        begun.append([at.share(band(h, pos[0], 0), nxt), at.share(band(h, pos[0], 1), prv)])
    for h in range(2):
        pos, nxt, prv = at.ways[h]
        begun[h] += [at.share(band(h, pos[0], 1), nxt), at.share(band(h, pos[0], 0), prv)]
    for h in range(2):
        forward(h, at.ways[h][0][0])
    for cp in sp:
        cp.wait_recv()
    total = qp[0]
    for j in range(1, NX * NY):
        total = total + qp[j]
    qz[at.t] = total
    sz = [at.share(qz.at[at.t], at.zdev[j]) for j in range(1, NZ)]
    relays = []
    for h in range(2):
        pos, nxt, prv = at.ways[h]
        begun[h][0].wait_recv()
        relays.append(at.share(band(h, pos[3], 0), nxt))
        begun[h][1].wait_recv()
        relays.append(at.share(band(h, pos[1], 1), prv))
    for cp in sz:
        cp.wait_recv()
    total = qz[0]
    for j in range(1, NZ):
        total = total + qz[j]
    scale = jnp.sqrt(jnp.concatenate([total[0:1, :], total[1:2, :]], axis=1) / N + 1e-06)
    inverse[...] = jnp.broadcast_to(1.0 / scale, (8, RANK))
    both[ROWS:, :] = (ortho * (math.sqrt(M / RANK) / scale)).astype(BF16)
    for h in range(2):
        pos = at.ways[h][0]
        begun[h][2].wait_recv()
        forward(h, pos[3])
        begun[h][3].wait_recv()
        forward(h, pos[1])
    for h in range(2):
        pos = at.ways[h][0]
        for k in range(2):
            relays[2 * h + k].wait_recv()
            forward(h, pos[2], k)
    for cp, (h, q, k) in zip(last, spans):
        cp.wait_recv()
        keep(h, q, k, other)
    at.finish()
    for k in range(1, 16):
        scattered[k].wait_send()

    @pl.when(jnp.logical_not(owner))
    def _():
        scattered[0].wait_send()

    @pl.when(owner)
    def _():
        for cp in across + gathered:
            cp.wait_send()

    for cp in stores:
        cp.wait()


def output_kernel(g_hbm, m_hbm, both_hbm, right_hbm, inv_hbm, update, new_momentum, new_basis,
                  gbuf, mbuf, both, rbuf, inv, ubuf, nbuf, bbuf, load, store):
    nc = COLS // STEP
    first = [
        pltpu.make_async_copy(both_hbm, both, load.at[4 * nc]),
        pltpu.make_async_copy(inv_hbm, inv, load.at[4 * nc + 1]),
    ]
    loads = []
    for c in range(nc):
        cols = pl.ds(c * STEP, STEP)
        loads.append([
            pltpu.make_async_copy(right_hbm.at[0, cols, :], rbuf.at[0, cols, :], load.at[4 * c]),
            pltpu.make_async_copy(right_hbm.at[1, cols, :], rbuf.at[1, cols, :], load.at[4 * c + 1]),
            pltpu.make_async_copy(g_hbm.at[:, cols], gbuf.at[:, cols], load.at[4 * c + 2]),
            pltpu.make_async_copy(m_hbm.at[:, cols], mbuf.at[:, cols], load.at[4 * c + 3]),
        ])
    for cp in first:
        cp.start()
    for group in loads:
        for cp in group:
            cp.start()
    for cp in first:
        cp.wait()
    stores = []
    for c in range(nc):
        cols = pl.ds(c * STEP, STEP)
        for cp in loads[c]:
            cp.wait()
        rr = jnp.concatenate([rbuf[0, cols, :], rbuf[1, cols, :]], axis=1)
        bbuf[cols, :] = (rr.astype(F32) * inv[0:1, :]).astype(BF16)
        product = dot(both[...], rr, 1, 1)
        ubuf[:, cols] = product[ROWS:].astype(BF16)
        buffer = mbuf[:, cols].astype(F32) + gbuf[:, cols].astype(F32)
        nbuf[:, cols] = (buffer - (1.0 - MU / 100.0) * product[:ROWS]).astype(BF16)
        three = [
            pltpu.make_async_copy(bbuf.at[cols, :], new_basis.at[cols, :], store.at[3 * c]),
            pltpu.make_async_copy(ubuf.at[:, cols], update.at[:, cols], store.at[3 * c + 1]),
            pltpu.make_async_copy(nbuf.at[:, cols], new_momentum.at[:, cols], store.at[3 * c + 2]),
        ]
        for cp in three:
            cp.start()
        stores += three
    for cp in stores:
        cp.wait()


def body(grad, momentum, basis):
    dma = pltpu.SemaphoreType.DMA
    zr = ROWS // NZ
    sends = 7 + 7 + 4 + 6 + 6 + 6 + 1 + 15 + 8 + 2 + 7 + 4 + 8
    right, both, inverse = pl.pallas_call(
        step_kernel,
        out_shape=(
            jax.ShapeDtypeStruct((2, 2, NX, NY, BLOCK, 128), BF16),
            jax.ShapeDtypeStruct((2 * ROWS, RANK), BF16),
            jax.ShapeDtypeStruct((8, RANK), F32),
        ),
        in_specs=[pl.BlockSpec(memory_space=pl.ANY)] * 3,
        out_specs=tuple(pl.BlockSpec(memory_space=v) for v in (pl.ANY, pltpu.VMEM, pltpu.VMEM)),
        scratch_shapes=[
            pltpu.VMEM((ROWS, COLS), BF16), pltpu.VMEM((ROWS, COLS), BF16), pltpu.VMEM((COLS, RANK), BF16),
            pltpu.VMEM((COLS, RANK), BF16),
            pltpu.VMEM((ROWS, RANK), BF16), pltpu.VMEM((NZ - 1, zr, RANK), BF16), pltpu.VMEM((ROWS, RANK), BF16),
            pltpu.VMEM((16, 24, 128), F32), pltpu.VMEM((31, 24, 128), F32),
            pltpu.VMEM((24, 128), F32), pltpu.VMEM((NZ - 1, 24, 128), F32), pltpu.VMEM((16, 24, 128), F32),
            pltpu.VMEM((2, 2, NX, NY, BLOCK, 128), BF16), pltpu.VMEM((2, NX, NY, BLOCK, 128), BF16),
            pltpu.VMEM((2, NX, NY, BLOCK, 128), F32), pltpu.VMEM((2, NX, NY, BLOCK, 128), BF16),
            pltpu.VMEM((2, NX, NY, BLOCK, 128), BF16), pltpu.VMEM((2, 3, 4, BLOCK, 128), BF16),
            pltpu.VMEM((2, 4, BLOCK, 128), F32), pltpu.VMEM((2, 4, BLOCK, 128), BF16), pltpu.VMEM((2, 3, BLOCK, 128), BF16),
            pltpu.VMEM((8, 128), F32), pltpu.VMEM((8, 128), F32),
            pltpu.VMEM((NX * NY, 8, 128), F32), pltpu.VMEM((NZ, 8, 128), F32),
            dma((3 * (COLS // STEP),)), dma((20,)), dma((47,)), dma((48,)), dma((16,)), dma((sends,)), dma((sends,)),
        ],
        compiler_params=pltpu.CompilerParams(collective_id=0, has_side_effects=True, vmem_limit_bytes=VMEM_LIMIT),
        name="step_kernel",
    )(grad, momentum, basis)
    nc = COLS // STEP
    wide = pltpu.VMEM((ROWS, COLS), BF16)
    return pl.pallas_call(
        output_kernel,
        out_shape=(
            jax.ShapeDtypeStruct((ROWS, COLS), BF16),
            jax.ShapeDtypeStruct((ROWS, COLS), BF16),
            jax.ShapeDtypeStruct((COLS, RANK), BF16),
        ),
        in_specs=[pl.BlockSpec(memory_space=pl.ANY)] * 5,
        out_specs=tuple(pl.BlockSpec(memory_space=pl.ANY) for _ in range(3)),
        scratch_shapes=[
            wide, wide, pltpu.VMEM((2 * ROWS, RANK), BF16), pltpu.VMEM((2, COLS, 128), BF16), pltpu.VMEM((8, RANK), F32),
            wide, wide, pltpu.VMEM((COLS, RANK), BF16),
            dma((4 * nc + 2,)), dma((3 * nc,)),
        ],
        compiler_params=pltpu.CompilerParams(vmem_limit_bytes=VMEM_LIMIT),
        name="output_kernel",
    )(grad, momentum, both, right.reshape(2, COLS, 128), inverse)


def solution(mesh):
    placed = (P("fsdp", "tp"), P("fsdp", "tp"), P("tp", None))
    return jax.shard_map(
        body,
        mesh=mesh,
        in_specs=placed,
        out_specs=(P("fsdp", "tp"), P("fsdp", "tp"), P("tp", None)),
        check_vma=False,
    )
```

```python
import math

import jax
import jax.numpy as jnp
from jax import lax
from jax.experimental import pallas as pl
from jax.experimental.pallas import tpu as pltpu
from jax.sharding import PartitionSpec as P

M = 8192
N = 28672
RANK = 256
MU = 90

MESH = pl.DeviceIdType.MESH
HI = lax.Precision.HIGHEST
F32 = jnp.float32
BF16 = jnp.bfloat16
NX, NY, NZ = 4, 4, 8
NF = NX * NY * 2
ROWS = M // NF
COLS = N // NZ
CHUNK = 896
BLOCK = COLS // NF
STEP = 512
VMEM_LIMIT = 60 * 1024 * 1024


def dot(a, b, ca, cb, precision=None):
    return lax.dot_general(
        a, b, (((ca,), (cb,)), ((), ())), precision=precision, preferred_element_type=F32
    )


def lane_of(tile, j):
    return jnp.broadcast_to(tile[j:j + 1, :], tile.shape)


def column_of(tile, j):
    return jnp.broadcast_to(tile[:, j:j + 1], tile.shape)


def reciprocal(v):
    near = pl.reciprocal(v, approx=True)
    return near * (2.0 - v * near)


def lower_inverse(gram, beside, b=64, s8=8):
    n = gram.shape[0]
    tiles = b // 8
    nt = n // 128
    rows = lax.broadcasted_iota(jnp.int32, (8, 128), 0)
    ln = lax.broadcasted_iota(jnp.int32, (8, 128), 1)
    lanes = lax.broadcasted_iota(jnp.int32, (b, n), 1)
    panels = [gram[p * b:(p + 1) * b, :] for p in range(n // b)]
    done = []
    for p in range(n // b):
        r0 = p * b
        home = r0 // 128
        P_ = panels[p]
        M_ = [[P_[8 * a:8 * a + 8, 128 * l:128 * l + 128] for l in range(nt)] for a in range(tiles)]
        for a in range(tiles):
            M_[a].append(jnp.where(ln + home * 128 == rows + (r0 + 8 * a), 1.0, 0.0))
        piv = [jnp.ones((8, 128), F32) for _ in range(tiles)]
        ahead = None
        for s in range(tiles):
            lane = r0 - home * 128 + s * s8
            C = []
            for k in range(s8):
                C.append([column_of(M_[a][home], lane + k) if a > s else None for a in range(tiles)])
                C[k][s] = column_of(M_[s][home], lane + k) if ahead is None else ahead[k]
            ahead = [column_of(M_[s + 1][home], lane + s8 + k) for k in range(s8)] if s + 1 < tiles else None
            for j in range(0, s8, 2):
                first, second = C[j], C[j + 1]
                p11 = lane_of(first[s], j)
                p12 = lane_of(first[s], j + 1)
                p22 = lane_of(second[s], j + 1)
                det = p11 * p22 - p12 * p12
                inv1 = reciprocal(p11)
                mult = p12 * inv1
                inv2 = p11 * reciprocal(det)
                w1 = [first[a] * inv1 if a >= s else None for a in range(tiles)]
                second = [second[a] - first[a] * mult if a >= s else None for a in range(tiles)]
                w2 = [second[a] * inv2 if a >= s else None for a in range(tiles)]
                if ahead is not None:
                    for k in range(s8):
                        b1, b2 = lane_of(first[s + 1], k), lane_of(second[s + 1], k)
                        ahead[k] = (ahead[k] - w1[s + 1] * b1) - w2[s + 1] * b2
                for k in range(j + 2, s8):
                    b1 = lane_of(first[s], k)
                    b2 = lane_of(second[s], k)
                    for a in range(s, tiles):
                        C[k][a] = (C[k][a] - w1[a] * b1) - w2[a] * b2
                w1[s] = jnp.where(rows > j, w1[s], 0.0)
                w2[s] = jnp.where(rows > j + 1, w2[s], 0.0)
                piv[s] = jnp.where(rows == j, p11, jnp.where(rows == j + 1, det * inv1, piv[s]))
                for l in range(nt + 1):
                    b1 = lane_of(M_[s][l], j)
                    b2 = lane_of(M_[s][l], j + 1) - b1 * mult
                    for a in range(s, tiles):
                        M_[a][l] = (M_[a][l] - w1[a] * b1) - w2[a] * b2
        full = []
        for a in range(tiles):
            root = lax.rsqrt(piv[a])
            out = [v * root for v in M_[a]]
            ident = out.pop()
            at = ln + home * 128
            out[home] = jnp.where((at >= r0) & (at < r0 + b), ident, out[home])
            full.append(jnp.concatenate(out, axis=1))
        U = jnp.concatenate(full, axis=0)
        done.append(U)
        if p + 1 < n // b:
            r1 = r0 + b
            cut = r1 // 128 * 128
            upd = dot(U[:, cut:], U, 0, 0, HI)
            for q in range(p + 1, n // b):
                old = jnp.where((lanes >= r0) & (lanes < r1), 0.0, panels[q])
                panels[q] = old - upd[q * b - cut:(q + 1) * b - cut, :]
            if p in beside:
                beside[p]()
    W = jnp.concatenate(done, axis=0)
    li = lax.broadcasted_iota(jnp.int32, (n, n), 1)
    si = lax.broadcasted_iota(jnp.int32, (n, n), 0)
    return jnp.where(li <= si, W, 0.0)


class Place:
    def __init__(self, ssem, rsem):
        self.ssem, self.rsem = ssem, rsem
        self.sends = []
        self.f = lax.axis_index("fsdp")
        self.t = lax.axis_index("tp")
        self.core = lax.rem(self.f, 2)
        self.other = 1 - self.core
        self.x = lax.rem(self.f // 2, NX)
        self.y = self.f // (2 * NX)
        self.xs = [lax.rem(self.x + j, NX) for j in range(NX)]
        self.ys = [lax.rem(self.y + j, NY) for j in range(NY)]
        self.zs = [lax.rem(self.t + j, NZ) for j in range(NZ)]
        self.sibling = self.dev(self.x, self.y, self.other)
        self.zdev = [(self.f, z) for z in self.zs]
        self.all = [lax.rem(self.f + j, NF) for j in range(NF)]
        self.fdev = [(g, self.t) for g in self.all]
        self.plane = [
            self.dev(self.xs[i], self.ys[j], self.core) for i in range(NX) for j in range(NY) if (i, j) != (0, 0)
        ]
        self.chips = [self.ys[j] * NX + self.xs[i] for i in range(NX) for j in range(NY) if (i, j) != (0, 0)]
        self.chip = self.y * NX + self.x
        self.ways = (
            (self.xs, self.dev(self.xs[1], self.y, self.core), self.dev(self.xs[3], self.y, self.core)),
            (self.ys, self.dev(self.x, self.ys[1], self.core), self.dev(self.x, self.ys[3], self.core)),
        )

        self.twins = (
            (self.dev(self.xs[1], self.y, self.other), self.dev(self.xs[3], self.y, self.other)),
            (self.dev(self.x, self.ys[1], self.other), self.dev(self.x, self.ys[3], self.other)),
        )

    def dev(self, px, py, pc):
        return ((py * NX + px) * 2 + pc, self.t)

    def y_x(self, i, j):
        return self.ys[j] * NX + self.xs[i]

    def greet(self, devices):
        barrier = pltpu.get_barrier_semaphore()
        for device in devices:
            pl.semaphore_signal(barrier, inc=1, device_id=device, device_id_type=MESH)
        return lambda: pl.semaphore_wait(barrier, len(devices))

    def exchange(self, src, dst, device):
        k = len(self.sends)
        cp = pltpu.make_async_remote_copy(
            src_ref=src, dst_ref=dst, send_sem=self.ssem.at[k], recv_sem=self.rsem.at[k],
            device_id=device, device_id_type=MESH,
        )
        cp.start()
        self.sends.append(cp)
        return cp

    def share(self, ref, device):
        return self.exchange(ref, ref, device)

    def finish(self):
        for cp in self.sends:
            cp.wait_send()


def piece(z, size):
    return pl.ds(pl.multiple_of(z * size, size), size)


def step_kernel(g_hbm, m_hbm, b_hbm, result, both, inverse, gbuf, mbuf, bbuf, bht, part, rz, left, gpart, rg, own, r2, gram,
                out, rs, r, rc, r16, f1, joined, sab, s16, f2, sq, qc, qp, qz, load, store, gsem, hsem, zsem, ssem, rsem):
    at = Place(ssem, rsem)
    core, other, x, y, xs, ys = at.core, at.other, at.x, at.y, at.xs, at.ys
    nc = COLS // STEP
    loads = []
    for c in range(nc):
        cols = pl.ds(c * STEP, STEP)
        three = [
            pltpu.make_async_copy(b_hbm.at[cols, :], bbuf.at[cols, :], load.at[3 * c]),
            pltpu.make_async_copy(g_hbm.at[:, cols], gbuf.at[:, cols], load.at[3 * c + 1]),
            pltpu.make_async_copy(m_hbm.at[:, cols], mbuf.at[:, cols], load.at[3 * c + 2]),
        ]
        for cp in three:
            cp.start()
        loads.append(three)
    ready = at.greet(at.zdev[1:] + at.fdev[1:])
    total = None
    for c in range(nc):
        for cp in loads[c]:
            cp.wait()
        cols = pl.ds(c * STEP, STEP)
        half = (mbuf[:, cols].astype(F32) + gbuf[:, cols].astype(F32)).astype(BF16)
        gbuf[:, cols] = half
        term = dot(half, bbuf[cols, :], 1, 0)
        total = term if c == 0 else total + term
    part[...] = (total * (1.0 / math.sqrt(N))).astype(BF16)
    ready()
    zr = ROWS // NZ
    cps = [at.exchange(part.at[piece(at.zs[j], zr), :], rz.at[j - 1], at.zdev[j]) for j in range(1, NZ)]
    for c in range(nc):
        cols = pl.ds(c * STEP, STEP)
        bht[cols, :] = gbuf[:, cols].T
    mine = part[piece(at.t, zr), :].astype(F32)
    for j in range(1, NZ):
        cps[j - 1].wait_recv()
        mine = mine + rz[j - 1].astype(F32)
    mine = mine.astype(BF16)
    left[piece(at.t, zr), :] = mine
    az = [at.share(left.at[piece(at.t, zr), :], at.zdev[j]) for j in range(1, NZ)]

    full = dot(mine, mine, 0, 0)
    gpart[:, 0:8, :] = full[:128, :128].reshape(16, 8, 128)
    gpart[:, 8:16, :] = full[:128, 128:].reshape(16, 8, 128)
    gpart[:, 16:24, :] = full[128:, 128:].reshape(16, 8, 128)
    owner = lax.rem(x + y, 2) == core
    chips = [(i, j) for i in range(NX) for j in range(NY)]

    def to_owner(k, slot):
        i, j = chips[k]
        device = at.dev(xs[i], ys[j], lax.rem(xs[i] + ys[j], 2))
        return pltpu.make_async_remote_copy(
            src_ref=gpart.at[at.y_x(i, j)], dst_ref=rg.at[slot], send_sem=gsem.at[k], recv_sem=gsem.at[16 + slot],
            device_id=device if k else at.sibling, device_id_type=MESH,
        )

    scattered = [to_owner(k, 2 * k - 1 + core if k else 0) for k in range(16)]

    @pl.when(jnp.logical_not(owner))
    def _():
        scattered[0].start()

    for k in range(1, 16):
        scattered[k].start()

    def to_all(k, c):
        i, j = chips[k]
        return pltpu.make_async_remote_copy(
            src_ref=gram.at[at.chip], dst_ref=gram.at[at.chip], send_sem=hsem.at[2 * k + c], recv_sem=hsem.at[32 + k],
            device_id=at.dev(xs[i], ys[j], c) if k else at.sibling, device_id_type=MESH,
        )

    gathered = [to_all(0, 0)] + [to_all(k, c) for k in range(1, 16) for c in range(2)]
    across = [
        pltpu.make_async_remote_copy(
            src_ref=own, dst_ref=r2.at[j - 1], send_sem=zsem.at[j], recv_sem=zsem.at[8 + j],
            device_id=at.zdev[j], device_id_type=MESH,
        )
        for j in range(1, NZ)
    ]

    @pl.when(owner)
    def _():
        acc = gpart[at.chip]
        for slot in range(31):
            to_owner(0, slot).wait_recv()
            acc = acc + rg[slot]
        own[...] = acc
        for cp in across:
            cp.start()

    for cp in az:
        cp.wait_recv()
    wide = COLS // 2
    nk = wide // CHUNK
    qk = NX // nk

    def product(k, pc, into):
        half = bht[pl.ds(pl.multiple_of(pc * wide + k * CHUNK, 128), CHUNK), :]
        val = dot(half, left[...], 1, 0)
        for h in range(2):
            into[h, k * qk:(k + 1) * qk] = val[:, 128 * h:128 * h + 128].reshape(qk, NY, BLOCK, 128).astype(into.dtype)

    cc = []
    for k in range(nk):
        product(k, other, rs)
        qs = pl.ds(k * qk, qk)
        cc.append([at.exchange(rs.at[h, qs], rc.at[h, qs], at.sibling) for h in range(2)])

    @pl.when(owner)
    def _():
        acc = own[...]
        for j in range(1, NZ):
            across[j - 1].wait_recv()
            acc = acc + r2[j - 1]
        gram[at.chip] = acc
        for cp in gathered:
            cp.start()

    for k in range(nk):
        product(k, core, r)
    for k in range(nk):
        qs = pl.ds(k * qk, qk)
        for h in range(2):
            cc[k][h].wait_recv()
            total = r[h, qs] + rc[h, qs].astype(F32)
            r[h, qs] = total
            r16[h, qs] = total.astype(BF16)

    def half_of(ref, h, q, k):
        return ref.at[0, q, pl.ds(2 * k, 2)] if h == 0 else ref.at[1, pl.ds(2 * k, 2), q]

    one = []
    for h in range(2):
        pos, nxt, prv = at.ways[h]
        one.append([
            at.exchange(half_of(r16, h, pos[2], 0), f1.at[h, 0], nxt), at.exchange(half_of(r16, h, pos[2], 1), f1.at[h, 1], prv),
        ])
    for h in range(2):
        pos, nxt, prv = at.ways[h]
        one[h] += [
            at.exchange(half_of(r16, h, pos[1], 1), f1.at[h, 2], nxt), at.exchange(half_of(r16, h, pos[3], 0), f1.at[h, 3], prv),
        ]
    for h in range(2):
        pos, nxt, prv = at.ways[h]
        for k, (q, to) in enumerate(((pos[1], nxt), (pos[3], prv))):
            one[h][k].wait_recv()
            joined[h, k] = (half_of(r, h, q, k)[...] + f1[h, k].astype(F32)).astype(BF16)
            one[h].append(at.exchange(joined.at[h, k], f1.at[h, 4 + k], to))
    for k in range(1, 16):
        to_all(k, 0).wait_recv()

    @pl.when(jnp.logical_not(owner))
    def _():
        to_all(0, 0).wait_recv()

    upper = jnp.concatenate([gram[:, 0:8, :].reshape(128, 128), gram[:, 8:16, :].reshape(128, 128)], axis=1)
    corner = gram[:, 16:24, :].reshape(128, 128)
    full = jnp.concatenate([upper, jnp.concatenate([jnp.zeros_like(corner), corner], axis=1)], axis=0)
    two = [[], []]

    def second_stage():
        for h in range(2):
            for k in range(2, 6):
                one[h][k].wait_recv()
            for k in range(2):
                total = half_of(r, h, x if h == 0 else y, k)[...] + f1[h, 3 - k].astype(F32) + f1[h, 4 + k].astype(F32)
                sab[h, 2 * k:2 * k + 2] = total
                s16[h, 2 * k:2 * k + 2] = total.astype(BF16)
            for j in range(1, NX):
                if h == 0:
                    two[h].append(at.exchange(s16.at[h, ys[j]], f2.at[h, j - 1], at.dev(x, ys[j], core)))
                else:
                    two[h].append(at.exchange(s16.at[h, xs[j]], f2.at[h, j - 1], at.dev(xs[j], y, core)))

    w = lower_inverse(full, {2: second_stage})
    ortho = dot(left[...].astype(F32), w, 1, 1, HI)
    both[0:ROWS, :] = ortho.astype(BF16)
    halves = []
    for h in range(2):
        total = sab[h, y if h == 0 else x]
        for j in range(1, NX):
            two[h][j - 1].wait_recv()
            total = total + f2[h, j - 1].astype(F32)
        halves.append(total)
    right = dot(jnp.concatenate(halves, axis=1), w, 1, 1, HI)
    rounded = right.astype(BF16)
    for h in range(2):
        out[h, core, x, y] = rounded[:, 128 * h:128 * h + 128]
    g2 = []
    for j in range(1, NX):
        g2.append(at.share(out.at[0, core, x, y], at.dev(x, ys[j], core)))
        g2.append(at.share(out.at[1, core, x, y], at.dev(xs[j], y, core)))
    total = jnp.sum(right * right, axis=0, keepdims=True)
    srow = lax.broadcasted_iota(jnp.int32, (8, 128), 0)
    sq[...] = jnp.where(srow == 0, total[:, :128], total[:, 128:])
    sc = at.exchange(sq, qc, at.sibling)
    sc.wait_recv()
    qp[at.chip] = sq[...] + qc[...]
    sp = [at.share(qp.at[at.chip], device) for device in at.plane]
    for cp in g2:
        cp.wait_recv()

    def band(h, q, k=None, ref=out, pc=core):
        if k is None:
            return ref.at[0, pc, q] if h == 0 else ref.at[1, pc, :, q]
        return ref.at[0, pc, q, pl.ds(2 * k, 2)] if h == 0 else ref.at[1, pc, pl.ds(2 * k, 2), q]

    last, spans, stores = [], [], []

    def keep(h, q, k, pc):
        cp = pltpu.make_async_copy(band(h, q, k, out, pc), band(h, q, k, result, pc), store.at[len(stores)])
        cp.start()
        stores.append(cp)

    def forward(h, q, k=None):
        last.append(at.share(band(h, q, k), at.sibling))
        spans.append((h, q, k))
        keep(h, q, k, core)

    begun = []
    for h in range(2):
        pos, nxt, prv = at.ways[h]
        begun.append([at.share(band(h, pos[0], 0), nxt), at.share(band(h, pos[0], 1), prv)])
    for h in range(2):
        pos, nxt, prv = at.ways[h]
        begun[h] += [at.share(band(h, pos[0], 1), nxt), at.share(band(h, pos[0], 0), prv)]
    for h in range(2):
        forward(h, at.ways[h][0][0])
    for cp in sp:
        cp.wait_recv()
    total = qp[0]
    for j in range(1, NX * NY):
        total = total + qp[j]
    qz[at.t] = total
    sz = [at.share(qz.at[at.t], at.zdev[j]) for j in range(1, NZ)]
    relays = []
    for h in range(2):
        pos, nxt, prv = at.ways[h]
        for k, (q, near, far) in enumerate(((pos[3], nxt, at.twins[h][0]), (pos[1], prv, at.twins[h][1]))):
            begun[h][k].wait_recv()
            relays.append((at.share(band(h, q, k), near), at.share(band(h, q, k), far)))
    for cp in sz:
        cp.wait_recv()
    total = qz[0]
    for j in range(1, NZ):
        total = total + qz[j]
    scale = jnp.sqrt(jnp.concatenate([total[0:1, :], total[1:2, :]], axis=1) / N + 1e-06)
    inverse[...] = jnp.broadcast_to(1.0 / scale, (8, RANK))
    both[ROWS:, :] = (ortho * (math.sqrt(M / RANK) / scale)).astype(BF16)
    for h in range(2):
        pos = at.ways[h][0]
        begun[h][2].wait_recv()
        forward(h, pos[3])
        begun[h][3].wait_recv()
        forward(h, pos[1])
    for cp, (h, q, k) in zip(last, spans):
        cp.wait_recv()
        keep(h, q, k, other)
    for h in range(2):
        pos = at.ways[h][0]
        for k in range(2):
            near, far = relays[2 * h + k]
            near.wait_recv()
            keep(h, pos[2], k, core)
            far.wait_recv()
            keep(h, pos[2], k, other)
    at.finish()
    for k in range(1, 16):
        scattered[k].wait_send()

    @pl.when(jnp.logical_not(owner))
    def _():
        scattered[0].wait_send()

    @pl.when(owner)
    def _():
        for cp in across + gathered:
            cp.wait_send()

    for cp in stores:
        cp.wait()


def output_kernel(g_hbm, m_hbm, both_hbm, right_hbm, inv_hbm, update, new_momentum, new_basis,
                  gbuf, mbuf, both, rbuf, inv, ubuf, nbuf, bbuf, load, store):
    nc = COLS // STEP
    first = [
        pltpu.make_async_copy(both_hbm, both, load.at[4 * nc]),
        pltpu.make_async_copy(inv_hbm, inv, load.at[4 * nc + 1]),
    ]
    loads = []
    for c in range(nc):
        cols = pl.ds(c * STEP, STEP)
        loads.append([
            pltpu.make_async_copy(right_hbm.at[0, cols, :], rbuf.at[0, cols, :], load.at[4 * c]),
            pltpu.make_async_copy(right_hbm.at[1, cols, :], rbuf.at[1, cols, :], load.at[4 * c + 1]),
            pltpu.make_async_copy(g_hbm.at[:, cols], gbuf.at[:, cols], load.at[4 * c + 2]),
            pltpu.make_async_copy(m_hbm.at[:, cols], mbuf.at[:, cols], load.at[4 * c + 3]),
        ])
    for cp in first:
        cp.start()
    for group in loads:
        for cp in group:
            cp.start()
    for cp in first:
        cp.wait()
    stores = []
    for c in range(nc):
        cols = pl.ds(c * STEP, STEP)
        for cp in loads[c]:
            cp.wait()
        rr = jnp.concatenate([rbuf[0, cols, :], rbuf[1, cols, :]], axis=1)
        bbuf[cols, :] = (rr.astype(F32) * inv[0:1, :]).astype(BF16)
        product = dot(both[...], rr, 1, 1)
        ubuf[:, cols] = product[ROWS:].astype(BF16)
        buffer = mbuf[:, cols].astype(F32) + gbuf[:, cols].astype(F32)
        nbuf[:, cols] = (buffer - (1.0 - MU / 100.0) * product[:ROWS]).astype(BF16)
        three = [
            pltpu.make_async_copy(bbuf.at[cols, :], new_basis.at[cols, :], store.at[3 * c]),
            pltpu.make_async_copy(ubuf.at[:, cols], update.at[:, cols], store.at[3 * c + 1]),
            pltpu.make_async_copy(nbuf.at[:, cols], new_momentum.at[:, cols], store.at[3 * c + 2]),
        ]
        for cp in three:
            cp.start()
        stores += three
    for cp in stores:
        cp.wait()


def body(grad, momentum, basis):
    dma = pltpu.SemaphoreType.DMA
    zr = ROWS // NZ
    sends = 7 + 7 + 4 + 12 + 6 + 6 + 1 + 15 + 8 + 6 + 7 + 8
    right, both, inverse = pl.pallas_call(
        step_kernel,
        out_shape=(
            jax.ShapeDtypeStruct((2, 2, NX, NY, BLOCK, 128), BF16),
            jax.ShapeDtypeStruct((2 * ROWS, RANK), BF16),
            jax.ShapeDtypeStruct((8, RANK), F32),
        ),
        in_specs=[pl.BlockSpec(memory_space=pl.ANY)] * 3,
        out_specs=tuple(pl.BlockSpec(memory_space=v) for v in (pl.ANY, pltpu.VMEM, pltpu.VMEM)),
        scratch_shapes=[
            pltpu.VMEM((ROWS, COLS), BF16), pltpu.VMEM((ROWS, COLS), BF16), pltpu.VMEM((COLS, RANK), BF16),
            pltpu.VMEM((COLS, RANK), BF16),
            pltpu.VMEM((ROWS, RANK), BF16), pltpu.VMEM((NZ - 1, zr, RANK), BF16), pltpu.VMEM((ROWS, RANK), BF16),
            pltpu.VMEM((16, 24, 128), F32), pltpu.VMEM((31, 24, 128), F32),
            pltpu.VMEM((24, 128), F32), pltpu.VMEM((NZ - 1, 24, 128), F32), pltpu.VMEM((16, 24, 128), F32),
            pltpu.VMEM((2, 2, NX, NY, BLOCK, 128), BF16), pltpu.VMEM((2, NX, NY, BLOCK, 128), BF16),
            pltpu.VMEM((2, NX, NY, BLOCK, 128), F32), pltpu.VMEM((2, NX, NY, BLOCK, 128), BF16),
            pltpu.VMEM((2, NX, NY, BLOCK, 128), BF16), pltpu.VMEM((2, 6, 2, BLOCK, 128), BF16), pltpu.VMEM((2, 2, 2, BLOCK, 128), BF16),
            pltpu.VMEM((2, 4, BLOCK, 128), F32), pltpu.VMEM((2, 4, BLOCK, 128), BF16), pltpu.VMEM((2, 3, BLOCK, 128), BF16),
            pltpu.VMEM((8, 128), F32), pltpu.VMEM((8, 128), F32),
            pltpu.VMEM((NX * NY, 8, 128), F32), pltpu.VMEM((NZ, 8, 128), F32),
            dma((3 * (COLS // STEP),)), dma((20,)), dma((47,)), dma((48,)), dma((16,)), dma((sends,)), dma((sends,)),
        ],
        compiler_params=pltpu.CompilerParams(collective_id=0, has_side_effects=True, vmem_limit_bytes=VMEM_LIMIT),
        name="step_kernel",
    )(grad, momentum, basis)
    nc = COLS // STEP
    wide = pltpu.VMEM((ROWS, COLS), BF16)
    return pl.pallas_call(
        output_kernel,
        out_shape=(
            jax.ShapeDtypeStruct((ROWS, COLS), BF16),
            jax.ShapeDtypeStruct((ROWS, COLS), BF16),
            jax.ShapeDtypeStruct((COLS, RANK), BF16),
        ),
        in_specs=[pl.BlockSpec(memory_space=pl.ANY)] * 5,
        out_specs=tuple(pl.BlockSpec(memory_space=pl.ANY) for _ in range(3)),
        scratch_shapes=[
            wide, wide, pltpu.VMEM((2 * ROWS, RANK), BF16), pltpu.VMEM((2, COLS, 128), BF16), pltpu.VMEM((8, RANK), F32),
            wide, wide, pltpu.VMEM((COLS, RANK), BF16),
            dma((4 * nc + 2,)), dma((3 * nc,)),
        ],
        compiler_params=pltpu.CompilerParams(vmem_limit_bytes=VMEM_LIMIT),
        name="output_kernel",
    )(grad, momentum, both, right.reshape(2, COLS, 128), inverse)


def solution(mesh):
    placed = (P("fsdp", "tp"), P("fsdp", "tp"), P("tp", None))
    return jax.shard_map(
        body,
        mesh=mesh,
        in_specs=placed,
        out_specs=(P("fsdp", "tp"), P("fsdp", "tp"), P("tp", None)),
        check_vma=False,
    )
```

```python
import math

import jax
import jax.numpy as jnp
from jax import lax
from jax.experimental import pallas as pl
from jax.experimental.pallas import tpu as pltpu
from jax.sharding import PartitionSpec as P

M = 8192
N = 28672
RANK = 256
MU = 90

MESH = pl.DeviceIdType.MESH
HI = lax.Precision.HIGHEST
F32 = jnp.float32
BF16 = jnp.bfloat16
NX, NY, NZ = 4, 4, 8
NF = NX * NY * 2
ROWS = M // NF
COLS = N // NZ
CHUNK = 896
BLOCK = COLS // NF
STEP = 512
VMEM_LIMIT = 60 * 1024 * 1024


def dot(a, b, ca, cb, precision=None):
    return lax.dot_general(
        a, b, (((ca,), (cb,)), ((), ())), precision=precision, preferred_element_type=F32
    )


def lane_of(tile, j):
    return jnp.broadcast_to(tile[j:j + 1, :], tile.shape)


def column_of(tile, j):
    return jnp.broadcast_to(tile[:, j:j + 1], tile.shape)


def reciprocal(v):
    near = pl.reciprocal(v, approx=True)
    return near * (2.0 - v * near)


def lower_inverse(gram, beside, b=64, s8=8):
    n = gram.shape[0]
    tiles = b // 8
    nt = n // 128
    rows = lax.broadcasted_iota(jnp.int32, (8, 128), 0)
    ln = lax.broadcasted_iota(jnp.int32, (8, 128), 1)
    lanes = lax.broadcasted_iota(jnp.int32, (b, n), 1)
    panels = [gram[p * b:(p + 1) * b, :] for p in range(n // b)]
    done = []
    for p in range(n // b):
        r0 = p * b
        home = r0 // 128
        P_ = panels[p]
        M_ = [[P_[8 * a:8 * a + 8, 128 * l:128 * l + 128] for l in range(nt)] for a in range(tiles)]
        for a in range(tiles):
            M_[a].append(jnp.where(ln + home * 128 == rows + (r0 + 8 * a), 1.0, 0.0))
        piv = [jnp.ones((8, 128), F32) for _ in range(tiles)]
        ahead = None
        for s in range(tiles):
            lane = r0 - home * 128 + s * s8
            C = []
            for k in range(s8):
                C.append([column_of(M_[a][home], lane + k) if a > s else None for a in range(tiles)])
                C[k][s] = column_of(M_[s][home], lane + k) if ahead is None else ahead[k]
            ahead = [column_of(M_[s + 1][home], lane + s8 + k) for k in range(s8)] if s + 1 < tiles else None
            for j in range(0, s8, 2):
                first, second = C[j], C[j + 1]
                p11 = lane_of(first[s], j)
                p12 = lane_of(first[s], j + 1)
                p22 = lane_of(second[s], j + 1)
                det = p11 * p22 - p12 * p12
                inv1 = reciprocal(p11)
                mult = p12 * inv1
                inv2 = p11 * reciprocal(det)
                w1 = [first[a] * inv1 if a >= s else None for a in range(tiles)]
                second = [second[a] - first[a] * mult if a >= s else None for a in range(tiles)]
                w2 = [second[a] * inv2 if a >= s else None for a in range(tiles)]
                if ahead is not None:
                    for k in range(s8):
                        b1, b2 = lane_of(first[s + 1], k), lane_of(second[s + 1], k)
                        ahead[k] = (ahead[k] - w1[s + 1] * b1) - w2[s + 1] * b2
                for k in range(j + 2, s8):
                    b1 = lane_of(first[s], k)
                    b2 = lane_of(second[s], k)
                    for a in range(s, tiles):
                        C[k][a] = (C[k][a] - w1[a] * b1) - w2[a] * b2
                w1[s] = jnp.where(rows > j, w1[s], 0.0)
                w2[s] = jnp.where(rows > j + 1, w2[s], 0.0)
                piv[s] = jnp.where(rows == j, p11, jnp.where(rows == j + 1, det * inv1, piv[s]))
                for l in range(nt + 1):
                    b1 = lane_of(M_[s][l], j)
                    b2 = lane_of(M_[s][l], j + 1) - b1 * mult
                    for a in range(s, tiles):
                        M_[a][l] = (M_[a][l] - w1[a] * b1) - w2[a] * b2
        full = []
        for a in range(tiles):
            root = lax.rsqrt(piv[a])
            out = [v * root for v in M_[a]]
            ident = out.pop()
            at = ln + home * 128
            out[home] = jnp.where((at >= r0) & (at < r0 + b), ident, out[home])
            full.append(jnp.concatenate(out, axis=1))
        U = jnp.concatenate(full, axis=0)
        done.append(U)
        if p + 1 < n // b:
            r1 = r0 + b
            cut = r1 // 128 * 128
            upd = dot(U[:, cut:], U, 0, 0, HI)
            for q in range(p + 1, n // b):
                old = jnp.where((lanes >= r0) & (lanes < r1), 0.0, panels[q])
                panels[q] = old - upd[q * b - cut:(q + 1) * b - cut, :]
            if p in beside:
                beside[p]()
    W = jnp.concatenate(done, axis=0)
    li = lax.broadcasted_iota(jnp.int32, (n, n), 1)
    si = lax.broadcasted_iota(jnp.int32, (n, n), 0)
    return jnp.where(li <= si, W, 0.0)


class Place:
    def __init__(self, ssem, rsem):
        self.ssem, self.rsem = ssem, rsem
        self.sends = []
        self.f = lax.axis_index("fsdp")
        self.t = lax.axis_index("tp")
        self.core = lax.rem(self.f, 2)
        self.other = 1 - self.core
        self.x = lax.rem(self.f // 2, NX)
        self.y = self.f // (2 * NX)
        self.xs = [lax.rem(self.x + j, NX) for j in range(NX)]
        self.ys = [lax.rem(self.y + j, NY) for j in range(NY)]
        self.zs = [lax.rem(self.t + j, NZ) for j in range(NZ)]
        self.sibling = self.dev(self.x, self.y, self.other)
        self.zdev = [(self.f, z) for z in self.zs]
        self.all = [lax.rem(self.f + j, NF) for j in range(NF)]
        self.fdev = [(g, self.t) for g in self.all]
        self.plane = [
            self.dev(self.xs[i], self.ys[j], self.core) for i in range(NX) for j in range(NY) if (i, j) != (0, 0)
        ]
        self.chips = [self.ys[j] * NX + self.xs[i] for i in range(NX) for j in range(NY) if (i, j) != (0, 0)]
        self.chip = self.y * NX + self.x
        self.ways = (
            (self.xs, self.dev(self.xs[1], self.y, self.core), self.dev(self.xs[3], self.y, self.core)),
            (self.ys, self.dev(self.x, self.ys[1], self.core), self.dev(self.x, self.ys[3], self.core)),
        )

        self.twins = (
            (self.dev(self.xs[1], self.y, self.other), self.dev(self.xs[3], self.y, self.other)),
            (self.dev(self.x, self.ys[1], self.other), self.dev(self.x, self.ys[3], self.other)),
        )

    def dev(self, px, py, pc):
        return ((py * NX + px) * 2 + pc, self.t)

    def y_x(self, i, j):
        return self.ys[j] * NX + self.xs[i]

    def greet(self, devices):
        barrier = pltpu.get_barrier_semaphore()
        for device in devices:
            pl.semaphore_signal(barrier, inc=1, device_id=device, device_id_type=MESH)
        return lambda: pl.semaphore_wait(barrier, len(devices))

    def exchange(self, src, dst, device):
        k = len(self.sends)
        cp = pltpu.make_async_remote_copy(
            src_ref=src, dst_ref=dst, send_sem=self.ssem.at[k], recv_sem=self.rsem.at[k],
            device_id=device, device_id_type=MESH,
        )
        cp.start()
        self.sends.append(cp)
        return cp

    def share(self, ref, device):
        return self.exchange(ref, ref, device)


def piece(z, size):
    return pl.ds(pl.multiple_of(z * size, size), size)


def step_kernel(g_hbm, m_hbm, b_hbm, result, both, inverse, gbuf, mbuf, bbuf, bht, part, rz, left, gpart, rg, own, r2, gram,
                out, rs, r, rc, r16, f1, joined, sab, s16, f2, sq, qc, qp, qz, load, store, gsem, hsem, zsem, ssem, rsem):
    at = Place(ssem, rsem)
    core, other, x, y, xs, ys = at.core, at.other, at.x, at.y, at.xs, at.ys
    nc = COLS // STEP
    loads = []
    for c in range(nc):
        cols = pl.ds(c * STEP, STEP)
        three = [
            pltpu.make_async_copy(b_hbm.at[cols, :], bbuf.at[cols, :], load.at[3 * c]),
            pltpu.make_async_copy(g_hbm.at[:, cols], gbuf.at[:, cols], load.at[3 * c + 1]),
            pltpu.make_async_copy(m_hbm.at[:, cols], mbuf.at[:, cols], load.at[3 * c + 2]),
        ]
        for cp in three:
            cp.start()
        loads.append(three)
    ready = at.greet(at.zdev[1:] + at.fdev[1:])
    total = None
    for c in range(nc):
        for cp in loads[c]:
            cp.wait()
        cols = pl.ds(c * STEP, STEP)
        half = (mbuf[:, cols].astype(F32) + gbuf[:, cols].astype(F32)).astype(BF16)
        gbuf[:, cols] = half
        term = dot(half, bbuf[cols, :], 1, 0)
        total = term if c == 0 else total + term
    part[...] = (total * (1.0 / math.sqrt(N))).astype(BF16)
    ready()
    zr = ROWS // NZ
    cps = [at.exchange(part.at[piece(at.zs[j], zr), :], rz.at[j - 1], at.zdev[j]) for j in range(1, NZ)]
    for c in range(nc):
        cols = pl.ds(c * STEP, STEP)
        bht[cols, :] = gbuf[:, cols].T
    mine = part[piece(at.t, zr), :].astype(F32)
    for j in range(1, NZ):
        cps[j - 1].wait_recv()
        mine = mine + rz[j - 1].astype(F32)
    mine = mine.astype(BF16)
    left[piece(at.t, zr), :] = mine
    az = [at.share(left.at[piece(at.t, zr), :], at.zdev[j]) for j in range(1, NZ)]

    full = dot(mine, mine, 0, 0)
    gpart[:, 0:8, :] = full[:128, :128].reshape(16, 8, 128)
    gpart[:, 8:16, :] = full[:128, 128:].reshape(16, 8, 128)
    gpart[:, 16:24, :] = full[128:, 128:].reshape(16, 8, 128)
    owner = lax.rem(x + y, 2) == core
    chips = [(i, j) for i in range(NX) for j in range(NY)]

    def to_owner(k, slot):
        i, j = chips[k]
        device = at.dev(xs[i], ys[j], lax.rem(xs[i] + ys[j], 2))
        return pltpu.make_async_remote_copy(
            src_ref=gpart.at[at.y_x(i, j)], dst_ref=rg.at[slot], send_sem=gsem.at[k], recv_sem=gsem.at[16 + slot],
            device_id=device if k else at.sibling, device_id_type=MESH,
        )

    scattered = [to_owner(k, 2 * k - 1 + core if k else 0) for k in range(16)]

    @pl.when(jnp.logical_not(owner))
    def _():
        scattered[0].start()

    for k in range(1, 16):
        scattered[k].start()

    def to_all(k, c):
        i, j = chips[k]
        return pltpu.make_async_remote_copy(
            src_ref=gram.at[at.chip], dst_ref=gram.at[at.chip], send_sem=hsem.at[2 * k + c], recv_sem=hsem.at[32 + k],
            device_id=at.dev(xs[i], ys[j], c) if k else at.sibling, device_id_type=MESH,
        )

    gathered = [to_all(0, 0)] + [to_all(k, c) for k in range(1, 16) for c in range(2)]
    across = [
        pltpu.make_async_remote_copy(
            src_ref=own, dst_ref=r2.at[j - 1], send_sem=zsem.at[j], recv_sem=zsem.at[8 + j],
            device_id=at.zdev[j], device_id_type=MESH,
        )
        for j in range(1, NZ)
    ]

    @pl.when(owner)
    def _():
        acc = gpart[at.chip]
        for slot in range(31):
            to_owner(0, slot).wait_recv()
            acc = acc + rg[slot]
        own[...] = acc
        for cp in across:
            cp.start()

    for cp in az:
        cp.wait_recv()
    wide = COLS // 2
    nk = wide // CHUNK
    qk = NX // nk

    def product(k, pc, into):
        half = bht[pl.ds(pl.multiple_of(pc * wide + k * CHUNK, 128), CHUNK), :]
        val = dot(half, left[...], 1, 0)
        for h in range(2):
            into[h, k * qk:(k + 1) * qk] = val[:, 128 * h:128 * h + 128].reshape(qk, NY, BLOCK, 128).astype(into.dtype)

    cc = []
    for k in range(nk):
        product(k, other, rs)
        qs = pl.ds(k * qk, qk)
        cc.append([at.exchange(rs.at[h, qs], rc.at[h, qs], at.sibling) for h in range(2)])

    @pl.when(owner)
    def _():
        acc = own[...]
        for j in range(1, NZ):
            across[j - 1].wait_recv()
            acc = acc + r2[j - 1]
        gram[at.chip] = acc
        for cp in gathered:
            cp.start()

    for k in range(nk):
        product(k, core, r)
    for k in range(nk):
        qs = pl.ds(k * qk, qk)
        for h in range(2):
            cc[k][h].wait_recv()
            total = r[h, qs] + rc[h, qs].astype(F32)
            r[h, qs] = total
            r16[h, qs] = total.astype(BF16)

    def half_of(ref, h, q, k):
        return ref.at[0, q, pl.ds(2 * k, 2)] if h == 0 else ref.at[1, pl.ds(2 * k, 2), q]

    one = []
    for h in range(2):
        pos, nxt, prv = at.ways[h]
        one.append([
            at.exchange(half_of(r16, h, pos[2], 0), f1.at[h, 0], nxt), at.exchange(half_of(r16, h, pos[2], 1), f1.at[h, 1], prv),
        ])
    for h in range(2):
        pos, nxt, prv = at.ways[h]
        one[h] += [
            at.exchange(half_of(r16, h, pos[1], 1), f1.at[h, 2], nxt), at.exchange(half_of(r16, h, pos[3], 0), f1.at[h, 3], prv),
        ]
    for h in range(2):
        pos, nxt, prv = at.ways[h]
        for k, (q, to) in enumerate(((pos[1], nxt), (pos[3], prv))):
            one[h][k].wait_recv()
            joined[h, k] = (half_of(r, h, q, k)[...] + f1[h, k].astype(F32)).astype(BF16)
            one[h].append(at.exchange(joined.at[h, k], f1.at[h, 4 + k], to))
    for k in range(1, 16):
        to_all(k, 0).wait_recv()

    @pl.when(jnp.logical_not(owner))
    def _():
        to_all(0, 0).wait_recv()

    upper = jnp.concatenate([gram[:, 0:8, :].reshape(128, 128), gram[:, 8:16, :].reshape(128, 128)], axis=1)
    corner = gram[:, 16:24, :].reshape(128, 128)
    full = jnp.concatenate([upper, jnp.concatenate([jnp.zeros_like(corner), corner], axis=1)], axis=0)
    two = [[], []]

    def second_stage():
        for h in range(2):
            for k in range(2, 6):
                one[h][k].wait_recv()
            for k in range(2):
                total = half_of(r, h, x if h == 0 else y, k)[...] + f1[h, 3 - k].astype(F32) + f1[h, 4 + k].astype(F32)
                sab[h, 2 * k:2 * k + 2] = total
                s16[h, 2 * k:2 * k + 2] = total.astype(BF16)
            for j in range(1, NX):
                if h == 0:
                    two[h].append(at.exchange(s16.at[h, ys[j]], f2.at[h, j - 1], at.dev(x, ys[j], core)))
                else:
                    two[h].append(at.exchange(s16.at[h, xs[j]], f2.at[h, j - 1], at.dev(xs[j], y, core)))

    w = lower_inverse(full, {2: second_stage})
    halves = []
    for h in range(2):
        total = sab[h, y if h == 0 else x]
        for j in range(1, NX):
            two[h][j - 1].wait_recv()
            total = total + f2[h, j - 1].astype(F32)
        halves.append(total)
    right = dot(jnp.concatenate(halves, axis=1), w, 1, 1, HI)
    rounded = right.astype(BF16)
    for h in range(2):
        out[h, core, x, y] = rounded[:, 128 * h:128 * h + 128]
    g2 = [[], []]
    for j in (2, 1, 3):
        g2[0].append(at.share(out.at[0, core, x, y], at.dev(x, ys[j], core)))
        g2[1].append(at.share(out.at[1, core, x, y], at.dev(xs[j], y, core)))
    total = jnp.sum(right * right, axis=0, keepdims=True)
    srow = lax.broadcasted_iota(jnp.int32, (8, 128), 0)
    sq[...] = jnp.where(srow == 0, total[:, :128], total[:, 128:])
    sc = at.exchange(sq, qc, at.sibling)
    ortho = dot(left[...].astype(F32), w, 1, 1, HI)
    both[0:ROWS, :] = ortho.astype(BF16)
    sc.wait_recv()
    qp[at.chip] = sq[...] + qc[...]
    sp = [at.share(qp.at[at.chip], device) for device in at.plane]
    def band(h, q, k=None, ref=out, pc=core):
        if k is None:
            return ref.at[0, pc, q] if h == 0 else ref.at[1, pc, :, q]
        return ref.at[0, pc, q, pl.ds(2 * k, 2)] if h == 0 else ref.at[1, pc, pl.ds(2 * k, 2), q]

    last, spans, stores = [], [], []

    def keep(h, q, k, pc):
        cp = pltpu.make_async_copy(band(h, q, k, out, pc), band(h, q, k, result, pc), store.at[len(stores)])
        cp.start()
        stores.append(cp)

    def forward(h, q, k=None):
        last.append(at.share(band(h, q, k), at.sibling))
        spans.append((h, q, k))
        keep(h, q, k, core)

    begun = []
    for h in range(2):
        for cp in g2[h]:
            cp.wait_recv()
        pos, nxt, prv = at.ways[h]
        begun.append([
            at.share(band(h, pos[0], 0), nxt), at.share(band(h, pos[0], 1), prv),
            at.share(band(h, pos[0], 1), nxt), at.share(band(h, pos[0], 0), prv),
        ])
    for h in range(2):
        forward(h, at.ways[h][0][0])
    old = len(at.sends) - 10
    for cp in sp:
        cp.wait_recv()
    total = qp[0]
    for j in range(1, NX * NY):
        total = total + qp[j]
    qz[at.t] = total
    sz = [at.share(qz.at[at.t], at.zdev[j]) for j in range(1, NZ)]
    relays = []
    for h in range(2):
        pos, nxt, prv = at.ways[h]
        for k, (q, near, far) in enumerate(((pos[3], nxt, at.twins[h][0]), (pos[1], prv, at.twins[h][1]))):
            begun[h][k].wait_recv()
            relays.append((at.share(band(h, q, k), near), at.share(band(h, q, k), far)))
    for h in range(2):
        pos = at.ways[h][0]
        begun[h][2].wait_recv()
        forward(h, pos[3])
        begun[h][3].wait_recv()
        forward(h, pos[1])
    for cp in at.sends[:old] + scattered[1:]:
        cp.wait_send()

    @pl.when(jnp.logical_not(owner))
    def _():
        scattered[0].wait_send()

    @pl.when(owner)
    def _():
        for cp in across + gathered:
            cp.wait_send()

    for cp in sz:
        cp.wait_recv()
    total = qz[0]
    for j in range(1, NZ):
        total = total + qz[j]
    scale = jnp.sqrt(jnp.concatenate([total[0:1, :], total[1:2, :]], axis=1) / N + 1e-06)
    inverse[...] = jnp.broadcast_to(1.0 / scale, (8, RANK))
    both[ROWS:, :] = (ortho * (math.sqrt(M / RANK) / scale)).astype(BF16)
    for cp, (h, q, k) in zip(last, spans):
        cp.wait_recv()
        keep(h, q, k, other)
    for h in range(2):
        pos = at.ways[h][0]
        for k in range(2):
            near, far = relays[2 * h + k]
            near.wait_recv()
            keep(h, pos[2], k, core)
            far.wait_recv()
            keep(h, pos[2], k, other)
    for cp in at.sends[old:]:
        cp.wait_send()
    for cp in stores:
        cp.wait()


def output_kernel(g_hbm, m_hbm, both_hbm, right_hbm, inv_hbm, update, new_momentum, new_basis,
                  gbuf, mbuf, both, rbuf, inv, ubuf, nbuf, bbuf, load, store):
    nc = COLS // STEP
    first = [
        pltpu.make_async_copy(both_hbm, both, load.at[4 * nc]),
        pltpu.make_async_copy(inv_hbm, inv, load.at[4 * nc + 1]),
    ]
    loads = []
    for c in range(nc):
        cols = pl.ds(c * STEP, STEP)
        loads.append([
            pltpu.make_async_copy(right_hbm.at[0, cols, :], rbuf.at[0, cols, :], load.at[4 * c]),
            pltpu.make_async_copy(right_hbm.at[1, cols, :], rbuf.at[1, cols, :], load.at[4 * c + 1]),
            pltpu.make_async_copy(g_hbm.at[:, cols], gbuf.at[:, cols], load.at[4 * c + 2]),
            pltpu.make_async_copy(m_hbm.at[:, cols], mbuf.at[:, cols], load.at[4 * c + 3]),
        ])
    for cp in first:
        cp.start()
    for group in loads:
        for cp in group:
            cp.start()
    for cp in first:
        cp.wait()
    stores = []
    for c in range(nc):
        cols = pl.ds(c * STEP, STEP)
        for cp in loads[c]:
            cp.wait()
        rr = jnp.concatenate([rbuf[0, cols, :], rbuf[1, cols, :]], axis=1)
        bbuf[cols, :] = (rr.astype(F32) * inv[0:1, :]).astype(BF16)
        product = dot(both[...], rr, 1, 1)
        ubuf[:, cols] = product[ROWS:].astype(BF16)
        buffer = mbuf[:, cols].astype(F32) + gbuf[:, cols].astype(F32)
        nbuf[:, cols] = (buffer - (1.0 - MU / 100.0) * product[:ROWS]).astype(BF16)
        three = [
            pltpu.make_async_copy(bbuf.at[cols, :], new_basis.at[cols, :], store.at[3 * c]),
            pltpu.make_async_copy(ubuf.at[:, cols], update.at[:, cols], store.at[3 * c + 1]),
            pltpu.make_async_copy(nbuf.at[:, cols], new_momentum.at[:, cols], store.at[3 * c + 2]),
        ]
        for cp in three:
            cp.start()
        stores += three
    for cp in stores:
        cp.wait()


def body(grad, momentum, basis):
    dma = pltpu.SemaphoreType.DMA
    zr = ROWS // NZ
    sends = 7 + 7 + 4 + 12 + 6 + 6 + 1 + 15 + 8 + 6 + 7 + 8
    right, both, inverse = pl.pallas_call(
        step_kernel,
        out_shape=(
            jax.ShapeDtypeStruct((2, 2, NX, NY, BLOCK, 128), BF16),
            jax.ShapeDtypeStruct((2 * ROWS, RANK), BF16),
            jax.ShapeDtypeStruct((8, RANK), F32),
        ),
        in_specs=[pl.BlockSpec(memory_space=pl.ANY)] * 3,
        out_specs=tuple(pl.BlockSpec(memory_space=v) for v in (pl.ANY, pltpu.VMEM, pltpu.VMEM)),
        scratch_shapes=[
            pltpu.VMEM((ROWS, COLS), BF16), pltpu.VMEM((ROWS, COLS), BF16), pltpu.VMEM((COLS, RANK), BF16),
            pltpu.VMEM((COLS, RANK), BF16),
            pltpu.VMEM((ROWS, RANK), BF16), pltpu.VMEM((NZ - 1, zr, RANK), BF16), pltpu.VMEM((ROWS, RANK), BF16),
            pltpu.VMEM((16, 24, 128), F32), pltpu.VMEM((31, 24, 128), F32),
            pltpu.VMEM((24, 128), F32), pltpu.VMEM((NZ - 1, 24, 128), F32), pltpu.VMEM((16, 24, 128), F32),
            pltpu.VMEM((2, 2, NX, NY, BLOCK, 128), BF16), pltpu.VMEM((2, NX, NY, BLOCK, 128), BF16),
            pltpu.VMEM((2, NX, NY, BLOCK, 128), F32), pltpu.VMEM((2, NX, NY, BLOCK, 128), BF16),
            pltpu.VMEM((2, NX, NY, BLOCK, 128), BF16), pltpu.VMEM((2, 6, 2, BLOCK, 128), BF16), pltpu.VMEM((2, 2, 2, BLOCK, 128), BF16),
            pltpu.VMEM((2, 4, BLOCK, 128), F32), pltpu.VMEM((2, 4, BLOCK, 128), BF16), pltpu.VMEM((2, 3, BLOCK, 128), BF16),
            pltpu.VMEM((8, 128), F32), pltpu.VMEM((8, 128), F32),
            pltpu.VMEM((NX * NY, 8, 128), F32), pltpu.VMEM((NZ, 8, 128), F32),
            dma((3 * (COLS // STEP),)), dma((20,)), dma((47,)), dma((48,)), dma((16,)), dma((sends,)), dma((sends,)),
        ],
        compiler_params=pltpu.CompilerParams(collective_id=0, has_side_effects=True, vmem_limit_bytes=VMEM_LIMIT),
        name="step_kernel",
    )(grad, momentum, basis)
    nc = COLS // STEP
    wide = pltpu.VMEM((ROWS, COLS), BF16)
    return pl.pallas_call(
        output_kernel,
        out_shape=(
            jax.ShapeDtypeStruct((ROWS, COLS), BF16),
            jax.ShapeDtypeStruct((ROWS, COLS), BF16),
            jax.ShapeDtypeStruct((COLS, RANK), BF16),
        ),
        in_specs=[pl.BlockSpec(memory_space=pl.ANY)] * 5,
        out_specs=tuple(pl.BlockSpec(memory_space=pl.ANY) for _ in range(3)),
        scratch_shapes=[
            wide, wide, pltpu.VMEM((2 * ROWS, RANK), BF16), pltpu.VMEM((2, COLS, 128), BF16), pltpu.VMEM((8, RANK), F32),
            wide, wide, pltpu.VMEM((COLS, RANK), BF16),
            dma((4 * nc + 2,)), dma((3 * nc,)),
        ],
        compiler_params=pltpu.CompilerParams(vmem_limit_bytes=VMEM_LIMIT),
        name="output_kernel",
    )(grad, momentum, both, right.reshape(2, COLS, 128), inverse)


def solution(mesh):
    placed = (P("fsdp", "tp"), P("fsdp", "tp"), P("tp", None))
    return jax.shard_map(
        body,
        mesh=mesh,
        in_specs=placed,
        out_specs=(P("fsdp", "tp"), P("fsdp", "tp"), P("tp", None)),
        check_vma=False,
    )
```

```python
import math

import jax
import jax.numpy as jnp
from jax import lax
from jax.experimental import pallas as pl
from jax.experimental.pallas import tpu as pltpu
from jax.sharding import PartitionSpec as P

M = 8192
N = 28672
RANK = 256
MU = 90

MESH = pl.DeviceIdType.MESH
HI = lax.Precision.HIGHEST
F32 = jnp.float32
BF16 = jnp.bfloat16
NX, NY, NZ = 4, 4, 8
NF = NX * NY * 2
ROWS = M // NF
COLS = N // NZ
CHUNK = 896
BLOCK = COLS // NF
STEP = 512
VMEM_LIMIT = 60 * 1024 * 1024


def dot(a, b, ca, cb, precision=None):
    return lax.dot_general(
        a, b, (((ca,), (cb,)), ((), ())), precision=precision, preferred_element_type=F32
    )


def lane_of(tile, j):
    return jnp.broadcast_to(tile[j:j + 1, :], tile.shape)


def column_of(tile, j):
    return jnp.broadcast_to(tile[:, j:j + 1], tile.shape)


def reciprocal(v):
    near = pl.reciprocal(v, approx=True)
    return near * (2.0 - v * near)


def parts(v):
    hi = v.astype(BF16)
    return hi, (v - hi.astype(F32)).astype(BF16)


def lower_inverse(gram, beside, b=64, s8=8):
    n = gram.shape[0]
    tiles = b // 8
    nt = n // 128
    rows = lax.broadcasted_iota(jnp.int32, (8, 128), 0)
    ln = lax.broadcasted_iota(jnp.int32, (8, 128), 1)
    lanes = lax.broadcasted_iota(jnp.int32, (b, n), 1)
    panels = [gram[p * b:(p + 1) * b, :] for p in range(n // b)]
    done = []
    for p in range(n // b):
        r0 = p * b
        home = r0 // 128
        P_ = panels[p]
        M_ = [[P_[8 * a:8 * a + 8, 128 * l:128 * l + 128] for l in range(nt)] for a in range(tiles)]
        for a in range(tiles):
            M_[a].append(jnp.where(ln + home * 128 == rows + (r0 + 8 * a), 1.0, 0.0))
        piv = [jnp.ones((8, 128), F32) for _ in range(tiles)]
        ahead = None
        for s in range(tiles):
            lane = r0 - home * 128 + s * s8
            C = []
            for k in range(s8):
                C.append([column_of(M_[a][home], lane + k) if a > s else None for a in range(tiles)])
                C[k][s] = column_of(M_[s][home], lane + k) if ahead is None else ahead[k]
            ahead = [column_of(M_[s + 1][home], lane + s8 + k) for k in range(s8)] if s + 1 < tiles else None
            for j in range(0, s8, 2):
                first, second = C[j], C[j + 1]
                p11 = lane_of(first[s], j)
                p12 = lane_of(first[s], j + 1)
                p22 = lane_of(second[s], j + 1)
                det = p11 * p22 - p12 * p12
                inv1 = reciprocal(p11)
                mult = p12 * inv1
                inv2 = p11 * reciprocal(det)
                w1 = [first[a] * inv1 if a >= s else None for a in range(tiles)]
                second = [second[a] - first[a] * mult if a >= s else None for a in range(tiles)]
                w2 = [second[a] * inv2 if a >= s else None for a in range(tiles)]
                if ahead is not None:
                    for k in range(s8):
                        b1, b2 = lane_of(first[s + 1], k), lane_of(second[s + 1], k)
                        ahead[k] = (ahead[k] - w1[s + 1] * b1) - w2[s + 1] * b2
                for k in range(j + 2, s8):
                    b1 = lane_of(first[s], k)
                    b2 = lane_of(second[s], k)
                    for a in range(s, tiles):
                        C[k][a] = (C[k][a] - w1[a] * b1) - w2[a] * b2
                w1[s] = jnp.where(rows > j, w1[s], 0.0)
                w2[s] = jnp.where(rows > j + 1, w2[s], 0.0)
                piv[s] = jnp.where(rows == j, p11, jnp.where(rows == j + 1, det * inv1, piv[s]))
                for l in range(nt + 1):
                    b1 = lane_of(M_[s][l], j)
                    b2 = lane_of(M_[s][l], j + 1) - b1 * mult
                    for a in range(s, tiles):
                        M_[a][l] = (M_[a][l] - w1[a] * b1) - w2[a] * b2
        full = []
        for a in range(tiles):
            root = lax.rsqrt(piv[a])
            out = [v * root for v in M_[a]]
            ident = out.pop()
            at = ln + home * 128
            out[home] = jnp.where((at >= r0) & (at < r0 + b), ident, out[home])
            full.append(jnp.concatenate(out, axis=1))
        U = jnp.concatenate(full, axis=0)
        done.append(U)
        if p + 1 < n // b:
            r1 = r0 + b
            cut = r1 // 128 * 128
            hi, lo = parts(U)
            lhs = jnp.concatenate([hi[:, cut:], hi[:, cut:], lo[:, cut:], lo[:, cut:]], axis=0).T
            rhs = jnp.concatenate([hi, lo, hi, lo], axis=0)
            for q in range(p + 1, n // b):
                old = jnp.where((lanes >= r0) & (lanes < r1), 0.0, panels[q])
                panels[q] = old - dot(lhs[q * b - cut:(q + 1) * b - cut, :], rhs, 1, 0)
            if p in beside:
                beside[p]()
    W = jnp.concatenate(done, axis=0)
    li = lax.broadcasted_iota(jnp.int32, (n, n), 1)
    si = lax.broadcasted_iota(jnp.int32, (n, n), 0)
    return jnp.where(li <= si, W, 0.0)


class Place:
    def __init__(self, ssem, rsem):
        self.ssem, self.rsem = ssem, rsem
        self.sends = []
        self.f = lax.axis_index("fsdp")
        self.t = lax.axis_index("tp")
        self.core = lax.rem(self.f, 2)
        self.other = 1 - self.core
        self.x = lax.rem(self.f // 2, NX)
        self.y = self.f // (2 * NX)
        self.xs = [lax.rem(self.x + j, NX) for j in range(NX)]
        self.ys = [lax.rem(self.y + j, NY) for j in range(NY)]
        self.zs = [lax.rem(self.t + j, NZ) for j in range(NZ)]
        self.sibling = self.dev(self.x, self.y, self.other)
        self.zdev = [(self.f, z) for z in self.zs]
        self.all = [lax.rem(self.f + j, NF) for j in range(NF)]
        self.fdev = [(g, self.t) for g in self.all]
        self.plane = [
            self.dev(self.xs[i], self.ys[j], self.core) for i in range(NX) for j in range(NY) if (i, j) != (0, 0)
        ]
        self.chips = [self.ys[j] * NX + self.xs[i] for i in range(NX) for j in range(NY) if (i, j) != (0, 0)]
        self.chip = self.y * NX + self.x
        self.ways = (
            (self.xs, self.dev(self.xs[1], self.y, self.core), self.dev(self.xs[3], self.y, self.core)),
            (self.ys, self.dev(self.x, self.ys[1], self.core), self.dev(self.x, self.ys[3], self.core)),
        )

        self.twins = (
            (self.dev(self.xs[1], self.y, self.other), self.dev(self.xs[3], self.y, self.other)),
            (self.dev(self.x, self.ys[1], self.other), self.dev(self.x, self.ys[3], self.other)),
        )

    def dev(self, px, py, pc):
        return ((py * NX + px) * 2 + pc, self.t)

    def y_x(self, i, j):
        return self.ys[j] * NX + self.xs[i]

    def greet(self, devices):
        barrier = pltpu.get_barrier_semaphore()
        for device in devices:
            pl.semaphore_signal(barrier, inc=1, device_id=device, device_id_type=MESH)
        return lambda: pl.semaphore_wait(barrier, len(devices))

    def exchange(self, src, dst, device):
        k = len(self.sends)
        cp = pltpu.make_async_remote_copy(
            src_ref=src, dst_ref=dst, send_sem=self.ssem.at[k], recv_sem=self.rsem.at[k],
            device_id=device, device_id_type=MESH,
        )
        cp.start()
        self.sends.append(cp)
        return cp

    def share(self, ref, device):
        return self.exchange(ref, ref, device)


def piece(z, size):
    return pl.ds(pl.multiple_of(z * size, size), size)


def step_kernel(g_hbm, m_hbm, b_hbm, result, both, inverse, gbuf, mbuf, bbuf, bht, part, rz, left, gpart, rg, own, r2, gram,
                out, rs, r, rc, r16, f1, joined, sab, s16, f2, sq, qc, qp, qz, load, store, gsem, hsem, zsem, ssem, rsem):
    at = Place(ssem, rsem)
    core, other, x, y, xs, ys = at.core, at.other, at.x, at.y, at.xs, at.ys
    nc = COLS // STEP
    loads = []
    for c in range(nc):
        cols = pl.ds(c * STEP, STEP)
        three = [
            pltpu.make_async_copy(b_hbm.at[cols, :], bbuf.at[cols, :], load.at[3 * c]),
            pltpu.make_async_copy(g_hbm.at[:, cols], gbuf.at[:, cols], load.at[3 * c + 1]),
            pltpu.make_async_copy(m_hbm.at[:, cols], mbuf.at[:, cols], load.at[3 * c + 2]),
        ]
        for cp in three:
            cp.start()
        loads.append(three)
    ready = at.greet(at.zdev[1:] + at.fdev[1:])
    total = None
    for c in range(nc):
        for cp in loads[c]:
            cp.wait()
        cols = pl.ds(c * STEP, STEP)
        half = (mbuf[:, cols].astype(F32) + gbuf[:, cols].astype(F32)).astype(BF16)
        gbuf[:, cols] = half
        term = dot(half, bbuf[cols, :], 1, 0)
        total = term if c == 0 else total + term
    part[...] = (total * (1.0 / math.sqrt(N))).astype(BF16)
    ready()
    zr = ROWS // NZ
    cps = [at.exchange(part.at[piece(at.zs[j], zr), :], rz.at[j - 1], at.zdev[j]) for j in range(1, NZ)]
    for c in range(nc):
        cols = pl.ds(c * STEP, STEP)
        bht[cols, :] = gbuf[:, cols].T
    mine = part[piece(at.t, zr), :].astype(F32)
    for j in range(1, NZ):
        cps[j - 1].wait_recv()
        mine = mine + rz[j - 1].astype(F32)
    mine = mine.astype(BF16)
    left[piece(at.t, zr), :] = mine
    az = [at.share(left.at[piece(at.t, zr), :], at.zdev[j]) for j in range(1, NZ)]

    full = dot(mine, mine, 0, 0)
    gpart[:, 0:8, :] = full[:128, :128].reshape(16, 8, 128)
    gpart[:, 8:16, :] = full[:128, 128:].reshape(16, 8, 128)
    gpart[:, 16:24, :] = full[128:, 128:].reshape(16, 8, 128)
    owner = lax.rem(x + y, 2) == core
    chips = [(i, j) for i in range(NX) for j in range(NY)]

    def to_owner(k, slot):
        i, j = chips[k]
        device = at.dev(xs[i], ys[j], lax.rem(xs[i] + ys[j], 2))
        return pltpu.make_async_remote_copy(
            src_ref=gpart.at[at.y_x(i, j)], dst_ref=rg.at[slot], send_sem=gsem.at[k], recv_sem=gsem.at[16 + slot],
            device_id=device if k else at.sibling, device_id_type=MESH,
        )

    scattered = [to_owner(k, 2 * k - 1 + core if k else 0) for k in range(16)]

    @pl.when(jnp.logical_not(owner))
    def _():
        scattered[0].start()

    for k in range(1, 16):
        scattered[k].start()

    def to_all(k, c):
        i, j = chips[k]
        return pltpu.make_async_remote_copy(
            src_ref=gram.at[at.chip], dst_ref=gram.at[at.chip], send_sem=hsem.at[2 * k + c], recv_sem=hsem.at[32 + k],
            device_id=at.dev(xs[i], ys[j], c) if k else at.sibling, device_id_type=MESH,
        )

    gathered = [to_all(0, 0)] + [to_all(k, c) for k in range(1, 16) for c in range(2)]
    across = [
        pltpu.make_async_remote_copy(
            src_ref=own, dst_ref=r2.at[j - 1], send_sem=zsem.at[j], recv_sem=zsem.at[8 + j],
            device_id=at.zdev[j], device_id_type=MESH,
        )
        for j in range(1, NZ)
    ]

    @pl.when(owner)
    def _():
        acc = gpart[at.chip]
        for slot in range(31):
            to_owner(0, slot).wait_recv()
            acc = acc + rg[slot]
        own[...] = acc
        for cp in across:
            cp.start()

    for cp in az:
        cp.wait_recv()
    wide = COLS // 2
    nk = wide // CHUNK
    qk = NX // nk

    def product(k, pc, into):
        half = bht[pl.ds(pl.multiple_of(pc * wide + k * CHUNK, 128), CHUNK), :]
        val = dot(half, left[...], 1, 0)
        for h in range(2):
            into[h, k * qk:(k + 1) * qk] = val[:, 128 * h:128 * h + 128].reshape(qk, NY, BLOCK, 128).astype(into.dtype)

    cc = []
    for k in range(nk):
        product(k, other, rs)
        qs = pl.ds(k * qk, qk)
        cc.append([at.exchange(rs.at[h, qs], rc.at[h, qs], at.sibling) for h in range(2)])

    @pl.when(owner)
    def _():
        acc = own[...]
        for j in range(1, NZ):
            across[j - 1].wait_recv()
            acc = acc + r2[j - 1]
        gram[at.chip] = acc
        for cp in gathered:
            cp.start()

    for k in range(nk):
        product(k, core, r)
    def half_of(ref, h, q, k):
        return ref.at[0, q, pl.ds(2 * k, 2)] if h == 0 else ref.at[1, pl.ds(2 * k, 2), q]

    one = []
    for h in range(2):
        for k in range(nk):
            qs = pl.ds(k * qk, qk)
            cc[k][h].wait_recv()
            total = r[h, qs] + rc[h, qs].astype(F32)
            r[h, qs] = total
            r16[h, qs] = total.astype(BF16)
        pos, nxt, prv = at.ways[h]
        one.append([
            at.exchange(half_of(r16, h, pos[2], 0), f1.at[h, 0], nxt), at.exchange(half_of(r16, h, pos[2], 1), f1.at[h, 1], prv),
        ])
    for h in range(2):
        pos, nxt, prv = at.ways[h]
        one[h] += [
            at.exchange(half_of(r16, h, pos[1], 1), f1.at[h, 2], nxt), at.exchange(half_of(r16, h, pos[3], 0), f1.at[h, 3], prv),
        ]
    for h in range(2):
        pos, nxt, prv = at.ways[h]
        for k, (q, to) in enumerate(((pos[1], nxt), (pos[3], prv))):
            one[h][k].wait_recv()
            joined[h, k] = (half_of(r, h, q, k)[...] + f1[h, k].astype(F32)).astype(BF16)
            one[h].append(at.exchange(joined.at[h, k], f1.at[h, 4 + k], to))
    for k in range(1, 16):
        to_all(k, 0).wait_recv()

    @pl.when(jnp.logical_not(owner))
    def _():
        to_all(0, 0).wait_recv()

    upper = jnp.concatenate([gram[:, 0:8, :].reshape(128, 128), gram[:, 8:16, :].reshape(128, 128)], axis=1)
    corner = gram[:, 16:24, :].reshape(128, 128)
    full = jnp.concatenate([upper, jnp.concatenate([jnp.zeros_like(corner), corner], axis=1)], axis=0)
    two = [[], []]

    def second_stage():
        for h in range(2):
            for k in range(2, 6):
                one[h][k].wait_recv()
            for k in range(2):
                total = half_of(r, h, x if h == 0 else y, k)[...] + f1[h, 3 - k].astype(F32) + f1[h, 4 + k].astype(F32)
                sab[h, 2 * k:2 * k + 2] = total
                s16[h, 2 * k:2 * k + 2] = total.astype(BF16)
            for j in range(1, NX):
                if h == 0:
                    two[h].append(at.exchange(s16.at[h, ys[j]], f2.at[h, j - 1], at.dev(x, ys[j], core)))
                else:
                    two[h].append(at.exchange(s16.at[h, xs[j]], f2.at[h, j - 1], at.dev(xs[j], y, core)))

    w = lower_inverse(full, {2: second_stage})
    whi, wlo = parts(w)
    halves = []
    for h in range(2):
        total = sab[h, y if h == 0 else x]
        for j in range(1, NX):
            two[h][j - 1].wait_recv()
            total = total + f2[h, j - 1].astype(F32)
        halves.append(total)
    hi, lo = parts(jnp.concatenate(halves, axis=1))
    right = dot(jnp.concatenate([hi, lo], axis=0), whi, 1, 1)
    right = right[:BLOCK] + right[BLOCK:] + dot(hi, wlo, 1, 1)
    rounded = right.astype(BF16)
    for h in range(2):
        out[h, core, x, y] = rounded[:, 128 * h:128 * h + 128]
    g2 = [[], []]
    for j in (2, 1, 3):
        g2[0].append(at.share(out.at[0, core, x, y], at.dev(x, ys[j], core)))
        g2[1].append(at.share(out.at[1, core, x, y], at.dev(xs[j], y, core)))
    total = jnp.sum(right * right, axis=0, keepdims=True)
    srow = lax.broadcasted_iota(jnp.int32, (8, 128), 0)
    sq[...] = jnp.where(srow == 0, total[:, :128], total[:, 128:])
    sc = at.exchange(sq, qc, at.sibling)
    ortho = dot(left[...], whi, 1, 1) + dot(left[...], wlo, 1, 1)
    both[0:ROWS, :] = ortho.astype(BF16)
    sc.wait_recv()
    qp[at.chip] = sq[...] + qc[...]
    sp = [at.share(qp.at[at.chip], device) for device in at.plane]
    def band(h, q, k=None, ref=out, pc=core):
        if k is None:
            return ref.at[0, pc, q] if h == 0 else ref.at[1, pc, :, q]
        return ref.at[0, pc, q, pl.ds(2 * k, 2)] if h == 0 else ref.at[1, pc, pl.ds(2 * k, 2), q]

    last, spans, stores = [], [], []

    def keep(h, q, k, pc):
        cp = pltpu.make_async_copy(band(h, q, k, out, pc), band(h, q, k, result, pc), store.at[len(stores)])
        cp.start()
        stores.append(cp)

    def forward(h, q, k=None):
        last.append(at.share(band(h, q, k), at.sibling))
        spans.append((h, q, k))
        keep(h, q, k, core)

    begun = []
    for h in range(2):
        for cp in g2[h]:
            cp.wait_recv()
        pos, nxt, prv = at.ways[h]
        begun.append([
            at.share(band(h, pos[0], 0), nxt), at.share(band(h, pos[0], 1), prv),
            at.share(band(h, pos[0], 1), nxt), at.share(band(h, pos[0], 0), prv),
        ])
    for h in range(2):
        forward(h, at.ways[h][0][0])
    old = len(at.sends) - 10
    for cp in sp:
        cp.wait_recv()
    total = qp[0]
    for j in range(1, NX * NY):
        total = total + qp[j]
    qz[at.t] = total
    sz = [at.share(qz.at[at.t], at.zdev[j]) for j in range(1, NZ)]
    relays = []
    for h in range(2):
        pos, nxt, prv = at.ways[h]
        for k, (q, near, far) in enumerate(((pos[3], nxt, at.twins[h][0]), (pos[1], prv, at.twins[h][1]))):
            begun[h][k].wait_recv()
            relays.append((at.share(band(h, q, k), near), at.share(band(h, q, k), far)))
    for h in range(2):
        pos = at.ways[h][0]
        begun[h][2].wait_recv()
        forward(h, pos[3])
        begun[h][3].wait_recv()
        forward(h, pos[1])
    for cp in at.sends[:old] + scattered[1:]:
        cp.wait_send()

    @pl.when(jnp.logical_not(owner))
    def _():
        scattered[0].wait_send()

    @pl.when(owner)
    def _():
        for cp in across + gathered:
            cp.wait_send()

    for cp in sz:
        cp.wait_recv()
    total = qz[0]
    for j in range(1, NZ):
        total = total + qz[j]
    scale = jnp.sqrt(jnp.concatenate([total[0:1, :], total[1:2, :]], axis=1) / N + 1e-06)
    inverse[...] = jnp.broadcast_to(1.0 / scale, (8, RANK))
    both[ROWS:, :] = (ortho * (math.sqrt(M / RANK) / scale)).astype(BF16)
    for cp, (h, q, k) in zip(last, spans):
        cp.wait_recv()
        keep(h, q, k, other)
    for h in range(2):
        pos = at.ways[h][0]
        for k in range(2):
            near, far = relays[2 * h + k]
            near.wait_recv()
            keep(h, pos[2], k, core)
            far.wait_recv()
            keep(h, pos[2], k, other)
    for cp in at.sends[old:]:
        cp.wait_send()
    for cp in stores:
        cp.wait()


def output_kernel(g_hbm, m_hbm, both_hbm, right_hbm, inv_hbm, update, new_momentum, new_basis,
                  gbuf, mbuf, both, rbuf, inv, ubuf, nbuf, bbuf, load, store):
    nc = COLS // STEP
    loads = []

    def fetch(c):
        cols = pl.ds(c * STEP, STEP)
        loads.append([
            pltpu.make_async_copy(right_hbm.at[:, cols, :], rbuf.at[:, cols, :], load.at[3 * c]),
            pltpu.make_async_copy(g_hbm.at[:, cols], gbuf.at[:, cols], load.at[3 * c + 1]),
            pltpu.make_async_copy(m_hbm.at[:, cols], mbuf.at[:, cols], load.at[3 * c + 2]),
        ])
        for cp in loads[c]:
            cp.start()

    first = [
        pltpu.make_async_copy(both_hbm, both, load.at[3 * nc]),
        pltpu.make_async_copy(inv_hbm, inv, load.at[3 * nc + 1]),
    ]
    for cp in first:
        cp.start()
    for c in range(3):
        fetch(c)
    for cp in first:
        cp.wait()
    stores = []
    for c in range(nc):
        cols = pl.ds(c * STEP, STEP)
        if c + 3 < nc:
            fetch(c + 3)
        for cp in loads[c]:
            cp.wait()
        rr = jnp.concatenate([rbuf[0, cols, :], rbuf[1, cols, :]], axis=1)
        bbuf[cols, :] = (rr.astype(F32) * inv[0:1, :]).astype(BF16)
        product = dot(both[...], rr, 1, 1)
        ubuf[:, cols] = product[ROWS:].astype(BF16)
        buffer = mbuf[:, cols].astype(F32) + gbuf[:, cols].astype(F32)
        nbuf[:, cols] = (buffer - (1.0 - MU / 100.0) * product[:ROWS]).astype(BF16)
        three = [
            pltpu.make_async_copy(bbuf.at[cols, :], new_basis.at[cols, :], store.at[3 * c]),
            pltpu.make_async_copy(ubuf.at[:, cols], update.at[:, cols], store.at[3 * c + 1]),
            pltpu.make_async_copy(nbuf.at[:, cols], new_momentum.at[:, cols], store.at[3 * c + 2]),
        ]
        for cp in three:
            cp.start()
        stores += three
    for cp in stores:
        cp.wait()


def body(grad, momentum, basis):
    dma = pltpu.SemaphoreType.DMA
    zr = ROWS // NZ
    sends = 7 + 7 + 4 + 12 + 6 + 6 + 1 + 15 + 8 + 6 + 7 + 8
    right, both, inverse = pl.pallas_call(
        step_kernel,
        out_shape=(
            jax.ShapeDtypeStruct((2, 2, NX, NY, BLOCK, 128), BF16),
            jax.ShapeDtypeStruct((2 * ROWS, RANK), BF16),
            jax.ShapeDtypeStruct((8, RANK), F32),
        ),
        in_specs=[pl.BlockSpec(memory_space=pl.ANY)] * 3,
        out_specs=tuple(pl.BlockSpec(memory_space=v) for v in (pl.ANY, pltpu.VMEM, pltpu.VMEM)),
        scratch_shapes=[
            pltpu.VMEM((ROWS, COLS), BF16), pltpu.VMEM((ROWS, COLS), BF16), pltpu.VMEM((COLS, RANK), BF16),
            pltpu.VMEM((COLS, RANK), BF16),
            pltpu.VMEM((ROWS, RANK), BF16), pltpu.VMEM((NZ - 1, zr, RANK), BF16), pltpu.VMEM((ROWS, RANK), BF16),
            pltpu.VMEM((16, 24, 128), F32), pltpu.VMEM((31, 24, 128), F32),
            pltpu.VMEM((24, 128), F32), pltpu.VMEM((NZ - 1, 24, 128), F32), pltpu.VMEM((16, 24, 128), F32),
            pltpu.VMEM((2, 2, NX, NY, BLOCK, 128), BF16), pltpu.VMEM((2, NX, NY, BLOCK, 128), BF16),
            pltpu.VMEM((2, NX, NY, BLOCK, 128), F32), pltpu.VMEM((2, NX, NY, BLOCK, 128), BF16),
            pltpu.VMEM((2, NX, NY, BLOCK, 128), BF16), pltpu.VMEM((2, 6, 2, BLOCK, 128), BF16), pltpu.VMEM((2, 2, 2, BLOCK, 128), BF16),
            pltpu.VMEM((2, 4, BLOCK, 128), F32), pltpu.VMEM((2, 4, BLOCK, 128), BF16), pltpu.VMEM((2, 3, BLOCK, 128), BF16),
            pltpu.VMEM((8, 128), F32), pltpu.VMEM((8, 128), F32),
            pltpu.VMEM((NX * NY, 8, 128), F32), pltpu.VMEM((NZ, 8, 128), F32),
            dma((3 * (COLS // STEP),)), dma((20,)), dma((47,)), dma((48,)), dma((16,)), dma((sends,)), dma((sends,)),
        ],
        compiler_params=pltpu.CompilerParams(collective_id=0, has_side_effects=True, vmem_limit_bytes=VMEM_LIMIT),
        name="step_kernel",
    )(grad, momentum, basis)
    nc = COLS // STEP
    wide = pltpu.VMEM((ROWS, COLS), BF16)
    return pl.pallas_call(
        output_kernel,
        out_shape=(
            jax.ShapeDtypeStruct((ROWS, COLS), BF16),
            jax.ShapeDtypeStruct((ROWS, COLS), BF16),
            jax.ShapeDtypeStruct((COLS, RANK), BF16),
        ),
        in_specs=[pl.BlockSpec(memory_space=pl.ANY)] * 5,
        out_specs=tuple(pl.BlockSpec(memory_space=pl.ANY) for _ in range(3)),
        scratch_shapes=[
            wide, wide, pltpu.VMEM((2 * ROWS, RANK), BF16), pltpu.VMEM((2, COLS, 128), BF16), pltpu.VMEM((8, RANK), F32),
            wide, wide, pltpu.VMEM((COLS, RANK), BF16),
            dma((3 * nc + 2,)), dma((3 * nc,)),
        ],
        compiler_params=pltpu.CompilerParams(vmem_limit_bytes=VMEM_LIMIT),
        name="output_kernel",
    )(grad, momentum, both, right.reshape(2, COLS, 128), inverse)


def solution(mesh):
    placed = (P("fsdp", "tp"), P("fsdp", "tp"), P("tp", None))
    return jax.shard_map(
        body,
        mesh=mesh,
        in_specs=placed,
        out_specs=(P("fsdp", "tp"), P("fsdp", "tp"), P("tp", None)),
        check_vma=False,
    )
```

```python
import math

import jax
import jax.numpy as jnp
from jax import lax
from jax.experimental import pallas as pl
from jax.experimental.pallas import tpu as pltpu
from jax.sharding import PartitionSpec as P

M = 8192
N = 28672
RANK = 256
MU = 90

MESH = pl.DeviceIdType.MESH
HI = lax.Precision.HIGHEST
F32 = jnp.float32
BF16 = jnp.bfloat16
NX, NY, NZ = 4, 4, 8
NF = NX * NY * 2
ROWS = M // NF
COLS = N // NZ
CHUNK = 896
BLOCK = COLS // NF
STEP = 512
VMEM_LIMIT = 60 * 1024 * 1024


def dot(a, b, ca, cb, precision=None):
    return lax.dot_general(
        a, b, (((ca,), (cb,)), ((), ())), precision=precision, preferred_element_type=F32
    )


def lane_of(tile, j):
    return jnp.broadcast_to(tile[j:j + 1, :], tile.shape)


def column_of(tile, j):
    return jnp.broadcast_to(tile[:, j:j + 1], tile.shape)


def reciprocal(v):
    near = pl.reciprocal(v, approx=True)
    return near * (2.0 - v * near)


def parts(v):
    hi = v.astype(BF16)
    return hi, (v - hi.astype(F32)).astype(BF16)


def lower_inverse(gram, beside, b=64, s8=8):
    n = gram.shape[0]
    tiles = b // 8
    nt = n // 128
    rows = lax.broadcasted_iota(jnp.int32, (8, 128), 0)
    ln = lax.broadcasted_iota(jnp.int32, (8, 128), 1)
    lanes = lax.broadcasted_iota(jnp.int32, (b, n), 1)
    panels = [gram[p * b:(p + 1) * b, :] for p in range(n // b)]
    done = []
    for p in range(n // b):
        r0 = p * b
        home = r0 // 128
        P_ = panels[p]
        M_ = [[P_[8 * a:8 * a + 8, 128 * l:128 * l + 128] for l in range(nt)] for a in range(tiles)]
        for a in range(tiles):
            M_[a].append(jnp.where(ln + home * 128 == rows + (r0 + 8 * a), 1.0, 0.0))
        piv = [jnp.ones((8, 128), F32) for _ in range(tiles)]
        ahead = None
        for s in range(tiles):
            lane = r0 - home * 128 + s * s8
            C = []
            for k in range(s8):
                C.append([column_of(M_[a][home], lane + k) if a > s else None for a in range(tiles)])
                C[k][s] = column_of(M_[s][home], lane + k) if ahead is None else ahead[k]
            ahead = [column_of(M_[s + 1][home], lane + s8 + k) for k in range(s8)] if s + 1 < tiles else None
            for j in range(0, s8, 2):
                first, second = C[j], C[j + 1]
                p11 = lane_of(first[s], j)
                p12 = lane_of(first[s], j + 1)
                p22 = lane_of(second[s], j + 1)
                det = p11 * p22 - p12 * p12
                inv1 = reciprocal(p11)
                mult = p12 * inv1
                inv2 = p11 * reciprocal(det)
                w1 = [first[a] * inv1 if a >= s else None for a in range(tiles)]
                second = [second[a] - first[a] * mult if a >= s else None for a in range(tiles)]
                w2 = [second[a] * inv2 if a >= s else None for a in range(tiles)]
                if ahead is not None:
                    for k in range(s8):
                        b1, b2 = lane_of(first[s + 1], k), lane_of(second[s + 1], k)
                        ahead[k] = (ahead[k] - w1[s + 1] * b1) - w2[s + 1] * b2
                for k in range(j + 2, s8):
                    b1 = lane_of(first[s], k)
                    b2 = lane_of(second[s], k)
                    for a in range(s, tiles):
                        C[k][a] = (C[k][a] - w1[a] * b1) - w2[a] * b2
                w1[s] = jnp.where(rows > j, w1[s], 0.0)
                w2[s] = jnp.where(rows > j + 1, w2[s], 0.0)
                piv[s] = jnp.where(rows == j, p11, jnp.where(rows == j + 1, det * inv1, piv[s]))
                for l in range(nt + 1):
                    b1 = lane_of(M_[s][l], j)
                    b2 = lane_of(M_[s][l], j + 1) - b1 * mult
                    for a in range(s, tiles):
                        M_[a][l] = (M_[a][l] - w1[a] * b1) - w2[a] * b2
        full = []
        for a in range(tiles):
            root = lax.rsqrt(piv[a])
            out = [v * root for v in M_[a]]
            ident = out.pop()
            at = ln + home * 128
            out[home] = jnp.where((at >= r0) & (at < r0 + b), ident, out[home])
            full.append(jnp.concatenate(out, axis=1))
        U = jnp.concatenate(full, axis=0)
        done.append(U)
        if p + 1 < n // b:
            r1 = r0 + b
            cut = r1 // 128 * 128
            hi, lo = parts(U)
            lhs = jnp.concatenate([hi[:, cut:], hi[:, cut:], lo[:, cut:], lo[:, cut:]], axis=0).T
            rhs = jnp.concatenate([hi, lo, hi, lo], axis=0)
            for q in range(p + 1, n // b):
                old = jnp.where((lanes >= r0) & (lanes < r1), 0.0, panels[q])
                panels[q] = old - dot(lhs[q * b - cut:(q + 1) * b - cut, :], rhs, 1, 0)
            if p in beside:
                beside[p]()
    W = jnp.concatenate(done, axis=0)
    li = lax.broadcasted_iota(jnp.int32, (n, n), 1)
    si = lax.broadcasted_iota(jnp.int32, (n, n), 0)
    return jnp.where(li <= si, W, 0.0)


class Place:
    def __init__(self, ssem, rsem):
        self.ssem, self.rsem = ssem, rsem
        self.sends = []
        self.f = lax.axis_index("fsdp")
        self.t = lax.axis_index("tp")
        self.core = lax.rem(self.f, 2)
        self.other = 1 - self.core
        self.x = lax.rem(self.f // 2, NX)
        self.y = self.f // (2 * NX)
        self.xs = [lax.rem(self.x + j, NX) for j in range(NX)]
        self.ys = [lax.rem(self.y + j, NY) for j in range(NY)]
        self.zs = [lax.rem(self.t + j, NZ) for j in range(NZ)]
        self.sibling = self.dev(self.x, self.y, self.other)
        self.zdev = [(self.f, z) for z in self.zs]
        self.all = [lax.rem(self.f + j, NF) for j in range(NF)]
        self.fdev = [(g, self.t) for g in self.all]
        self.plane = [
            self.dev(self.xs[i], self.ys[j], self.core) for i in range(NX) for j in range(NY) if (i, j) != (0, 0)
        ]
        self.chips = [self.ys[j] * NX + self.xs[i] for i in range(NX) for j in range(NY) if (i, j) != (0, 0)]
        self.chip = self.y * NX + self.x
        self.ways = (
            (self.xs, self.dev(self.xs[1], self.y, self.core), self.dev(self.xs[3], self.y, self.core)),
            (self.ys, self.dev(self.x, self.ys[1], self.core), self.dev(self.x, self.ys[3], self.core)),
        )

        self.twins = (
            (self.dev(self.xs[1], self.y, self.other), self.dev(self.xs[3], self.y, self.other)),
            (self.dev(self.x, self.ys[1], self.other), self.dev(self.x, self.ys[3], self.other)),
        )

    def dev(self, px, py, pc):
        return ((py * NX + px) * 2 + pc, self.t)

    def y_x(self, i, j):
        return self.ys[j] * NX + self.xs[i]

    def greet(self, devices):
        barrier = pltpu.get_barrier_semaphore()
        for device in devices:
            pl.semaphore_signal(barrier, inc=1, device_id=device, device_id_type=MESH)
        return lambda: pl.semaphore_wait(barrier, len(devices))

    def exchange(self, src, dst, device):
        k = len(self.sends)
        cp = pltpu.make_async_remote_copy(
            src_ref=src, dst_ref=dst, send_sem=self.ssem.at[k], recv_sem=self.rsem.at[k],
            device_id=device, device_id_type=MESH,
        )
        cp.start()
        self.sends.append(cp)
        return cp

    def share(self, ref, device):
        return self.exchange(ref, ref, device)


def piece(z, size):
    return pl.ds(pl.multiple_of(z * size, size), size)


def step_kernel(g_hbm, m_hbm, b_hbm, result, both_hbm, inv_hbm, half_hbm, both, inverse, gbuf, mbuf, bbuf, bht, part, rz, left, gpart, rg, own, r2, gram,
                out, rs, r, rc, r16, f1, joined, sab, s16, f2, sq, qc, qp, qz, load, store, gsem, hsem, zsem, ssem, rsem):
    at = Place(ssem, rsem)
    core, other, x, y, xs, ys = at.core, at.other, at.x, at.y, at.xs, at.ys
    nc = COLS // STEP
    loads = []
    for c in range(nc):
        cols = pl.ds(c * STEP, STEP)
        three = [
            pltpu.make_async_copy(b_hbm.at[cols, :], bbuf.at[cols, :], load.at[3 * c]),
            pltpu.make_async_copy(g_hbm.at[:, cols], gbuf.at[:, cols], load.at[3 * c + 1]),
            pltpu.make_async_copy(m_hbm.at[:, cols], mbuf.at[:, cols], load.at[3 * c + 2]),
        ]
        for cp in three:
            cp.start()
        loads.append(three)
    ready = at.greet(at.zdev[1:] + at.fdev[1:])
    total = None
    for c in range(nc):
        for cp in loads[c]:
            cp.wait()
        cols = pl.ds(c * STEP, STEP)
        half = (mbuf[:, cols].astype(F32) + gbuf[:, cols].astype(F32)).astype(BF16)
        gbuf[:, cols] = half
        term = dot(half, bbuf[cols, :], 1, 0)
        total = term if c == 0 else total + term
    part[...] = (total * (1.0 / math.sqrt(N))).astype(BF16)
    ready()
    zr = ROWS // NZ
    cps = [at.exchange(part.at[piece(at.zs[j], zr), :], rz.at[j - 1], at.zdev[j]) for j in range(1, NZ)]
    for c in range(nc):
        cols = pl.ds(c * STEP, STEP)
        bht[cols, :] = gbuf[:, cols].T
    kept = pltpu.make_async_copy(gbuf, half_hbm, store.at[20])
    kept.start()
    mine = part[piece(at.t, zr), :].astype(F32)
    for j in range(1, NZ):
        cps[j - 1].wait_recv()
        mine = mine + rz[j - 1].astype(F32)
    mine = mine.astype(BF16)
    left[piece(at.t, zr), :] = mine
    az = [at.share(left.at[piece(at.t, zr), :], at.zdev[j]) for j in range(1, NZ)]

    full = dot(mine, mine, 0, 0)
    gpart[:, 0:8, :] = full[:128, :128].reshape(16, 8, 128)
    gpart[:, 8:16, :] = full[:128, 128:].reshape(16, 8, 128)
    gpart[:, 16:24, :] = full[128:, 128:].reshape(16, 8, 128)
    owner = lax.rem(x + y, 2) == core
    chips = [(i, j) for i in range(NX) for j in range(NY)]

    def to_owner(k, slot):
        i, j = chips[k]
        device = at.dev(xs[i], ys[j], lax.rem(xs[i] + ys[j], 2))
        return pltpu.make_async_remote_copy(
            src_ref=gpart.at[at.y_x(i, j)], dst_ref=rg.at[slot], send_sem=gsem.at[k], recv_sem=gsem.at[16 + slot],
            device_id=device if k else at.sibling, device_id_type=MESH,
        )

    scattered = [to_owner(k, 2 * k - 1 + core if k else 0) for k in range(16)]

    @pl.when(jnp.logical_not(owner))
    def _():
        scattered[0].start()

    for k in range(1, 16):
        scattered[k].start()

    def to_all(k, c):
        i, j = chips[k]
        return pltpu.make_async_remote_copy(
            src_ref=gram.at[at.chip], dst_ref=gram.at[at.chip], send_sem=hsem.at[2 * k + c], recv_sem=hsem.at[32 + k],
            device_id=at.dev(xs[i], ys[j], c) if k else at.sibling, device_id_type=MESH,
        )

    gathered = [to_all(0, 0)] + [to_all(k, c) for k in range(1, 16) for c in range(2)]
    across = [
        pltpu.make_async_remote_copy(
            src_ref=own, dst_ref=r2.at[j - 1], send_sem=zsem.at[j], recv_sem=zsem.at[8 + j],
            device_id=at.zdev[j], device_id_type=MESH,
        )
        for j in range(1, NZ)
    ]

    @pl.when(owner)
    def _():
        acc = gpart[at.chip]
        for slot in range(31):
            to_owner(0, slot).wait_recv()
            acc = acc + rg[slot]
        own[...] = acc
        for cp in across:
            cp.start()

    for cp in az:
        cp.wait_recv()
    wide = COLS // 2
    nk = wide // CHUNK
    qk = NX // nk

    def product(k, pc, into):
        half = bht[pl.ds(pl.multiple_of(pc * wide + k * CHUNK, 128), CHUNK), :]
        val = dot(half, left[...], 1, 0)
        for h in range(2):
            into[h, k * qk:(k + 1) * qk] = val[:, 128 * h:128 * h + 128].reshape(qk, NY, BLOCK, 128).astype(into.dtype)

    cc = []
    for k in range(nk):
        product(k, other, rs)
        qs = pl.ds(k * qk, qk)
        cc.append([at.exchange(rs.at[h, qs], rc.at[h, qs], at.sibling) for h in range(2)])

    @pl.when(owner)
    def _():
        acc = own[...]
        for j in range(1, NZ):
            across[j - 1].wait_recv()
            acc = acc + r2[j - 1]
        gram[at.chip] = acc
        for cp in gathered:
            cp.start()

    for k in range(nk):
        product(k, core, r)
    def half_of(ref, h, q, k):
        return ref.at[0, q, pl.ds(2 * k, 2)] if h == 0 else ref.at[1, pl.ds(2 * k, 2), q]

    one = []
    for h in range(2):
        for k in range(nk):
            qs = pl.ds(k * qk, qk)
            cc[k][h].wait_recv()
            total = r[h, qs] + rc[h, qs].astype(F32)
            r[h, qs] = total
            r16[h, qs] = total.astype(BF16)
        pos, nxt, prv = at.ways[h]
        one.append([
            at.exchange(half_of(r16, h, pos[2], 0), f1.at[h, 0], nxt), at.exchange(half_of(r16, h, pos[2], 1), f1.at[h, 1], prv),
        ])
    for h in range(2):
        pos, nxt, prv = at.ways[h]
        one[h] += [
            at.exchange(half_of(r16, h, pos[1], 1), f1.at[h, 2], nxt), at.exchange(half_of(r16, h, pos[3], 0), f1.at[h, 3], prv),
        ]
    for h in range(2):
        pos, nxt, prv = at.ways[h]
        for k, (q, to) in enumerate(((pos[1], nxt), (pos[3], prv))):
            one[h][k].wait_recv()
            joined[h, k] = (half_of(r, h, q, k)[...] + f1[h, k].astype(F32)).astype(BF16)
            one[h].append(at.exchange(joined.at[h, k], f1.at[h, 4 + k], to))
    for k in range(1, 16):
        to_all(k, 0).wait_recv()

    @pl.when(jnp.logical_not(owner))
    def _():
        to_all(0, 0).wait_recv()

    upper = jnp.concatenate([gram[:, 0:8, :].reshape(128, 128), gram[:, 8:16, :].reshape(128, 128)], axis=1)
    corner = gram[:, 16:24, :].reshape(128, 128)
    full = jnp.concatenate([upper, jnp.concatenate([jnp.zeros_like(corner), corner], axis=1)], axis=0)
    two = [[], []]

    def second_stage():
        for h in range(2):
            for k in range(2, 6):
                one[h][k].wait_recv()
            for k in range(2):
                total = half_of(r, h, x if h == 0 else y, k)[...] + f1[h, 3 - k].astype(F32) + f1[h, 4 + k].astype(F32)
                sab[h, 2 * k:2 * k + 2] = total
                s16[h, 2 * k:2 * k + 2] = total.astype(BF16)
            for j in range(1, NX):
                if h == 0:
                    two[h].append(at.exchange(s16.at[h, ys[j]], f2.at[h, j - 1], at.dev(x, ys[j], core)))
                else:
                    two[h].append(at.exchange(s16.at[h, xs[j]], f2.at[h, j - 1], at.dev(xs[j], y, core)))

    w = lower_inverse(full, {2: second_stage})
    whi, wlo = parts(w)
    halves = []
    for h in range(2):
        total = sab[h, y if h == 0 else x]
        for j in range(1, NX):
            two[h][j - 1].wait_recv()
            total = total + f2[h, j - 1].astype(F32)
        halves.append(total)
    hi, lo = parts(jnp.concatenate(halves, axis=1))
    right = dot(jnp.concatenate([hi, lo], axis=0), whi, 1, 1)
    right = right[:BLOCK] + right[BLOCK:] + dot(hi, wlo, 1, 1)
    rounded = right.astype(BF16)
    for h in range(2):
        out[h, core, x, y] = rounded[:, 128 * h:128 * h + 128]
    g2 = [[], []]
    for j in (2, 1, 3):
        g2[0].append(at.share(out.at[0, core, x, y], at.dev(x, ys[j], core)))
        g2[1].append(at.share(out.at[1, core, x, y], at.dev(xs[j], y, core)))
    total = jnp.sum(right * right, axis=0, keepdims=True)
    srow = lax.broadcasted_iota(jnp.int32, (8, 128), 0)
    sq[...] = jnp.where(srow == 0, total[:, :128], total[:, 128:])
    sc = at.exchange(sq, qc, at.sibling)
    ortho = dot(left[...], whi, 1, 1) + dot(left[...], wlo, 1, 1)
    both[0:ROWS, :] = ortho.astype(BF16)
    sc.wait_recv()
    qp[at.chip] = sq[...] + qc[...]
    sp = [at.share(qp.at[at.chip], device) for device in at.plane]
    def band(h, q, k=None, ref=out, pc=core):
        if k is None:
            return ref.at[0, pc, q] if h == 0 else ref.at[1, pc, :, q]
        return ref.at[0, pc, q, pl.ds(2 * k, 2)] if h == 0 else ref.at[1, pc, pl.ds(2 * k, 2), q]

    last, spans, stores = [], [], []

    def keep(h, q, k, pc):
        cp = pltpu.make_async_copy(band(h, q, k, out, pc), band(h, q, k, result, pc), store.at[len(stores)])
        cp.start()
        stores.append(cp)

    def forward(h, q, k=None):
        last.append(at.share(band(h, q, k), at.sibling))
        spans.append((h, q, k))
        keep(h, q, k, core)

    begun = []
    for h in range(2):
        for cp in g2[h]:
            cp.wait_recv()
        pos, nxt, prv = at.ways[h]
        begun.append([
            at.share(band(h, pos[0], 0), nxt), at.share(band(h, pos[0], 1), prv),
            at.share(band(h, pos[0], 1), nxt), at.share(band(h, pos[0], 0), prv),
        ])
    for h in range(2):
        forward(h, at.ways[h][0][0])
    old = len(at.sends) - 10
    for cp in sp:
        cp.wait_recv()
    total = qp[0]
    for j in range(1, NX * NY):
        total = total + qp[j]
    qz[at.t] = total
    sz = [at.share(qz.at[at.t], at.zdev[j]) for j in range(1, NZ)]
    relays = []
    for h in range(2):
        pos, nxt, prv = at.ways[h]
        for k, (q, near, far) in enumerate(((pos[3], nxt, at.twins[h][0]), (pos[1], prv, at.twins[h][1]))):
            begun[h][k].wait_recv()
            relays.append((at.share(band(h, q, k), near), at.share(band(h, q, k), far)))
    for h in range(2):
        pos = at.ways[h][0]
        begun[h][2].wait_recv()
        forward(h, pos[3])
        begun[h][3].wait_recv()
        forward(h, pos[1])
    for cp in at.sends[:old] + scattered[1:]:
        cp.wait_send()
    kept.wait()

    @pl.when(jnp.logical_not(owner))
    def _():
        scattered[0].wait_send()

    @pl.when(owner)
    def _():
        for cp in across + gathered:
            cp.wait_send()

    for cp in sz:
        cp.wait_recv()
    total = qz[0]
    for j in range(1, NZ):
        total = total + qz[j]
    scale = jnp.sqrt(jnp.concatenate([total[0:1, :], total[1:2, :]], axis=1) / N + 1e-06)
    inverse[...] = jnp.broadcast_to(1.0 / scale, (8, RANK))
    both[ROWS:, :] = (ortho * (math.sqrt(M / RANK) / scale)).astype(BF16)
    small = [
        pltpu.make_async_copy(both, both_hbm, store.at[21]), pltpu.make_async_copy(inverse, inv_hbm, store.at[22]),
    ]
    for cp in small:
        cp.start()
    for cp, (h, q, k) in zip(last, spans):
        cp.wait_recv()
        keep(h, q, k, other)
    for h in range(2):
        pos = at.ways[h][0]
        for k in range(2):
            near, far = relays[2 * h + k]
            near.wait_recv()
            keep(h, pos[2], k, core)
            far.wait_recv()
            keep(h, pos[2], k, other)
    for cp in at.sends[old:]:
        cp.wait_send()
    for cp in stores + small:
        cp.wait()


def output_kernel(half_hbm, both_hbm, right_hbm, inv_hbm, update, new_momentum, new_basis,
                  hbuf, both, rbuf, inv, ubuf, nbuf, bbuf, load, store):
    nc = COLS // STEP
    first = [
        pltpu.make_async_copy(both_hbm, both, load.at[3 * nc]),
        pltpu.make_async_copy(inv_hbm, inv, load.at[3 * nc + 1]),
    ]
    loads = []
    for c in range(nc):
        cols = pl.ds(c * STEP, STEP)
        loads.append([
            pltpu.make_async_copy(right_hbm.at[0, cols, :], rbuf.at[0, cols, :], load.at[3 * c]),
            pltpu.make_async_copy(right_hbm.at[1, cols, :], rbuf.at[1, cols, :], load.at[3 * c + 1]),
            pltpu.make_async_copy(half_hbm.at[:, cols], hbuf.at[:, cols], load.at[3 * c + 2]),
        ])
    for cp in first:
        cp.start()
    for group in loads:
        for cp in group:
            cp.start()
    for cp in first:
        cp.wait()
    stores = []
    for c in range(nc):
        cols = pl.ds(c * STEP, STEP)
        for cp in loads[c]:
            cp.wait()
        rr = jnp.concatenate([rbuf[0, cols, :], rbuf[1, cols, :]], axis=1)
        bbuf[cols, :] = (rr.astype(F32) * inv[0:1, :]).astype(BF16)
        product = dot(both[...], rr, 1, 1)
        ubuf[:, cols] = product[ROWS:].astype(BF16)
        nbuf[:, cols] = (hbuf[:, cols].astype(F32) - (1.0 - MU / 100.0) * product[:ROWS]).astype(BF16)
        three = [
            pltpu.make_async_copy(bbuf.at[cols, :], new_basis.at[cols, :], store.at[3 * c]),
            pltpu.make_async_copy(ubuf.at[:, cols], update.at[:, cols], store.at[3 * c + 1]),
            pltpu.make_async_copy(nbuf.at[:, cols], new_momentum.at[:, cols], store.at[3 * c + 2]),
        ]
        for cp in three:
            cp.start()
        stores += three
    for cp in stores:
        cp.wait()


def body(grad, momentum, basis):
    dma = pltpu.SemaphoreType.DMA
    zr = ROWS // NZ
    sends = 7 + 7 + 4 + 12 + 6 + 6 + 1 + 15 + 8 + 6 + 7 + 8
    right, both, inverse, half = pl.pallas_call(
        step_kernel,
        out_shape=(
            jax.ShapeDtypeStruct((2, 2, NX, NY, BLOCK, 128), BF16),
            jax.ShapeDtypeStruct((2 * ROWS, RANK), BF16),
            jax.ShapeDtypeStruct((8, RANK), F32),
            jax.ShapeDtypeStruct((ROWS, COLS), BF16),
        ),
        in_specs=[pl.BlockSpec(memory_space=pl.ANY)] * 3,
        out_specs=tuple(pl.BlockSpec(memory_space=pl.ANY) for _ in range(4)),
        scratch_shapes=[
            pltpu.VMEM((2 * ROWS, RANK), BF16), pltpu.VMEM((8, RANK), F32),
            pltpu.VMEM((ROWS, COLS), BF16), pltpu.VMEM((ROWS, COLS), BF16), pltpu.VMEM((COLS, RANK), BF16),
            pltpu.VMEM((COLS, RANK), BF16),
            pltpu.VMEM((ROWS, RANK), BF16), pltpu.VMEM((NZ - 1, zr, RANK), BF16), pltpu.VMEM((ROWS, RANK), BF16),
            pltpu.VMEM((16, 24, 128), F32), pltpu.VMEM((31, 24, 128), F32),
            pltpu.VMEM((24, 128), F32), pltpu.VMEM((NZ - 1, 24, 128), F32), pltpu.VMEM((16, 24, 128), F32),
            pltpu.VMEM((2, 2, NX, NY, BLOCK, 128), BF16), pltpu.VMEM((2, NX, NY, BLOCK, 128), BF16),
            pltpu.VMEM((2, NX, NY, BLOCK, 128), F32), pltpu.VMEM((2, NX, NY, BLOCK, 128), BF16),
            pltpu.VMEM((2, NX, NY, BLOCK, 128), BF16), pltpu.VMEM((2, 6, 2, BLOCK, 128), BF16), pltpu.VMEM((2, 2, 2, BLOCK, 128), BF16),
            pltpu.VMEM((2, 4, BLOCK, 128), F32), pltpu.VMEM((2, 4, BLOCK, 128), BF16), pltpu.VMEM((2, 3, BLOCK, 128), BF16),
            pltpu.VMEM((8, 128), F32), pltpu.VMEM((8, 128), F32),
            pltpu.VMEM((NX * NY, 8, 128), F32), pltpu.VMEM((NZ, 8, 128), F32),
            dma((3 * (COLS // STEP),)), dma((23,)), dma((47,)), dma((48,)), dma((16,)), dma((sends,)), dma((sends,)),
        ],
        compiler_params=pltpu.CompilerParams(collective_id=0, has_side_effects=True, vmem_limit_bytes=VMEM_LIMIT),
        name="step_kernel",
    )(grad, momentum, basis)
    nc = COLS // STEP
    wide = pltpu.VMEM((ROWS, COLS), BF16)
    return pl.pallas_call(
        output_kernel,
        out_shape=(
            jax.ShapeDtypeStruct((ROWS, COLS), BF16),
            jax.ShapeDtypeStruct((ROWS, COLS), BF16),
            jax.ShapeDtypeStruct((COLS, RANK), BF16),
        ),
        in_specs=[pl.BlockSpec(memory_space=pl.ANY)] * 4,
        out_specs=tuple(pl.BlockSpec(memory_space=pl.ANY) for _ in range(3)),
        scratch_shapes=[
            wide, pltpu.VMEM((2 * ROWS, RANK), BF16), pltpu.VMEM((2, COLS, 128), BF16), pltpu.VMEM((8, RANK), F32),
            wide, wide, pltpu.VMEM((COLS, RANK), BF16),
            dma((3 * nc + 2,)), dma((3 * nc,)),
        ],
        compiler_params=pltpu.CompilerParams(vmem_limit_bytes=VMEM_LIMIT),
        name="output_kernel",
    )(half, both, right.reshape(2, COLS, 128), inverse)


def solution(mesh):
    placed = (P("fsdp", "tp"), P("fsdp", "tp"), P("tp", None))
    return jax.shard_map(
        body,
        mesh=mesh,
        in_specs=placed,
        out_specs=(P("fsdp", "tp"), P("fsdp", "tp"), P("tp", None)),
        check_vma=False,
    )
```

```python
import math

import jax
import jax.numpy as jnp
from jax import lax
from jax.experimental import pallas as pl
from jax.experimental.pallas import tpu as pltpu
from jax.sharding import PartitionSpec as P

M = 8192
N = 28672
RANK = 256
MU = 90

MESH = pl.DeviceIdType.MESH
HI = lax.Precision.HIGHEST
F32 = jnp.float32
BF16 = jnp.bfloat16
NX, NY, NZ = 4, 4, 8
NF = NX * NY * 2
ROWS = M // NF
COLS = N // NZ
CHUNK = 896
BLOCK = COLS // NF
FAR_FIRST = sorted(range(1, NZ), key=lambda j: -min(j, NZ - j))
STEP = 512
VMEM_LIMIT = 60 * 1024 * 1024


def dot(a, b, ca, cb, precision=None):
    return lax.dot_general(
        a, b, (((ca,), (cb,)), ((), ())), precision=precision, preferred_element_type=F32
    )


def lane_of(tile, j):
    return jnp.broadcast_to(tile[j:j + 1, :], tile.shape)


def column_of(tile, j):
    return jnp.broadcast_to(tile[:, j:j + 1], tile.shape)


def reciprocal(v):
    near = pl.reciprocal(v, approx=True)
    return near * (2.0 - v * near)


def parts(v):
    hi = v.astype(BF16)
    return hi, (v - hi.astype(F32)).astype(BF16)


def lower_inverse(gram, beside, b=64, s8=8):
    n = gram.shape[0]
    tiles = b // 8
    nt = n // 128
    rows = lax.broadcasted_iota(jnp.int32, (8, 128), 0)
    ln = lax.broadcasted_iota(jnp.int32, (8, 128), 1)
    lanes = lax.broadcasted_iota(jnp.int32, (b, n), 1)
    panels = [gram[p * b:(p + 1) * b, :] for p in range(n // b)]
    done = []
    for p in range(n // b):
        r0 = p * b
        home = r0 // 128
        P_ = panels[p]
        M_ = [[P_[8 * a:8 * a + 8, 128 * l:128 * l + 128] for l in range(nt)] for a in range(tiles)]
        for a in range(tiles):
            M_[a].append(jnp.where(ln + home * 128 == rows + (r0 + 8 * a), 1.0, 0.0))
        piv = [jnp.ones((8, 128), F32) for _ in range(tiles)]
        ahead = None
        for s in range(tiles):
            lane = r0 - home * 128 + s * s8
            C = []
            for k in range(s8):
                C.append([column_of(M_[a][home], lane + k) if a > s else None for a in range(tiles)])
                C[k][s] = column_of(M_[s][home], lane + k) if ahead is None else ahead[k]
            ahead = [column_of(M_[s + 1][home], lane + s8 + k) for k in range(s8)] if s + 1 < tiles else None
            for j in range(0, s8, 2):
                first, second = C[j], C[j + 1]
                p11 = lane_of(first[s], j)
                p12 = lane_of(first[s], j + 1)
                p22 = lane_of(second[s], j + 1)
                det = p11 * p22 - p12 * p12
                inv1 = reciprocal(p11)
                mult = p12 * inv1
                near = pl.reciprocal(det, approx=True)
                fix = 2.0 - det * near
                w1 = [first[a] * inv1 if a >= s else None for a in range(tiles)]
                second = [second[a] - first[a] * mult if a >= s else None for a in range(tiles)]
                w2 = [((second[a] * p11) * near) * fix if a >= s else None for a in range(tiles)]
                if ahead is not None:
                    for k in range(s8):
                        b1, b2 = lane_of(first[s + 1], k), lane_of(second[s + 1], k)
                        ahead[k] = (ahead[k] - w1[s + 1] * b1) - w2[s + 1] * b2
                for k in range(j + 2, s8):
                    b1 = lane_of(first[s], k)
                    b2 = lane_of(second[s], k)
                    for a in range(s, tiles):
                        C[k][a] = (C[k][a] - w1[a] * b1) - w2[a] * b2
                w1[s] = jnp.where(rows > j, w1[s], 0.0)
                w2[s] = jnp.where(rows > j + 1, w2[s], 0.0)
                piv[s] = jnp.where(rows == j, p11, jnp.where(rows == j + 1, det * inv1, piv[s]))
                for l in range(nt + 1):
                    b1 = lane_of(M_[s][l], j)
                    b2 = lane_of(M_[s][l], j + 1) - b1 * mult
                    for a in range(s, tiles):
                        M_[a][l] = (M_[a][l] - w1[a] * b1) - w2[a] * b2
        full = []
        for a in range(tiles):
            root = lax.rsqrt(piv[a])
            out = [v * root for v in M_[a]]
            ident = out.pop()
            at = ln + home * 128
            out[home] = jnp.where((at >= r0) & (at < r0 + b), ident, out[home])
            full.append(jnp.concatenate(out, axis=1))
        U = jnp.concatenate(full, axis=0)
        done.append(U)
        if p + 1 < n // b:
            r1 = r0 + b
            cut = r1 // 128 * 128
            hi, lo = parts(U)
            lhs = jnp.concatenate([hi[:, cut:], hi[:, cut:], lo[:, cut:], lo[:, cut:]], axis=0).T
            rhs = jnp.concatenate([hi, lo, hi, lo], axis=0)
            for q in range(p + 1, n // b):
                old = jnp.where((lanes >= r0) & (lanes < r1), 0.0, panels[q])
                panels[q] = old - dot(lhs[q * b - cut:(q + 1) * b - cut, :], rhs, 1, 0)
            if p in beside:
                beside[p]()
    W = jnp.concatenate(done, axis=0)
    li = lax.broadcasted_iota(jnp.int32, (n, n), 1)
    si = lax.broadcasted_iota(jnp.int32, (n, n), 0)
    return jnp.where(li <= si, W, 0.0)


class Place:
    def __init__(self, ssem, rsem):
        self.ssem, self.rsem = ssem, rsem
        self.sends = []
        self.f = lax.axis_index("fsdp")
        self.t = lax.axis_index("tp")
        self.core = lax.rem(self.f, 2)
        self.other = 1 - self.core
        self.x = lax.rem(self.f // 2, NX)
        self.y = self.f // (2 * NX)
        self.xs = [lax.rem(self.x + j, NX) for j in range(NX)]
        self.ys = [lax.rem(self.y + j, NY) for j in range(NY)]
        self.zs = [lax.rem(self.t + j, NZ) for j in range(NZ)]
        self.sibling = self.dev(self.x, self.y, self.other)
        self.zdev = [(self.f, z) for z in self.zs]
        self.all = [lax.rem(self.f + j, NF) for j in range(NF)]
        self.fdev = [(g, self.t) for g in self.all]
        self.plane = [
            self.dev(self.xs[i], self.ys[j], self.core) for i in range(NX) for j in range(NY) if (i, j) != (0, 0)
        ]
        self.chips = [self.ys[j] * NX + self.xs[i] for i in range(NX) for j in range(NY) if (i, j) != (0, 0)]
        self.chip = self.y * NX + self.x
        self.ways = (
            (self.xs, self.dev(self.xs[1], self.y, self.core), self.dev(self.xs[3], self.y, self.core)),
            (self.ys, self.dev(self.x, self.ys[1], self.core), self.dev(self.x, self.ys[3], self.core)),
        )

        self.twins = (
            (self.dev(self.xs[1], self.y, self.other), self.dev(self.xs[3], self.y, self.other)),
            (self.dev(self.x, self.ys[1], self.other), self.dev(self.x, self.ys[3], self.other)),
        )

    def dev(self, px, py, pc):
        return ((py * NX + px) * 2 + pc, self.t)

    def y_x(self, i, j):
        return self.ys[j] * NX + self.xs[i]

    def greet(self, devices):
        barrier = pltpu.get_barrier_semaphore()
        for device in devices:
            pl.semaphore_signal(barrier, inc=1, device_id=device, device_id_type=MESH)
        return lambda: pl.semaphore_wait(barrier, len(devices))

    def exchange(self, src, dst, device):
        k = len(self.sends)
        cp = pltpu.make_async_remote_copy(
            src_ref=src, dst_ref=dst, send_sem=self.ssem.at[k], recv_sem=self.rsem.at[k],
            device_id=device, device_id_type=MESH,
        )
        cp.start()
        self.sends.append(cp)
        return cp

    def share(self, ref, device):
        return self.exchange(ref, ref, device)


def piece(z, size):
    return pl.ds(pl.multiple_of(z * size, size), size)


def step_kernel(g_hbm, m_hbm, b_hbm, result, both_hbm, inv_hbm, half_hbm, both, inverse, gbuf, mbuf, bbuf, bht, part, rz, left, gpart, rg, own, r2, gram,
                out, rs, r, rc, r16, f1, joined, sab, s16, f2, sq, qc, qp, qz, load, store, gsem, hsem, zsem, ssem, rsem):
    at = Place(ssem, rsem)
    core, other, x, y, xs, ys = at.core, at.other, at.x, at.y, at.xs, at.ys
    nc = COLS // STEP
    loads = []
    for c in range(nc):
        cols = pl.ds(c * STEP, STEP)
        three = [
            pltpu.make_async_copy(b_hbm.at[cols, :], bbuf.at[cols, :], load.at[3 * c]),
            pltpu.make_async_copy(g_hbm.at[:, cols], gbuf.at[:, cols], load.at[3 * c + 1]),
            pltpu.make_async_copy(m_hbm.at[:, cols], mbuf.at[:, cols], load.at[3 * c + 2]),
        ]
        for cp in three:
            cp.start()
        loads.append(three)
    ready = at.greet(at.zdev[1:] + at.fdev[1:])
    total = None
    for c in range(nc):
        for cp in loads[c]:
            cp.wait()
        cols = pl.ds(c * STEP, STEP)
        half = (mbuf[:, cols].astype(F32) + gbuf[:, cols].astype(F32)).astype(BF16)
        gbuf[:, cols] = half
        term = dot(half, bbuf[cols, :], 1, 0)
        total = term if c == 0 else total + term
    part[...] = (total * (1.0 / math.sqrt(N))).astype(BF16)
    ready()
    zr = ROWS // NZ
    cps = [at.exchange(part.at[piece(at.zs[j], zr), :], rz.at[j - 1], at.zdev[j]) for j in FAR_FIRST]
    for c in range(nc):
        cols = pl.ds(c * STEP, STEP)
        bht[cols, :] = gbuf[:, cols].T
    kept = pltpu.make_async_copy(gbuf, half_hbm, store.at[20])
    kept.start()
    mine = part[piece(at.t, zr), :].astype(F32)
    for cp in cps:
        cp.wait_recv()
    for j in range(1, NZ):
        mine = mine + rz[j - 1].astype(F32)
    mine = mine.astype(BF16)
    left[piece(at.t, zr), :] = mine
    az = [at.share(left.at[piece(at.t, zr), :], at.zdev[j]) for j in FAR_FIRST]

    full = dot(mine, mine, 0, 0)
    gpart[:, 0:8, :] = full[:128, :128].reshape(16, 8, 128)
    gpart[:, 8:16, :] = full[:128, 128:].reshape(16, 8, 128)
    gpart[:, 16:24, :] = full[128:, 128:].reshape(16, 8, 128)
    owner = lax.rem(x + y, 2) == core
    chips = sorted(((i, j) for i in range(NX) for j in range(NY)), key=lambda c: -min(c[0], NX - c[0]) - min(c[1], NY - c[1]))
    chips = chips[-1:] + chips[:-1]

    def to_owner(k, slot):
        i, j = chips[k]
        device = at.dev(xs[i], ys[j], lax.rem(xs[i] + ys[j], 2))
        return pltpu.make_async_remote_copy(
            src_ref=gpart.at[at.y_x(i, j)], dst_ref=rg.at[slot], send_sem=gsem.at[k], recv_sem=gsem.at[16 + slot],
            device_id=device if k else at.sibling, device_id_type=MESH,
        )

    scattered = [to_owner(k, 2 * k - 1 + core if k else 0) for k in range(16)]

    @pl.when(jnp.logical_not(owner))
    def _():
        scattered[0].start()

    for k in range(1, 16):
        scattered[k].start()

    def to_all(k, c):
        i, j = chips[k]
        return pltpu.make_async_remote_copy(
            src_ref=gram.at[at.chip], dst_ref=gram.at[at.chip], send_sem=hsem.at[2 * k + c], recv_sem=hsem.at[32 + k],
            device_id=at.dev(xs[i], ys[j], c) if k else at.sibling, device_id_type=MESH,
        )

    gathered = [to_all(0, 0)] + [to_all(k, c) for k in range(1, 16) for c in range(2)]
    across = [
        pltpu.make_async_remote_copy(
            src_ref=own, dst_ref=r2.at[j - 1], send_sem=zsem.at[j], recv_sem=zsem.at[8 + j],
            device_id=at.zdev[j], device_id_type=MESH,
        )
        for j in range(1, NZ)
    ]

    @pl.when(owner)
    def _():
        acc = gpart[at.chip]
        for slot in range(31):
            to_owner(0, slot).wait_recv()
            acc = acc + rg[slot]
        own[...] = acc
        for j in FAR_FIRST:
            across[j - 1].start()

    for cp in az:
        cp.wait_recv()
    wide = COLS // 2
    nk = wide // CHUNK
    qk = NX // nk

    def product(k, pc, into):
        half = bht[pl.ds(pl.multiple_of(pc * wide + k * CHUNK, 128), CHUNK), :]
        val = dot(half, left[...], 1, 0)
        for h in range(2):
            into[h, k * qk:(k + 1) * qk] = val[:, 128 * h:128 * h + 128].reshape(qk, NY, BLOCK, 128).astype(into.dtype)

    cc = []
    for k in range(nk):
        product(k, other, rs)
        qs = pl.ds(k * qk, qk)
        cc.append([at.exchange(rs.at[h, qs], rc.at[h, qs], at.sibling) for h in range(2)])

    @pl.when(owner)
    def _():
        acc = own[...]
        for j in range(1, NZ):
            across[j - 1].wait_recv()
            acc = acc + r2[j - 1]
        gram[at.chip] = acc
        for cp in gathered:
            cp.start()

    for k in range(nk):
        product(k, core, r)
    def half_of(ref, h, q, k):
        return ref.at[0, q, pl.ds(2 * k, 2)] if h == 0 else ref.at[1, pl.ds(2 * k, 2), q]

    one = []
    for h in range(2):
        for k in range(nk):
            qs = pl.ds(k * qk, qk)
            cc[k][h].wait_recv()
            total = r[h, qs] + rc[h, qs].astype(F32)
            r[h, qs] = total
            r16[h, qs] = total.astype(BF16)
        pos, nxt, prv = at.ways[h]
        one.append([
            at.exchange(half_of(r16, h, pos[2], 0), f1.at[h, 0], nxt), at.exchange(half_of(r16, h, pos[2], 1), f1.at[h, 1], prv),
        ])
    for h in range(2):
        pos, nxt, prv = at.ways[h]
        one[h] += [
            at.exchange(half_of(r16, h, pos[1], 1), f1.at[h, 2], nxt), at.exchange(half_of(r16, h, pos[3], 0), f1.at[h, 3], prv),
        ]
    for h in range(2):
        pos, nxt, prv = at.ways[h]
        for k, (q, to) in enumerate(((pos[1], nxt), (pos[3], prv))):
            one[h][k].wait_recv()
            joined[h, k] = (half_of(r, h, q, k)[...] + f1[h, k].astype(F32)).astype(BF16)
            one[h].append(at.exchange(joined.at[h, k], f1.at[h, 4 + k], to))
    for k in range(1, 16):
        to_all(k, 0).wait_recv()

    @pl.when(jnp.logical_not(owner))
    def _():
        to_all(0, 0).wait_recv()

    upper = jnp.concatenate([gram[:, 0:8, :].reshape(128, 128), gram[:, 8:16, :].reshape(128, 128)], axis=1)
    corner = gram[:, 16:24, :].reshape(128, 128)
    full = jnp.concatenate([upper, jnp.concatenate([jnp.zeros_like(corner), corner], axis=1)], axis=0)
    two = [[], []]

    def second_stage():
        for h in range(2):
            for k in range(2, 6):
                one[h][k].wait_recv()
            for k in range(2):
                total = half_of(r, h, x if h == 0 else y, k)[...] + f1[h, 3 - k].astype(F32) + f1[h, 4 + k].astype(F32)
                sab[h, 2 * k:2 * k + 2] = total
                s16[h, 2 * k:2 * k + 2] = total.astype(BF16)
            for j in (2, 1, 3):
                if h == 0:
                    two[h].append(at.exchange(s16.at[h, ys[j]], f2.at[h, j - 1], at.dev(x, ys[j], core)))
                else:
                    two[h].append(at.exchange(s16.at[h, xs[j]], f2.at[h, j - 1], at.dev(xs[j], y, core)))

    unit = lax.rsqrt(full[0:1, 0:1])
    w = lower_inverse((full * unit) * unit, {2: second_stage}) * unit
    whi, wlo = parts(w)
    halves = []
    for h in range(2):
        total = sab[h, y if h == 0 else x]
        for cp in two[h]:
            cp.wait_recv()
        for j in range(1, NX):
            total = total + f2[h, j - 1].astype(F32)
        halves.append(total)
    hi, lo = parts(jnp.concatenate(halves, axis=1))
    right = dot(jnp.concatenate([hi, lo], axis=0), whi, 1, 1)
    right = right[:BLOCK] + right[BLOCK:] + dot(hi, wlo, 1, 1)
    rounded = right.astype(BF16)
    for h in range(2):
        out[h, core, x, y] = rounded[:, 128 * h:128 * h + 128]
    g2 = [[], []]
    for j in (2, 1, 3):
        g2[0].append(at.share(out.at[0, core, x, y], at.dev(x, ys[j], core)))
        g2[1].append(at.share(out.at[1, core, x, y], at.dev(xs[j], y, core)))
    total = jnp.sum(right * right, axis=0, keepdims=True)
    srow = lax.broadcasted_iota(jnp.int32, (8, 128), 0)
    sq[...] = jnp.where(srow == 0, total[:, :128], total[:, 128:])
    sc = at.exchange(sq, qc, at.sibling)
    ortho = dot(left[...], whi, 1, 1) + dot(left[...], wlo, 1, 1)
    both[0:ROWS, :] = ortho.astype(BF16)
    sc.wait_recv()
    qp[at.chip] = sq[...] + qc[...]
    sp = [at.share(qp.at[at.chip], device) for device in at.plane]
    def band(h, q, k=None, ref=out, pc=core):
        if k is None:
            return ref.at[0, pc, q] if h == 0 else ref.at[1, pc, :, q]
        return ref.at[0, pc, q, pl.ds(2 * k, 2)] if h == 0 else ref.at[1, pc, pl.ds(2 * k, 2), q]

    last, spans, stores = [], [], []

    def keep(h, q, k, pc):
        cp = pltpu.make_async_copy(band(h, q, k, out, pc), band(h, q, k, result, pc), store.at[len(stores)])
        cp.start()
        stores.append(cp)

    def forward(h, q, k=None):
        last.append(at.share(band(h, q, k), at.sibling))
        spans.append((h, q, k))
        keep(h, q, k, core)

    begun = []
    for h in range(2):
        for cp in g2[h]:
            cp.wait_recv()
        pos, nxt, prv = at.ways[h]
        begun.append([
            at.share(band(h, pos[0], 0), nxt), at.share(band(h, pos[0], 1), prv),
            at.share(band(h, pos[0], 1), nxt), at.share(band(h, pos[0], 0), prv),
        ])
    for h in range(2):
        forward(h, at.ways[h][0][0])
    old = len(at.sends) - 10
    for cp in sp:
        cp.wait_recv()
    total = qp[0]
    for j in range(1, NX * NY):
        total = total + qp[j]
    qz[at.t] = total
    sz = [at.share(qz.at[at.t], at.zdev[j]) for j in range(1, NZ)]
    relays = []
    for h in range(2):
        pos, nxt, prv = at.ways[h]
        for k, (q, near, far) in enumerate(((pos[3], nxt, at.twins[h][0]), (pos[1], prv, at.twins[h][1]))):
            begun[h][k].wait_recv()
            relays.append((at.share(band(h, q, k), near), at.share(band(h, q, k), far)))
    for h in range(2):
        pos = at.ways[h][0]
        begun[h][2].wait_recv()
        forward(h, pos[3])
        begun[h][3].wait_recv()
        forward(h, pos[1])
    for cp in at.sends[:old] + scattered[1:]:
        cp.wait_send()
    kept.wait()

    @pl.when(jnp.logical_not(owner))
    def _():
        scattered[0].wait_send()

    @pl.when(owner)
    def _():
        for cp in across + gathered:
            cp.wait_send()

    for cp in sz:
        cp.wait_recv()
    total = qz[0]
    for j in range(1, NZ):
        total = total + qz[j]
    scale = jnp.sqrt(jnp.concatenate([total[0:1, :], total[1:2, :]], axis=1) / N + 1e-06)
    inverse[...] = jnp.broadcast_to(1.0 / scale, (8, RANK))
    both[ROWS:, :] = (ortho * (math.sqrt(M / RANK) / scale)).astype(BF16)
    small = [
        pltpu.make_async_copy(both, both_hbm, store.at[21]), pltpu.make_async_copy(inverse, inv_hbm, store.at[22]),
    ]
    for cp in small:
        cp.start()
    for cp, (h, q, k) in zip(last, spans):
        cp.wait_recv()
        keep(h, q, k, other)
    for h in range(2):
        pos = at.ways[h][0]
        for k in range(2):
            near, far = relays[2 * h + k]
            near.wait_recv()
            keep(h, pos[2], k, core)
            far.wait_recv()
            keep(h, pos[2], k, other)
    for cp in at.sends[old:]:
        cp.wait_send()
    for cp in stores + small:
        cp.wait()


def output_kernel(half_hbm, both_hbm, right_hbm, inv_hbm, update, new_momentum, new_basis,
                  hbuf, both, rbuf, inv, ubuf, nbuf, bbuf, load, store):
    nc = COLS // STEP
    first = [
        pltpu.make_async_copy(both_hbm, both, load.at[3 * nc]),
        pltpu.make_async_copy(inv_hbm, inv, load.at[3 * nc + 1]),
    ]
    loads = []
    for c in range(nc):
        cols = pl.ds(c * STEP, STEP)
        loads.append([
            pltpu.make_async_copy(right_hbm.at[0, cols, :], rbuf.at[0, cols, :], load.at[3 * c]),
            pltpu.make_async_copy(right_hbm.at[1, cols, :], rbuf.at[1, cols, :], load.at[3 * c + 1]),
            pltpu.make_async_copy(half_hbm.at[:, cols], hbuf.at[:, cols], load.at[3 * c + 2]),
        ])
    for cp in first:
        cp.start()
    for group in loads:
        for cp in group:
            cp.start()
    for cp in first:
        cp.wait()
    stores = []
    for c in range(nc):
        cols = pl.ds(c * STEP, STEP)
        for cp in loads[c]:
            cp.wait()
        rr = jnp.concatenate([rbuf[0, cols, :], rbuf[1, cols, :]], axis=1)
        bbuf[cols, :] = (rr.astype(F32) * inv[0:1, :]).astype(BF16)
        product = dot(both[...], rr, 1, 1)
        ubuf[:, cols] = product[ROWS:].astype(BF16)
        nbuf[:, cols] = (hbuf[:, cols].astype(F32) - (1.0 - MU / 100.0) * product[:ROWS]).astype(BF16)
        three = [
            pltpu.make_async_copy(bbuf.at[cols, :], new_basis.at[cols, :], store.at[3 * c]),
            pltpu.make_async_copy(ubuf.at[:, cols], update.at[:, cols], store.at[3 * c + 1]),
            pltpu.make_async_copy(nbuf.at[:, cols], new_momentum.at[:, cols], store.at[3 * c + 2]),
        ]
        for cp in three:
            cp.start()
        stores += three
    for cp in stores:
        cp.wait()


def body(grad, momentum, basis):
    dma = pltpu.SemaphoreType.DMA
    zr = ROWS // NZ
    sends = 7 + 7 + 4 + 12 + 6 + 6 + 1 + 15 + 8 + 6 + 7 + 8
    right, both, inverse, half = pl.pallas_call(
        step_kernel,
        out_shape=(
            jax.ShapeDtypeStruct((2, 2, NX, NY, BLOCK, 128), BF16),
            jax.ShapeDtypeStruct((2 * ROWS, RANK), BF16),
            jax.ShapeDtypeStruct((8, RANK), F32),
            jax.ShapeDtypeStruct((ROWS, COLS), BF16),
        ),
        in_specs=[pl.BlockSpec(memory_space=pl.ANY)] * 3,
        out_specs=tuple(pl.BlockSpec(memory_space=pl.ANY) for _ in range(4)),
        scratch_shapes=[
            pltpu.VMEM((2 * ROWS, RANK), BF16), pltpu.VMEM((8, RANK), F32),
            pltpu.VMEM((ROWS, COLS), BF16), pltpu.VMEM((ROWS, COLS), BF16), pltpu.VMEM((COLS, RANK), BF16),
            pltpu.VMEM((COLS, RANK), BF16),
            pltpu.VMEM((ROWS, RANK), BF16), pltpu.VMEM((NZ - 1, zr, RANK), BF16), pltpu.VMEM((ROWS, RANK), BF16),
            pltpu.VMEM((16, 24, 128), F32), pltpu.VMEM((31, 24, 128), F32),
            pltpu.VMEM((24, 128), F32), pltpu.VMEM((NZ - 1, 24, 128), F32), pltpu.VMEM((16, 24, 128), F32),
            pltpu.VMEM((2, 2, NX, NY, BLOCK, 128), BF16), pltpu.VMEM((2, NX, NY, BLOCK, 128), BF16),
            pltpu.VMEM((2, NX, NY, BLOCK, 128), F32), pltpu.VMEM((2, NX, NY, BLOCK, 128), BF16),
            pltpu.VMEM((2, NX, NY, BLOCK, 128), BF16), pltpu.VMEM((2, 6, 2, BLOCK, 128), BF16), pltpu.VMEM((2, 2, 2, BLOCK, 128), BF16),
            pltpu.VMEM((2, 4, BLOCK, 128), F32), pltpu.VMEM((2, 4, BLOCK, 128), BF16), pltpu.VMEM((2, 3, BLOCK, 128), BF16),
            pltpu.VMEM((8, 128), F32), pltpu.VMEM((8, 128), F32),
            pltpu.VMEM((NX * NY, 8, 128), F32), pltpu.VMEM((NZ, 8, 128), F32),
            dma((3 * (COLS // STEP),)), dma((23,)), dma((47,)), dma((48,)), dma((16,)), dma((sends,)), dma((sends,)),
        ],
        compiler_params=pltpu.CompilerParams(collective_id=0, has_side_effects=True, vmem_limit_bytes=VMEM_LIMIT),
        name="step_kernel",
    )(grad, momentum, basis)
    nc = COLS // STEP
    wide = pltpu.VMEM((ROWS, COLS), BF16)
    return pl.pallas_call(
        output_kernel,
        out_shape=(
            jax.ShapeDtypeStruct((ROWS, COLS), BF16),
            jax.ShapeDtypeStruct((ROWS, COLS), BF16),
            jax.ShapeDtypeStruct((COLS, RANK), BF16),
        ),
        in_specs=[pl.BlockSpec(memory_space=pl.ANY)] * 4,
        out_specs=tuple(pl.BlockSpec(memory_space=pl.ANY) for _ in range(3)),
        scratch_shapes=[
            wide, pltpu.VMEM((2 * ROWS, RANK), BF16), pltpu.VMEM((2, COLS, 128), BF16), pltpu.VMEM((8, RANK), F32),
            wide, wide, pltpu.VMEM((COLS, RANK), BF16),
            dma((3 * nc + 2,)), dma((3 * nc,)),
        ],
        compiler_params=pltpu.CompilerParams(vmem_limit_bytes=VMEM_LIMIT),
        name="output_kernel",
    )(half, both, right.reshape(2, COLS, 128), inverse)


def solution(mesh):
    placed = (P("fsdp", "tp"), P("fsdp", "tp"), P("tp", None))
    return jax.shard_map(
        body,
        mesh=mesh,
        in_specs=placed,
        out_specs=(P("fsdp", "tp"), P("fsdp", "tp"), P("tp", None)),
        check_vma=False,
    )
```

```python
import math

import jax
import jax.numpy as jnp
from jax import lax
from jax.experimental import pallas as pl
from jax.experimental.pallas import tpu as pltpu
from jax.sharding import PartitionSpec as P

M = 8192
N = 28672
RANK = 256
MU = 90

MESH = pl.DeviceIdType.MESH
HI = lax.Precision.HIGHEST
F32 = jnp.float32
BF16 = jnp.bfloat16
NX, NY, NZ = 4, 4, 8
NF = NX * NY * 2
ROWS = M // NF
COLS = N // NZ
CHUNK = 896
BLOCK = COLS // NF
FAR_FIRST = sorted(range(1, NZ), key=lambda j: -min(j, NZ - j))
STEP = 512
VMEM_LIMIT = 60 * 1024 * 1024


def dot(a, b, ca, cb, precision=None):
    return lax.dot_general(
        a, b, (((ca,), (cb,)), ((), ())), precision=precision, preferred_element_type=F32
    )


def lane_of(tile, j):
    return jnp.broadcast_to(tile[j:j + 1, :], tile.shape)


def column_of(tile, j):
    return jnp.broadcast_to(tile[:, j:j + 1], tile.shape)


def reciprocal(v):
    near = pl.reciprocal(v, approx=True)
    return near * (2.0 - v * near)


def parts(v):
    hi = v.astype(BF16)
    return hi, (v - hi.astype(F32)).astype(BF16)


def lower_inverse(gram, beside, b=64, s8=8):
    n = gram.shape[0]
    tiles = b // 8
    nt = n // 128
    rows = lax.broadcasted_iota(jnp.int32, (8, 128), 0)
    ln = lax.broadcasted_iota(jnp.int32, (8, 128), 1)
    lanes = lax.broadcasted_iota(jnp.int32, (b, n), 1)
    panels = [gram[p * b:(p + 1) * b, :] for p in range(n // b)]
    done = []
    for p in range(n // b):
        r0 = p * b
        home = r0 // 128
        P_ = panels[p]
        M_ = [[P_[8 * a:8 * a + 8, 128 * l:128 * l + 128] for l in range(nt)] for a in range(tiles)]
        for a in range(tiles):
            M_[a].append(jnp.where(ln + home * 128 == rows + (r0 + 8 * a), 1.0, 0.0))
        piv = [jnp.ones((8, 128), F32) for _ in range(tiles)]
        ahead = None
        for s in range(tiles):
            lane = r0 - home * 128 + s * s8
            C = []
            for k in range(s8):
                C.append([column_of(M_[a][home], lane + k) if a > s else None for a in range(tiles)])
                C[k][s] = column_of(M_[s][home], lane + k) if ahead is None else ahead[k]
            ahead = [column_of(M_[s + 1][home], lane + s8 + k) for k in range(s8)] if s + 1 < tiles else None
            for j in range(0, s8, 2):
                first, second = C[j], C[j + 1]
                p11 = lane_of(first[s], j)
                p12 = lane_of(first[s], j + 1)
                p22 = lane_of(second[s], j + 1)
                det = p11 * p22 - p12 * p12
                inv1 = reciprocal(p11)
                mult = p12 * inv1
                near = pl.reciprocal(det, approx=True)
                fix = 2.0 - det * near
                w1 = [first[a] * inv1 if a >= s else None for a in range(tiles)]
                second = [second[a] - first[a] * mult if a >= s else None for a in range(tiles)]
                w2 = [((second[a] * p11) * near) * fix if a >= s else None for a in range(tiles)]
                if ahead is not None:
                    for k in range(s8):
                        b1, b2 = lane_of(first[s + 1], k), lane_of(second[s + 1], k)
                        ahead[k] = (ahead[k] - w1[s + 1] * b1) - w2[s + 1] * b2
                for k in range(j + 2, s8):
                    b1 = lane_of(first[s], k)
                    b2 = lane_of(second[s], k)
                    for a in range(s, tiles):
                        C[k][a] = (C[k][a] - w1[a] * b1) - w2[a] * b2
                w1[s] = jnp.where(rows > j, w1[s], 0.0)
                w2[s] = jnp.where(rows > j + 1, w2[s], 0.0)
                piv[s] = jnp.where(rows == j, p11, jnp.where(rows == j + 1, det * inv1, piv[s]))
                for l in range(nt + 1):
                    b1 = lane_of(M_[s][l], j)
                    b2 = lane_of(M_[s][l], j + 1) - b1 * mult
                    for a in range(s, tiles):
                        M_[a][l] = (M_[a][l] - w1[a] * b1) - w2[a] * b2
        full = []
        for a in range(tiles):
            root = lax.rsqrt(piv[a])
            out = [v * root for v in M_[a]]
            ident = out.pop()
            at = ln + home * 128
            out[home] = jnp.where((at >= r0) & (at < r0 + b), ident, out[home])
            full.append(jnp.concatenate(out, axis=1))
        U = jnp.concatenate(full, axis=0)
        done.append(U)
        if p + 1 < n // b:
            r1 = r0 + b
            cut = r1 // 128 * 128
            hi, lo = parts(U)
            lhs = jnp.concatenate([hi[:, cut:], hi[:, cut:], lo[:, cut:], lo[:, cut:]], axis=0).T
            rhs = jnp.concatenate([hi, lo, hi, lo], axis=0)
            for q in range(p + 1, n // b):
                old = jnp.where((lanes >= r0) & (lanes < r1), 0.0, panels[q])
                panels[q] = old - dot(lhs[q * b - cut:(q + 1) * b - cut, :], rhs, 1, 0)
            if p in beside:
                beside[p]()
    W = jnp.concatenate(done, axis=0)
    li = lax.broadcasted_iota(jnp.int32, (n, n), 1)
    si = lax.broadcasted_iota(jnp.int32, (n, n), 0)
    return jnp.where(li <= si, W, 0.0)


class Place:
    def __init__(self, ssem, rsem):
        self.ssem, self.rsem = ssem, rsem
        self.sends = []
        self.f = lax.axis_index("fsdp")
        self.t = lax.axis_index("tp")
        self.core = lax.rem(self.f, 2)
        self.other = 1 - self.core
        self.x = lax.rem(self.f // 2, NX)
        self.y = self.f // (2 * NX)
        self.xs = [lax.rem(self.x + j, NX) for j in range(NX)]
        self.ys = [lax.rem(self.y + j, NY) for j in range(NY)]
        self.zs = [lax.rem(self.t + j, NZ) for j in range(NZ)]
        self.sibling = self.dev(self.x, self.y, self.other)
        self.zdev = [(self.f, z) for z in self.zs]
        self.all = [lax.rem(self.f + j, NF) for j in range(NF)]
        self.fdev = [(g, self.t) for g in self.all]
        self.plane = [
            self.dev(self.xs[i], self.ys[j], self.core) for i in range(NX) for j in range(NY) if (i, j) != (0, 0)
        ]
        self.chips = [self.ys[j] * NX + self.xs[i] for i in range(NX) for j in range(NY) if (i, j) != (0, 0)]
        self.chip = self.y * NX + self.x
        self.ways = (
            (self.xs, self.dev(self.xs[1], self.y, self.core), self.dev(self.xs[3], self.y, self.core)),
            (self.ys, self.dev(self.x, self.ys[1], self.core), self.dev(self.x, self.ys[3], self.core)),
        )

        self.twins = (
            (self.dev(self.xs[1], self.y, self.other), self.dev(self.xs[3], self.y, self.other)),
            (self.dev(self.x, self.ys[1], self.other), self.dev(self.x, self.ys[3], self.other)),
        )

    def dev(self, px, py, pc):
        return ((py * NX + px) * 2 + pc, self.t)

    def y_x(self, i, j):
        return self.ys[j] * NX + self.xs[i]

    def greet(self, devices):
        barrier = pltpu.get_barrier_semaphore()
        for device in devices:
            pl.semaphore_signal(barrier, inc=1, device_id=device, device_id_type=MESH)
        return lambda: pl.semaphore_wait(barrier, len(devices))

    def exchange(self, src, dst, device):
        k = len(self.sends)
        cp = pltpu.make_async_remote_copy(
            src_ref=src, dst_ref=dst, send_sem=self.ssem.at[k], recv_sem=self.rsem.at[k],
            device_id=device, device_id_type=MESH,
        )
        cp.start()
        self.sends.append(cp)
        return cp

    def share(self, ref, device):
        return self.exchange(ref, ref, device)


def piece(z, size):
    return pl.ds(pl.multiple_of(z * size, size), size)


def step_kernel(g_hbm, m_hbm, b_hbm, result, both_hbm, inv_hbm, half_hbm, both, inverse, gbuf, mbuf, bbuf, bht, part, rz, left, gpart, rg, own, r2, gram,
                out, rs, r, rc, r16, f1, joined, sab, s16, f2, sq, qc, qp, qz, load, store, gsem, hsem, zsem, ssem, rsem):
    at = Place(ssem, rsem)
    core, other, x, y, xs, ys = at.core, at.other, at.x, at.y, at.xs, at.ys
    nc = COLS // STEP
    loads = []
    for c in range(nc):
        cols = pl.ds(c * STEP, STEP)
        three = [
            pltpu.make_async_copy(b_hbm.at[cols, :], bbuf.at[cols, :], load.at[3 * c]),
            pltpu.make_async_copy(g_hbm.at[:, cols], gbuf.at[:, cols], load.at[3 * c + 1]),
            pltpu.make_async_copy(m_hbm.at[:, cols], mbuf.at[:, cols], load.at[3 * c + 2]),
        ]
        for cp in three:
            cp.start()
        loads.append(three)
    ready = at.greet(at.zdev[1:] + at.fdev[1:])
    total = None
    for c in range(nc):
        for cp in loads[c]:
            cp.wait()
        cols = pl.ds(c * STEP, STEP)
        half = (mbuf[:, cols].astype(F32) + gbuf[:, cols].astype(F32)).astype(BF16)
        gbuf[:, cols] = half
        term = dot(half, bbuf[cols, :], 1, 0)
        total = term if c == 0 else total + term
    part[...] = (total * (1.0 / math.sqrt(N))).astype(BF16)
    ready()
    zr = ROWS // NZ
    cps = [at.exchange(part.at[piece(at.zs[j], zr), :], rz.at[j - 1], at.zdev[j]) for j in FAR_FIRST]
    for c in range(nc):
        cols = pl.ds(c * STEP, STEP)
        bht[cols, :] = gbuf[:, cols].T
    kept = pltpu.make_async_copy(gbuf, half_hbm, store.at[20])
    kept.start()
    mine = part[piece(at.t, zr), :].astype(F32)
    for cp in cps:
        cp.wait_recv()
    for j in range(1, NZ):
        mine = mine + rz[j - 1].astype(F32)
    mine = mine.astype(BF16)
    left[piece(at.t, zr), :] = mine
    az = [at.share(left.at[piece(at.t, zr), :], at.zdev[j]) for j in FAR_FIRST]

    full = dot(mine, mine, 0, 0)
    gpart[:, 0:8, :] = full[:128, :128].reshape(16, 8, 128)
    gpart[:, 8:16, :] = full[:128, 128:].reshape(16, 8, 128)
    gpart[:, 16:24, :] = full[128:, 128:].reshape(16, 8, 128)
    owner = lax.rem(x + y, 2) == core
    chips = sorted(((i, j) for i in range(NX) for j in range(NY)), key=lambda c: -min(c[0], NX - c[0]) - min(c[1], NY - c[1]))
    chips = chips[-1:] + chips[:-1]

    def to_owner(k, slot):
        i, j = chips[k]
        device = at.dev(xs[i], ys[j], lax.rem(xs[i] + ys[j], 2))
        return pltpu.make_async_remote_copy(
            src_ref=gpart.at[at.y_x(i, j)], dst_ref=rg.at[slot], send_sem=gsem.at[k], recv_sem=gsem.at[16 + slot],
            device_id=device if k else at.sibling, device_id_type=MESH,
        )

    scattered = [to_owner(k, 2 * k - 1 + core if k else 0) for k in range(16)]

    for k in range(1, 16):
        scattered[k].start()

    @pl.when(jnp.logical_not(owner))
    def _():
        scattered[0].start()

    def to_all(k, c):
        i, j = chips[k]
        return pltpu.make_async_remote_copy(
            src_ref=gram.at[at.chip], dst_ref=gram.at[at.chip], send_sem=hsem.at[2 * k + c], recv_sem=hsem.at[32 + k],
            device_id=at.dev(xs[i], ys[j], c) if k else at.sibling, device_id_type=MESH,
        )

    gathered = [to_all(0, 0)] + [to_all(k, c) for k in range(1, 16) for c in range(2)]
    across = [
        pltpu.make_async_remote_copy(
            src_ref=own, dst_ref=r2.at[j - 1], send_sem=zsem.at[j], recv_sem=zsem.at[8 + j],
            device_id=at.zdev[j], device_id_type=MESH,
        )
        for j in range(1, NZ)
    ]

    @pl.when(owner)
    def _():
        acc = gpart[at.chip]
        for slot in range(31):
            to_owner(0, slot).wait_recv()
            acc = acc + rg[slot]
        own[...] = acc
        for j in FAR_FIRST:
            across[j - 1].start()

    for cp in az:
        cp.wait_recv()
    wide = COLS // 2
    nk = wide // CHUNK
    qk = NX // nk

    def product(k, pc, into):
        half = bht[pl.ds(pl.multiple_of(pc * wide + k * CHUNK, 128), CHUNK), :]
        val = dot(half, left[...], 1, 0)
        for h in range(2):
            into[h, k * qk:(k + 1) * qk] = val[:, 128 * h:128 * h + 128].reshape(qk, NY, BLOCK, 128).astype(into.dtype)

    cc = []
    for k in range(nk):
        product(k, other, rs)
        qs = pl.ds(k * qk, qk)
        cc.append([at.exchange(rs.at[h, qs], rc.at[h, qs], at.sibling) for h in range(2)])

    @pl.when(owner)
    def _():
        acc = own[...]
        for j in range(1, NZ):
            across[j - 1].wait_recv()
            acc = acc + r2[j - 1]
        gram[at.chip] = acc
        for cp in gathered[1:] + gathered[:1]:
            cp.start()

    for k in range(nk):
        product(k, core, r)
    def half_of(ref, h, q, k):
        return ref.at[0, q, pl.ds(2 * k, 2)] if h == 0 else ref.at[1, pl.ds(2 * k, 2), q]

    one = []
    for h in range(2):
        for k in range(nk):
            qs = pl.ds(k * qk, qk)
            cc[k][h].wait_recv()
            total = r[h, qs] + rc[h, qs].astype(F32)
            r[h, qs] = total
            r16[h, qs] = total.astype(BF16)
        pos, nxt, prv = at.ways[h]
        one.append([
            at.exchange(half_of(r16, h, pos[2], 0), f1.at[h, 0], nxt), at.exchange(half_of(r16, h, pos[2], 1), f1.at[h, 1], prv),
        ])
    for h in range(2):
        pos, nxt, prv = at.ways[h]
        one[h] += [
            at.exchange(half_of(r16, h, pos[1], 1), f1.at[h, 2], nxt), at.exchange(half_of(r16, h, pos[3], 0), f1.at[h, 3], prv),
        ]
    for h in range(2):
        pos, nxt, prv = at.ways[h]
        for k, (q, to) in enumerate(((pos[1], nxt), (pos[3], prv))):
            one[h][k].wait_recv()
            joined[h, k] = (half_of(r, h, q, k)[...] + f1[h, k].astype(F32)).astype(BF16)
            one[h].append(at.exchange(joined.at[h, k], f1.at[h, 4 + k], to))
    for k in range(1, 16):
        to_all(k, 0).wait_recv()

    @pl.when(jnp.logical_not(owner))
    def _():
        to_all(0, 0).wait_recv()

    upper = jnp.concatenate([gram[:, 0:8, :].reshape(128, 128), gram[:, 8:16, :].reshape(128, 128)], axis=1)
    corner = gram[:, 16:24, :].reshape(128, 128)
    full = jnp.concatenate([upper, jnp.concatenate([jnp.zeros_like(corner), corner], axis=1)], axis=0)
    two = [[], []]

    def second_stage():
        for h in range(2):
            for k in range(2, 6):
                one[h][k].wait_recv()
            for k in range(2):
                total = half_of(r, h, x if h == 0 else y, k)[...] + f1[h, 3 - k].astype(F32) + f1[h, 4 + k].astype(F32)
                sab[h, 2 * k:2 * k + 2] = total
                s16[h, 2 * k:2 * k + 2] = total.astype(BF16)
            for j in (2, 1, 3):
                if h == 0:
                    two[h].append(at.exchange(s16.at[h, ys[j]], f2.at[h, j - 1], at.dev(x, ys[j], core)))
                else:
                    two[h].append(at.exchange(s16.at[h, xs[j]], f2.at[h, j - 1], at.dev(xs[j], y, core)))

    unit = lax.rsqrt(full[0:1, 0:1])
    w = lower_inverse((full * unit) * unit, {2: second_stage}) * unit
    whi, wlo = parts(w)
    halves = []
    for h in range(2):
        total = sab[h, y if h == 0 else x]
        for cp in two[h]:
            cp.wait_recv()
        for j in range(1, NX):
            total = total + f2[h, j - 1].astype(F32)
        halves.append(total)
    hi, lo = parts(jnp.concatenate(halves, axis=1))
    right = dot(jnp.concatenate([hi, lo], axis=0), whi, 1, 1)
    right = right[:BLOCK] + right[BLOCK:] + dot(hi, wlo, 1, 1)
    rounded = right.astype(BF16)
    for h in range(2):
        out[h, core, x, y] = rounded[:, 128 * h:128 * h + 128]
    g2 = [[], []]
    for j in (2, 1, 3):
        g2[0].append(at.share(out.at[0, core, x, y], at.dev(x, ys[j], core)))
        g2[1].append(at.share(out.at[1, core, x, y], at.dev(xs[j], y, core)))
    total = jnp.sum(right * right, axis=0, keepdims=True)
    srow = lax.broadcasted_iota(jnp.int32, (8, 128), 0)
    sq[...] = jnp.where(srow == 0, total[:, :128], total[:, 128:])
    sc = at.exchange(sq, qc, at.sibling)
    ortho = dot(left[...], whi, 1, 1) + dot(left[...], wlo, 1, 1)
    both[0:ROWS, :] = ortho.astype(BF16)
    sc.wait_recv()
    qp[at.chip] = sq[...] + qc[...]
    sp = [at.share(qp.at[at.chip], at.dev(xs[i], ys[j], core)) for i, j in chips[1:]]
    def band(h, q, k=None, ref=out, pc=core):
        if k is None:
            return ref.at[0, pc, q] if h == 0 else ref.at[1, pc, :, q]
        return ref.at[0, pc, q, pl.ds(2 * k, 2)] if h == 0 else ref.at[1, pc, pl.ds(2 * k, 2), q]

    last, spans, stores = [], [], []

    def keep(h, q, k, pc):
        cp = pltpu.make_async_copy(band(h, q, k, out, pc), band(h, q, k, result, pc), store.at[len(stores)])
        cp.start()
        stores.append(cp)

    def forward(h, q, k=None):
        last.append(at.share(band(h, q, k), at.sibling))
        spans.append((h, q, k))
        keep(h, q, k, core)

    begun = []
    for h in range(2):
        for cp in g2[h]:
            cp.wait_recv()
        pos, nxt, prv = at.ways[h]
        begun.append([
            at.share(band(h, pos[0], 0), nxt), at.share(band(h, pos[0], 1), prv),
            at.share(band(h, pos[0], 1), nxt), at.share(band(h, pos[0], 0), prv),
        ])
    for h in range(2):
        forward(h, at.ways[h][0][0])
    old = len(at.sends) - 10
    for cp in sp:
        cp.wait_recv()
    total = qp[0]
    for j in range(1, NX * NY):
        total = total + qp[j]
    qz[at.t] = total
    sz = [at.share(qz.at[at.t], at.zdev[j]) for j in FAR_FIRST]
    relays = []
    for h in range(2):
        pos, nxt, prv = at.ways[h]
        for k, (q, near, far) in enumerate(((pos[3], nxt, at.twins[h][0]), (pos[1], prv, at.twins[h][1]))):
            begun[h][k].wait_recv()
            relays.append((at.share(band(h, q, k), near), at.share(band(h, q, k), far)))
    for h in range(2):
        pos = at.ways[h][0]
        begun[h][2].wait_recv()
        forward(h, pos[3])
        begun[h][3].wait_recv()
        forward(h, pos[1])
    for cp in at.sends[:old] + scattered[1:]:
        cp.wait_send()
    kept.wait()

    @pl.when(jnp.logical_not(owner))
    def _():
        scattered[0].wait_send()

    @pl.when(owner)
    def _():
        for cp in across + gathered:
            cp.wait_send()

    for cp in sz:
        cp.wait_recv()
    total = qz[0]
    for j in range(1, NZ):
        total = total + qz[j]
    scale = jnp.sqrt(jnp.concatenate([total[0:1, :], total[1:2, :]], axis=1) / N + 1e-06)
    inverse[...] = jnp.broadcast_to(1.0 / scale, (8, RANK))
    both[ROWS:, :] = (ortho * (math.sqrt(M / RANK) / scale)).astype(BF16)
    small = [
        pltpu.make_async_copy(both, both_hbm, store.at[21]), pltpu.make_async_copy(inverse, inv_hbm, store.at[22]),
    ]
    for cp in small:
        cp.start()
    for cp, (h, q, k) in zip(last, spans):
        cp.wait_recv()
        keep(h, q, k, other)
    for h in range(2):
        pos = at.ways[h][0]
        for k in range(2):
            near, far = relays[2 * h + k]
            near.wait_recv()
            keep(h, pos[2], k, core)
            far.wait_recv()
            keep(h, pos[2], k, other)
    for cp in at.sends[old:]:
        cp.wait_send()
    for cp in stores + small:
        cp.wait()


def output_kernel(half_hbm, both_hbm, right_hbm, inv_hbm, update, new_momentum, new_basis,
                  hbuf, both, rbuf, inv, ubuf, nbuf, bbuf, load, store):
    nc = COLS // STEP
    first = [
        pltpu.make_async_copy(both_hbm, both, load.at[3 * nc]),
        pltpu.make_async_copy(inv_hbm, inv, load.at[3 * nc + 1]),
    ]
    loads = []
    for c in range(nc):
        cols = pl.ds(c * STEP, STEP)
        loads.append([
            pltpu.make_async_copy(right_hbm.at[0, cols, :], rbuf.at[0, cols, :], load.at[3 * c]),
            pltpu.make_async_copy(right_hbm.at[1, cols, :], rbuf.at[1, cols, :], load.at[3 * c + 1]),
            pltpu.make_async_copy(half_hbm.at[:, cols], hbuf.at[:, cols], load.at[3 * c + 2]),
        ])
    for cp in first:
        cp.start()
    for group in loads:
        for cp in group:
            cp.start()
    for cp in first:
        cp.wait()
    stores = []
    for c in range(nc):
        cols = pl.ds(c * STEP, STEP)
        for cp in loads[c]:
            cp.wait()
        rr = jnp.concatenate([rbuf[0, cols, :], rbuf[1, cols, :]], axis=1)
        bbuf[cols, :] = (rr.astype(F32) * inv[0:1, :]).astype(BF16)
        product = dot(both[...], rr, 1, 1)
        ubuf[:, cols] = product[ROWS:].astype(BF16)
        nbuf[:, cols] = (hbuf[:, cols].astype(F32) - (1.0 - MU / 100.0) * product[:ROWS]).astype(BF16)
        three = [
            pltpu.make_async_copy(bbuf.at[cols, :], new_basis.at[cols, :], store.at[3 * c]),
            pltpu.make_async_copy(ubuf.at[:, cols], update.at[:, cols], store.at[3 * c + 1]),
            pltpu.make_async_copy(nbuf.at[:, cols], new_momentum.at[:, cols], store.at[3 * c + 2]),
        ]
        for cp in three:
            cp.start()
        stores += three
    for cp in stores:
        cp.wait()


def body(grad, momentum, basis):
    dma = pltpu.SemaphoreType.DMA
    zr = ROWS // NZ
    sends = 7 + 7 + 4 + 12 + 6 + 6 + 1 + 15 + 8 + 6 + 7 + 8
    right, both, inverse, half = pl.pallas_call(
        step_kernel,
        out_shape=(
            jax.ShapeDtypeStruct((2, 2, NX, NY, BLOCK, 128), BF16),
            jax.ShapeDtypeStruct((2 * ROWS, RANK), BF16),
            jax.ShapeDtypeStruct((8, RANK), F32),
            jax.ShapeDtypeStruct((ROWS, COLS), BF16),
        ),
        in_specs=[pl.BlockSpec(memory_space=pl.ANY)] * 3,
        out_specs=tuple(pl.BlockSpec(memory_space=pl.ANY) for _ in range(4)),
        scratch_shapes=[
            pltpu.VMEM((2 * ROWS, RANK), BF16), pltpu.VMEM((8, RANK), F32),
            pltpu.VMEM((ROWS, COLS), BF16), pltpu.VMEM((ROWS, COLS), BF16), pltpu.VMEM((COLS, RANK), BF16),
            pltpu.VMEM((COLS, RANK), BF16),
            pltpu.VMEM((ROWS, RANK), BF16), pltpu.VMEM((NZ - 1, zr, RANK), BF16), pltpu.VMEM((ROWS, RANK), BF16),
            pltpu.VMEM((16, 24, 128), F32), pltpu.VMEM((31, 24, 128), F32),
            pltpu.VMEM((24, 128), F32), pltpu.VMEM((NZ - 1, 24, 128), F32), pltpu.VMEM((16, 24, 128), F32),
            pltpu.VMEM((2, 2, NX, NY, BLOCK, 128), BF16), pltpu.VMEM((2, NX, NY, BLOCK, 128), BF16),
            pltpu.VMEM((2, NX, NY, BLOCK, 128), F32), pltpu.VMEM((2, NX, NY, BLOCK, 128), BF16),
            pltpu.VMEM((2, NX, NY, BLOCK, 128), BF16), pltpu.VMEM((2, 6, 2, BLOCK, 128), BF16), pltpu.VMEM((2, 2, 2, BLOCK, 128), BF16),
            pltpu.VMEM((2, 4, BLOCK, 128), F32), pltpu.VMEM((2, 4, BLOCK, 128), BF16), pltpu.VMEM((2, 3, BLOCK, 128), BF16),
            pltpu.VMEM((8, 128), F32), pltpu.VMEM((8, 128), F32),
            pltpu.VMEM((NX * NY, 8, 128), F32), pltpu.VMEM((NZ, 8, 128), F32),
            dma((3 * (COLS // STEP),)), dma((23,)), dma((47,)), dma((48,)), dma((16,)), dma((sends,)), dma((sends,)),
        ],
        compiler_params=pltpu.CompilerParams(collective_id=0, has_side_effects=True, vmem_limit_bytes=VMEM_LIMIT),
        name="step_kernel",
    )(grad, momentum, basis)
    nc = COLS // STEP
    wide = pltpu.VMEM((ROWS, COLS), BF16)
    return pl.pallas_call(
        output_kernel,
        out_shape=(
            jax.ShapeDtypeStruct((ROWS, COLS), BF16),
            jax.ShapeDtypeStruct((ROWS, COLS), BF16),
            jax.ShapeDtypeStruct((COLS, RANK), BF16),
        ),
        in_specs=[pl.BlockSpec(memory_space=pl.ANY)] * 4,
        out_specs=tuple(pl.BlockSpec(memory_space=pl.ANY) for _ in range(3)),
        scratch_shapes=[
            wide, pltpu.VMEM((2 * ROWS, RANK), BF16), pltpu.VMEM((2, COLS, 128), BF16), pltpu.VMEM((8, RANK), F32),
            wide, wide, pltpu.VMEM((COLS, RANK), BF16),
            dma((3 * nc + 2,)), dma((3 * nc,)),
        ],
        compiler_params=pltpu.CompilerParams(vmem_limit_bytes=VMEM_LIMIT),
        name="output_kernel",
    )(half, both, right.reshape(2, COLS, 128), inverse)


def solution(mesh):
    placed = (P("fsdp", "tp"), P("fsdp", "tp"), P("tp", None))
    return jax.shard_map(
        body,
        mesh=mesh,
        in_specs=placed,
        out_specs=(P("fsdp", "tp"), P("fsdp", "tp"), P("tp", None)),
        check_vma=False,
    )
```
